32 devices in a mesh: cuts: 4 (over y, core), fsdp: 8 (over z, x).
Axes of the slice: x: 2, y: 2, z: 4, core: 2. Of those that a mesh axis runs over, the one named last changes fastest.
Arguments:
- hidden_states: bfloat16 [16384, 8192], P(('cuts', 'fsdp')), may hold values from -1200 to 1200
- key_cotangent: bfloat16 [16384, 512], P(('cuts', 'fsdp')), may hold values from -60 to 60
- old_weight: bfloat16 [16384, 256], P(('cuts', 'fsdp')), may hold values from -0.0625 to 0.0625
- old_first: bfloat16 [16384, 256], P(('cuts', 'fsdp')), may hold values from -1 to 1
- old_first_scale: float32 [16384], P(('cuts', 'fsdp')), may hold values from 3e-05 to 0.0003
- old_second: bfloat16 [16384, 256], P(('cuts', 'fsdp')), may hold values from 0 to 1
- old_second_scale: float32 [16384], P(('cuts', 'fsdp')), may hold values from 1e-08 to 1e-07
- send_counts: int32 [32, 32], P(('cuts', 'fsdp')), may hold values from 0 to 32, as said below
Outputs:
- input_grad: bfloat16 [16384, 8192], P(('cuts', 'fsdp'))
- new_weight: bfloat16 [8192, 512], P(('cuts', 'fsdp'))
- first_code: bfloat16 [8192, 512], P(('cuts', 'fsdp'))
- first_scale: float32 [8192, 2], P(('cuts', 'fsdp'))
- second_code: bfloat16 [8192, 512], P(('cuts', 'fsdp'))
- second_scale: float32 [8192, 2], P(('cuts', 'fsdp'))
The draws below stay inside these ranges and needn't reach their ends.
Inputs may be any that keep to these rules, and one draw needn't show every extreme that they name: Every row and every column of send_counts sums to 512; each entry is 0, 16 or 32, and every row and every column holds 32 exactly once.
All inputs are finite; a program needn't handle non-finite values.
Results may differ from the reference program's by a relative error of at most 0.00075.
Values may be sent and summed in bfloat16 or wider, within the bound.
No kernel may reach another device: no remote copies, remote signals or barrier semaphores. Data moves between devices by JAX's collectives and lax.ppermute only.
A program may use at most 128 MiB of HBM per device.

```python
import math
import jax
import jax.numpy as jnp
from jax import lax

D = 8192
QB = 256
TOK_DEV = 512
STEP = 2000
PEERS = 32
KW = 512
TOKENS = 16384
NB = 16384
NBD = 512
RC = 256
BPR = 2


def draw_hidden_states(key, part):
    key_base, key_rough, key_pair = jax.random.split(jax.random.fold_in(key, 11), 3)
    feature = jnp.arange(D, dtype=jnp.float32) / D
    rough = jnp.exp(jax.random.uniform(key_rough, (D,), jnp.float32, 0.0, math.log(3.3)))
    values = jnp.clip(jax.random.normal(key_base, (TOKENS, D), jnp.float32), -6.0, 6.0)
    rising = jnp.exp(math.log(3.0) * feature)
    pairing = jax.random.permutation(key_pair, PEERS)
    holder = jnp.arange(TOKENS, dtype=jnp.int32) // TOK_DEV
    feature_owner = jnp.arange(D, dtype=jnp.int32) // RC
    paired = pairing[holder][:, None] == feature_owner[None, :]
    spike = jnp.where(paired, 8.0, 1.0)
    return (values * rising[None, :] * rough[None, :] * spike).astype(jnp.bfloat16)


def draw_key_cotangent(key, part):
    key_base, key_scale = jax.random.split(jax.random.fold_in(key, 23), 2)
    values = jnp.clip(jax.random.normal(key_base, (TOKENS, KW), jnp.float32), -6.0, 6.0)
    column_scale = jnp.exp(jax.random.uniform(key_scale, (KW,), jnp.float32, 0.0, math.log(10.0)))
    return (values * column_scale[None, :]).astype(jnp.bfloat16)


def draw_send_counts(key, part):
    key_perm, key_shift = jax.random.split(jax.random.fold_in(key, 37), 2)
    base_count = NBD // PEERS
    ordering = jax.random.permutation(key_perm, PEERS)
    shift_by = jax.random.randint(key_shift, (), 1, PEERS)
    index = jnp.arange(PEERS, dtype=jnp.int32)
    second_order = ordering[(index + shift_by) % PEERS]
    columns = jnp.arange(PEERS, dtype=jnp.int32)[None, :]
    raised = (ordering[:, None] == columns).astype(jnp.int32)
    lowered = (second_order[:, None] == columns).astype(jnp.int32)
    return (base_count + base_count * raised - base_count * lowered).astype(jnp.int32)


def shard_levels(rng, shape, cuts, least, largest):
    loudness, own = 1.0, jax.random.fold_in(rng, 6)
    for dim, parts in cuts:
        draws = jnp.exp(jax.random.uniform(jax.random.fold_in(own, dim), (parts,), jnp.float32, least / len(cuts), largest / len(cuts)))
        loudness = loudness * jnp.repeat(draws, shape[dim] // parts).reshape([-1 if axis == dim else 1 for axis in range(len(shape))])
    return loudness


def normal_values(rng, shape, deviation, most, cuts=(), kind=jnp.bfloat16):
    drawn = deviation * jax.random.normal(rng, shape, jnp.float32)
    if cuts:
        drawn = drawn * shard_levels(rng, shape, cuts, -0.22, 0.18)
    return jnp.clip(drawn, -most, most).astype(kind)


def setup_inputs(seed: int = 0) -> dict:
    seeds = jax.random.split(jax.random.key(seed), 9)
    return {
        "hidden_states": draw_hidden_states(jax.random.fold_in(seeds[8], 71), 0),
        "key_cotangent": draw_key_cotangent(jax.random.fold_in(seeds[8], 71), 0),
        "old_weight": normal_values(seeds[2], (PEERS * NBD, QB), D ** -0.5, 0.0625, ((0, 32),)),
        "old_first": jnp.clip(jax.random.uniform(seeds[3], (PEERS * NBD, QB), jnp.float32, -1.0, 1.0) * shard_levels(seeds[3], (PEERS * NBD, QB), ((0, 32),), -0.4, 0.0), -1.0, 1.0).astype(jnp.bfloat16),
        "old_first_scale": jnp.clip(jnp.exp(math.log(0.0003) - 2.3025852 * jax.random.uniform(seeds[4], (PEERS * NBD,), jnp.float32) ** shard_levels(seeds[4], (PEERS * NBD,), ((0, 32),), -0.2, 0.2)), 2.9999999242136255e-05, 0.0003),
        "old_second": jnp.clip(1.0 * jax.random.uniform(seeds[5], (PEERS * NBD, QB), jnp.float32) ** shard_levels(seeds[5], (PEERS * NBD, QB), ((0, 32),), -0.2, 0.2), 0.0, 1.0).astype(jnp.bfloat16),
        "old_second_scale": jnp.clip(jnp.exp(math.log(1.0000000116860974e-07) - 2.3025851 * jax.random.uniform(seeds[6], (PEERS * NBD,), jnp.float32) ** shard_levels(seeds[6], (PEERS * NBD,), ((0, 32),), -0.2, 0.2)), 9.99999993922529e-09, 1.0000000116860974e-07),
        "send_counts": draw_send_counts(jax.random.fold_in(seeds[8], 71), 0),
    }


beta_first = 0.9
beta_second = 0.95
adam_epsilon = 1e-05
learn_rate = 0.001
weight_decay = 0.1
clip_norm = 1.0
tiny_scale = 1e-30

def reshard(counts, blocks):
    peer_count = counts.shape[0]
    slot_count = blocks.shape[0] // peer_count
    slot_ends = jnp.cumsum(counts, axis=1).astype(jnp.int32)
    starts = slot_ends - counts
    offsets = jnp.cumsum(counts, axis=0).astype(jnp.int32) - counts
    slot_index = jnp.arange(slot_count, dtype=jnp.int32)
    owner = lax.optimization_barrier(jnp.sum((slot_ends[:, None, :] <= slot_index[None, :, None]).astype(jnp.int32), axis=2)).astype(jnp.int32)
    first_slot = jnp.take_along_axis(starts, owner, axis=1)
    base_slot = jnp.take_along_axis(offsets, owner, axis=1)
    target = (owner * slot_count + base_slot + slot_index[None, :] - first_slot).astype(jnp.int32)
    return jnp.zeros_like(blocks).at[target.reshape(-1)].set(blocks)

def adam_blocks(clipped, weight, first, first_scale, second, second_scale):
    m_old = first.astype(jnp.float32) * first_scale[:, None]
    v_old = second.astype(jnp.float32) * second_scale[:, None]
    m_new = beta_first * m_old + (1.0 - beta_first) * clipped
    v_new = beta_second * v_old + (1.0 - beta_second) * clipped * clipped
    m_hat = m_new / (1.0 - beta_first ** STEP)
    v_hat = v_new / (1.0 - beta_second ** STEP)
    w_old = weight.astype(jnp.float32)
    w_new = (w_old - learn_rate * (m_hat / (jnp.sqrt(v_hat) + adam_epsilon) + weight_decay * w_old)).astype(jnp.bfloat16)
    m_scale = lax.optimization_barrier(jnp.max(jnp.abs(m_new), axis=1)) + tiny_scale
    v_scale = lax.optimization_barrier(jnp.max(v_new, axis=1)) + tiny_scale
    m_code = (m_new / m_scale[:, None]).astype(jnp.bfloat16)
    v_code = (v_new / v_scale[:, None]).astype(jnp.bfloat16)
    return (w_new, m_code, m_scale, v_code, v_scale)

def reference(hidden_states, key_cotangent, old_weight, old_first, old_first_scale, old_second, old_second_scale, send_counts):
    weight_blocks = reshard(send_counts, old_weight)
    first_blocks = reshard(send_counts, old_first)
    second_blocks = reshard(send_counts, old_second)
    first_scales = reshard(send_counts, old_first_scale)
    second_scales = reshard(send_counts, old_second_scale)
    full_weight = weight_blocks.reshape(D, KW)
    input_grad = lax.dot_general(key_cotangent, full_weight, (((1,), (1,)), ((), ())), preferred_element_type=jnp.float32).astype(jnp.bfloat16)
    gradient = lax.dot_general(hidden_states, key_cotangent, (((0,), (0,)), ((), ())), preferred_element_type=jnp.float32) / TOKENS
    norm_value = jnp.sqrt(jnp.sum(gradient * gradient))
    factor = jnp.minimum(1.0, clip_norm / (norm_value + 1e-06))
    clipped = (gradient * factor).reshape(NB, QB)
    w_new, m_code, m_scale, v_code, v_scale = adam_blocks(clipped, weight_blocks, first_blocks, first_scales, second_blocks, second_scales)
    return (input_grad, w_new.reshape(D, KW), m_code.reshape(D, KW), m_scale.reshape(D, BPR), v_code.reshape(D, KW), v_scale.reshape(D, BPR))
```

```python
import functools

import jax
import jax.numpy as jnp
from jax import lax
from jax.experimental import pallas as pl
from jax.experimental.pallas import tpu as pltpu
from jax.sharding import PartitionSpec as P

STEP = 2000


beta_first = 0.9
beta_second = 0.95
adam_epsilon = 1e-05
learn_rate = 0.001
weight_decay = 0.1
clip_norm = 1.0
tiny_scale = 1e-30

AXES = ("cuts", "fsdp")
LIMIT = 48 * 1024 * 1024
TAIL = 16


class Grid:
    def __init__(self, cuts, fsdp):
        self.cuts, self.fsdp = cuts, fsdp
        self.ny = cuts // 2
        self.nz = 4
        self.nx = fsdp // 4
        self.size = cuts * fsdp

    def split(self, i):
        x = i % self.nx
        z = (i // self.nx) % self.nz
        c = (i // self.fsdp) % 2
        y = i // (2 * self.fsdp)
        return y, c, z, x

    def join(self, y, c, z, x):
        return ((y * 2 + c) * self.nz + z) * self.nx + x

    def send(self, a, dy=0, dc=0, dz=0, dx=0):
        pairs = []
        for i in range(self.size):
            y, c, z, x = self.split(i)
            pairs.append((i, self.join(y ^ dy, c ^ dc, z ^ dz, x ^ dx)))
        return lax.ppermute(a, AXES, pairs)


def params():
    return pltpu.CompilerParams(vmem_limit_bytes=LIMIT)


def encode(g, ref, lead, col):
    rows, width = g.shape
    top = jnp.max(jnp.abs(g), axis=1, keepdims=True)
    k = jnp.ceil(jnp.log2(jnp.maximum(top, 1e-30) / 32700.0) * 256.0)
    q = jnp.round(g * jnp.exp2(k * (-1.0 / 256.0)))
    ref[lead + (pl.ds(0, rows), pl.ds(col, width))] = q.astype(jnp.int32).astype(jnp.int16)
    kt = jnp.transpose(jnp.broadcast_to(k, (rows, 128)))[:TAIL]
    ref[lead + (pl.ds(rows, TAIL), pl.ds(col, rows))] = kt.astype(jnp.int32).astype(jnp.int16)


def decode(ref, lead, col, rows, width):
    k = ref[lead + (pl.ds(rows, TAIL), pl.ds(col, rows))].astype(jnp.int32).astype(jnp.float32)
    s = jnp.exp2(k[:1] * (1.0 / 256.0))
    s = jnp.transpose(jnp.broadcast_to(s, (128, rows)))
    q = ref[lead + (pl.ds(0, rows), pl.ds(col, width))].astype(jnp.int32).astype(jnp.float32)
    return q * jnp.concatenate([s] * (width // 128), axis=1)


def partial_kernel(coded, cols_ref, own_ref, part_ref, c_ref, cp_ref, *outs):
    dims = (((0,), (0,)), ((), ()))
    g = lax.dot_general(own_ref[...], c_ref[...], dims, preferred_element_type=jnp.float32)
    g = g + lax.dot_general(part_ref[...], cp_ref[...], dims, preferred_element_type=jnp.float32)
    half = g.shape[1] // 2
    for i, out in enumerate(outs):
        part = g[:, i * half : (i + 1) * half]
        if coded[i]:
            encode(part, out, (0,), 0)
        else:
            out[0] = part


def partial_sums(coded, cols, hidden, part, cot, cot_part, rows):
    tokens, width = cot.shape
    nz, half = cols.shape[0], width // 2
    shapes = [
        jax.ShapeDtypeStruct((nz, rows + TAIL, half), jnp.int16)
        if k
        else jax.ShapeDtypeStruct((nz, rows, half), jnp.float32)
        for k in coded
    ]
    whole = pl.BlockSpec((tokens, width), lambda i, cols: (0, 0))
    lane = max(rows, 128)
    if rows == lane:
        own_spec = pl.BlockSpec((tokens, rows), lambda i, cols: (0, cols[i]))
        own = hidden
    else:
        own = jnp.stack([lax.dynamic_slice_in_dim(hidden, cols[i] * rows, rows, 1) for i in range(nz)])
        own_spec = pl.BlockSpec((None, tokens, rows), lambda i, cols: (i, 0, 0))
    if part.ndim == 2:
        part_spec = pl.BlockSpec((tokens, rows), lambda i, cols: (0, i))
    else:
        part_spec = pl.BlockSpec((None, tokens, rows), lambda i, cols: (i, 0, 0))
    return pl.pallas_call(
        functools.partial(partial_kernel, coded),
        out_shape=shapes,
        grid_spec=pltpu.PrefetchScalarGridSpec(
            num_scalar_prefetch=1,
            grid=(nz,),
            in_specs=[own_spec, part_spec, whole, whole],
            out_specs=[pl.BlockSpec((1,) + s.shape[1:], lambda i, cols: (i, 0, 0)) for s in shapes],
        ),
        compiler_params=params(),
        cost_estimate=pl.CostEstimate(
            flops=4 * tokens * nz * rows * width, bytes_accessed=4 * tokens * nz * rows + 4 * nz * rows * width, transcendentals=0
        ),
        name="partial_sums",
    )(cols, own, part, cot, cot_part)


def relay_kernel(count, keep_ref, *refs):
    out = refs[count]
    rows, width = keep_ref.shape[1:]
    total = keep_ref[0]
    for ref in refs[:count]:
        total = total + decode(ref, (0,), 0, rows, width)
    encode(total, out, (0,), 0)


def relay(keep, coded):
    nz, rows, width = keep.shape
    spec = pl.BlockSpec((1, rows + TAIL, width), lambda i: (i, 0, 0))
    return pl.pallas_call(
        functools.partial(relay_kernel, len(coded)),
        out_shape=jax.ShapeDtypeStruct((nz, rows + TAIL, width), jnp.int16),
        grid=(nz,),
        in_specs=[pl.BlockSpec((1, rows, width), lambda i: (i, 0, 0))] + [spec] * len(coded),
        out_specs=spec,
        compiler_params=params(),
        name="relay",
    )(keep, *coded)


def corner_kernel(counts, keep_a, keep_b, *refs):
    coded, outs = refs[: sum(counts)], refs[sum(counts) :]
    nz, rows, half = keep_a.shape
    for dz in range(nz):
        for i, keep in enumerate((keep_a, keep_b)):
            total = keep[dz]
            for ref in coded[i * counts[0] : i * counts[0] + counts[i]]:
                total = total + decode(ref, (dz,), 0, rows, half)
            if dz == 0:
                outs[0][:, i * half : (i + 1) * half] = total
            else:
                encode(total, outs[dz], (), i * half)


def corner(keep_a, keep_b, coded_a, coded_b):
    nz, rows, half = keep_a.shape
    shapes = [jax.ShapeDtypeStruct((rows, 2 * half), jnp.float32)]
    shapes += [jax.ShapeDtypeStruct((rows + TAIL, 2 * half), jnp.int16)] * (nz - 1)
    return pl.pallas_call(
        functools.partial(corner_kernel, (len(coded_a), len(coded_b))),
        out_shape=shapes,
        compiler_params=params(),
        name="corner",
    )(keep_a, keep_b, *coded_a, *coded_b)


def total_kernel(tokens, keep_ref, *refs):
    grad_ref, sum_ref = refs[-2:]
    rows, width = keep_ref.shape
    half = width // 2
    square = jnp.zeros((1, 1), jnp.float32)
    for i in range(2):
        total = keep_ref[:, i * half : (i + 1) * half]
        for ref in refs[:-2]:
            total = total + decode(ref, (), i * half, rows, half)
        total = total / tokens
        grad_ref[:, i * half : (i + 1) * half] = total
        square = square + jnp.sum(jnp.sum(total * total, axis=1, keepdims=True), axis=0, keepdims=True)
    sum_ref[...] = jnp.broadcast_to(square, sum_ref.shape)


def total_gradient(tokens, keep, coded):
    return pl.pallas_call(
        functools.partial(total_kernel, tokens),
        out_shape=[jax.ShapeDtypeStruct(keep.shape, jnp.float32), jax.ShapeDtypeStruct((8, 128), jnp.float32)],
        compiler_params=params(),
        name="total_gradient",
    )(keep, *coded)


def adam_kernel(sums_ref, grad_ref, w_ref, f_ref, fs_ref, s_ref, ss_ref, wo, mo, mso, vo, vso):
    sums = sums_ref[...]
    square_sum = jnp.sum(sums, axis=0, keepdims=True)[:, :1]
    factor = jnp.minimum(1.0, clip_norm / (jnp.sqrt(square_sum) + 1e-06))
    rows, width = grad_ref.shape
    blocks = fs_ref.shape[1]
    size = width // blocks
    m_scales, v_scales = [], []
    for i in range(blocks):
        at = slice(i * size, (i + 1) * size)
        clipped = grad_ref[:, at] * factor
        m_old = f_ref[:, at].astype(jnp.float32) * fs_ref[:, i : i + 1]
        v_old = s_ref[:, at].astype(jnp.float32) * ss_ref[:, i : i + 1]
        m_new = beta_first * m_old + (1.0 - beta_first) * clipped
        v_new = beta_second * v_old + (1.0 - beta_second) * clipped * clipped
        m_hat = m_new / (1.0 - beta_first**STEP)
        v_hat = v_new / (1.0 - beta_second**STEP)
        w_old = w_ref[:, at].astype(jnp.float32)
        wo[:, at] = (
            w_old - learn_rate * (m_hat / (jnp.sqrt(v_hat) + adam_epsilon) + weight_decay * w_old)
        ).astype(jnp.bfloat16)
        m_scale = jnp.max(jnp.abs(m_new), axis=1, keepdims=True) + tiny_scale
        v_scale = jnp.max(v_new, axis=1, keepdims=True) + tiny_scale
        mo[:, at] = (m_new / m_scale).astype(jnp.bfloat16)
        vo[:, at] = (v_new / v_scale).astype(jnp.bfloat16)
        mso[:, i : i + 1] = m_scale
        vso[:, i : i + 1] = v_scale


def adam_step(sums, grad, weight, first, first_scale, second, second_scale):
    rows, width = grad.shape
    codes = jax.ShapeDtypeStruct((rows, width), jnp.bfloat16)
    scale = jax.ShapeDtypeStruct(first_scale.shape, jnp.float32)
    return pl.pallas_call(
        adam_kernel,
        out_shape=[codes, codes, scale, codes, scale],
        compiler_params=params(),
        name="adam",
    )(sums, grad, weight, first, first_scale, second, second_scale)


def pack_kernel(start_ref, first_ref, second_ref, out_ref):
    peers, lanes = out_ref.shape[:2]
    for e in range(peers):
        for k in range(lanes):
            s = jnp.minimum(start_ref[e] + k, peers - 1)
            out_ref[e, k, 0] = first_ref[s]
            out_ref[e, k, 1] = second_ref[s]


def pack_units(start, first, second, lanes):
    return pl.pallas_call(
        pack_kernel,
        out_shape=jax.ShapeDtypeStruct((first.shape[0], lanes, 2) + first.shape[1:], first.dtype),
        in_specs=[pl.BlockSpec(memory_space=pltpu.SMEM)] + [pl.BlockSpec(memory_space=pltpu.VMEM)] * 2,
        compiler_params=params(),
        name="pack_units",
    )(start, first, second)


def unpack_kernel(pick_ref, got_ref, first_ref, second_ref):
    peers, lanes = got_ref.shape[:2]
    for u in range(first_ref.shape[0]):
        p = pick_ref[u]
        first_ref[u] = got_ref[p // lanes, p % lanes, 0]
        second_ref[u] = got_ref[p // lanes, p % lanes, 1]


def unpack_units(pick, got):
    units = jax.ShapeDtypeStruct((pick.shape[0],) + got.shape[3:], got.dtype)
    return pl.pallas_call(
        unpack_kernel,
        out_shape=[units, units],
        in_specs=[pl.BlockSpec(memory_space=pltpu.SMEM), pl.BlockSpec(memory_space=pltpu.VMEM)],
        compiler_params=params(),
        name="unpack_units",
    )(pick, got)


def three_parts(a):
    high = lax.reduce_precision(a, 8, 7)
    mid = lax.reduce_precision(a - high, 8, 7)
    low = lax.reduce_precision(a - high - mid, 8, 7)
    return [p.astype(jnp.bfloat16) for p in (high, mid, low)]


def state_by_units(grid, me, w, f, fs, s, ss, counts, key_width):
    peers = grid.size
    slots, block = w.shape
    unit = slots // peers
    per_row = key_width // block
    unit_rows = unit // per_row
    lanes = 2
    row_units = counts[0] // unit
    start = jnp.cumsum(row_units) - row_units
    shape = (peers, unit_rows, key_width)
    packed = pack_units(start, f.reshape(shape), s.reshape(shape), lanes)
    got = lax.all_to_all(packed, AXES, 0, 0, tiled=True)

    pad = lambda a: jnp.pad(a, (0, key_width - a.shape[0]))[None]
    meta = [pad(p) for p in three_parts(fs) + three_parts(ss) + [row_units.astype(jnp.bfloat16)]]
    meta = jnp.concatenate(meta + [jnp.zeros((unit_rows - len(meta), key_width), jnp.bfloat16)])
    payload = jnp.concatenate([meta[None], w.reshape(shape)])
    cut = (peers + 1 + 1) // 2
    along_z = [payload] + [grid.send(payload, dz=dz) for dz in range(1, grid.nz)]
    parts_a = [jnp.stack([p[:cut] for p in along_z])]
    parts_b = [jnp.stack([p[cut:] for p in along_z])]
    for name, parts in (("xy", parts_a), ("yx", parts_b)):
        for axis in name:
            held = parts[0] if len(parts) == 1 else jnp.concatenate(parts)
            for d in range(1, grid.nx if axis == "x" else grid.ny):
                parts.append(grid.send(held, **{"d" + axis: d}))
    parts_a += [grid.send(p, dc=1) for p in parts_a]
    parts_b += [grid.send(p, dc=1) for p in parts_b]
    all_a, all_b = jnp.concatenate(parts_a), jnp.concatenate(parts_b)

    holder = jnp.arange(peers, dtype=jnp.int32)
    dy, dc, dz, dx = (p ^ q for p, q in zip(grid.split(holder), grid.split(me)))
    place_a = ((dc * grid.ny + dy) * grid.nx + dx) * grid.nz + dz
    place_b = ((dc * grid.nx + dx) * grid.ny + dy) * grid.nz + dz
    metas = all_a[:, 0][place_a].astype(jnp.float32)
    all_fs = (metas[:, 0] + metas[:, 1] + metas[:, 2])[:, :slots]
    all_ss = (metas[:, 3] + metas[:, 4] + metas[:, 5])[:, :slots]
    table = metas[:, 6, :peers].astype(jnp.int32)
    starts = jnp.cumsum(table, axis=1) - table
    offsets = jnp.cumsum(table, axis=0) - table

    u = jnp.arange(peers, dtype=jnp.int32)
    ahead = u[None, None, :] - offsets[:, :, None]
    hit = (ahead >= 0) & (ahead < table[:, :, None])
    slot = starts[:, :, None] + ahead
    from_a = place_a[:, None, None] * cut + slot + 1
    from_b = peers * cut + place_b[:, None, None] * (peers + 1 - cut) + slot + 1 - cut
    pick = jnp.sum(jnp.where(hit, jnp.where(slot + 1 < cut, from_a, from_b), 0), axis=0)
    lane = holder[:, None, None] * lanes + ahead
    own = lambda a: lax.dynamic_index_in_dim(a, me, 0, keepdims=False)
    pick_state = own(jnp.sum(jnp.where(hit, lane, 0), axis=0))
    pick_scale = own(jnp.sum(jnp.where(hit, holder[:, None, None] * peers + slot, 0), axis=0))

    units = jnp.concatenate([all_a.reshape(-1, unit_rows, key_width), all_b.reshape(-1, unit_rows, key_width)])
    weight = units[pick.reshape(-1)].reshape(-1, key_width)
    first, second = unpack_units(pick_state, got)
    rows = slots // per_row
    scale = lambda a: a.reshape(peers * peers, unit)[pick_scale].reshape(rows, per_row)
    own_weight = lax.dynamic_slice_in_dim(weight, me * rows, rows, 0)
    two = lambda a: a.reshape(rows, key_width)
    return weight, own_weight, two(first), scale(all_fs), two(second), scale(all_ss)


def state_by_blocks(grid, me, w, f, fs, s, ss, counts, key_width):
    peers = grid.size
    slots, block = w.shape
    per_row = key_width // block
    rows = slots // per_row
    gather = lambda a: lax.all_gather(a, AXES, axis=0, tiled=True)
    table = gather(counts)
    starts = jnp.cumsum(table, axis=1) - table
    offsets = jnp.cumsum(table, axis=0) - table
    j = jnp.arange(slots, dtype=jnp.int32)
    ahead = j[None, None, :] - offsets[:, :, None]
    hit = (ahead >= 0) & (ahead < table[:, :, None])
    holder = jnp.arange(peers, dtype=jnp.int32)[:, None, None]
    pick = jnp.sum(jnp.where(hit, holder * slots + starts[:, :, None] + ahead, 0), axis=0)
    weight = gather(w)[pick.reshape(-1)].reshape(-1, key_width)
    mine = lax.dynamic_index_in_dim(pick, me, 0, keepdims=False)
    own_weight = lax.dynamic_slice_in_dim(weight, me * rows, rows, 0)
    two = lambda a: gather(a)[mine].reshape(rows, key_width)
    scale = lambda a: gather(a)[mine].reshape(rows, per_row)
    return weight, own_weight, two(f), scale(fs), two(s), scale(ss)


def shards(
    hidden_states,
    key_cotangent,
    old_weight,
    old_first,
    old_first_scale,
    old_second,
    old_second_scale,
    send_counts,
):
    grid = Grid(lax.axis_size("cuts"), lax.axis_size("fsdp"))
    me = lax.axis_index(AXES).astype(jnp.int32)
    y, c, z, x = grid.split(me)
    slots, block = old_weight.shape
    key_width = key_cotangent.shape[1]
    rows = slots * block // key_width
    tokens = hidden_states.shape[0]
    peers = grid.size
    per_row = key_width // block
    unit = slots // peers
    by_units = unit % per_row == 0 and unit // per_row >= 8 and slots <= key_width
    state = state_by_units if by_units else state_by_blocks

    groups = [(dy, dx) for dy in range(grid.ny) for dx in range(grid.nx)]
    groups.sort(key=lambda g: (g == (0, 0), not (g[0] and g[1])))

    def columns(dy, dx, core):
        return [grid.join(y ^ dy, core, z ^ dz, x ^ dx) for dz in range(grid.nz)]

    cot_part = grid.send(key_cotangent, dc=1)
    keep, sent = {}, {}
    for dy, dx in groups:
        out = [lax.dynamic_slice_in_dim(hidden_states, o * rows, rows, 1) for o in columns(dy, dx, 1 - c)]
        out = jnp.concatenate(out, axis=1) if rows % 128 == 0 else jnp.stack(out)
        part = grid.send(out, dc=1)
        coded = (dx != 0, dy != 0)
        got = partial_sums(
            coded, jnp.stack(columns(dy, dx, c)), hidden_states, part, key_cotangent, cot_part, rows
        )
        for half in range(2):
            if coded[half]:
                sent[half, dy, dx] = grid.send(got[half], **({"dx": dx} if half == 0 else {"dy": dy}))
            else:
                keep[half, dy, dx] = got[half]
    late = [[], []]
    for dy in range(1, grid.ny):
        late[0].append(grid.send(relay(keep[0, dy, 0], [sent[0, dy, dx] for dx in range(1, grid.nx)]), dy=dy))
    for dx in range(1, grid.nx):
        late[1].append(grid.send(relay(keep[1, 0, dx], [sent[1, dy, dx] for dy in range(1, grid.ny)]), dx=dx))
    mine = corner(
        keep[0, 0, 0],
        keep[1, 0, 0],
        [sent[0, 0, dx] for dx in range(1, grid.nx)] + late[0],
        [sent[1, dy, 0] for dy in range(1, grid.ny)] + late[1],
    )
    over_z = [grid.send(mine[dz], dz=dz) for dz in range(1, grid.nz)]
    gradient, square = total_gradient(tokens * peers, mine[0], over_z)
    sums = lax.all_to_all(
        jnp.broadcast_to(square[None, :1], (peers, 1, 128)), AXES, 0, 0, tiled=True
    ).reshape(peers, 128)

    weight, own_weight, first, first_scale, second, second_scale = state(
        grid, me, old_weight, old_first, old_first_scale, old_second, old_second_scale, send_counts, key_width
    )
    input_grad = lax.dot_general(
        key_cotangent, weight, (((1,), (1,)), ((), ())), preferred_element_type=jnp.float32
    ).astype(jnp.bfloat16)
    w_new, m_code, m_scale, v_code, v_scale = adam_step(
        sums, gradient, own_weight, first, first_scale, second, second_scale
    )
    return input_grad, w_new, m_code, m_scale, v_code, v_scale


def solution(mesh):
    placed = (
        P(("cuts", "fsdp"), None),
        P(("cuts", "fsdp"), None),
        P(("cuts", "fsdp"), None),
        P(("cuts", "fsdp"), None),
        P(("cuts", "fsdp")),
        P(("cuts", "fsdp"), None),
        P(("cuts", "fsdp")),
        P(("cuts", "fsdp"), None),
    )
    return jax.shard_map(
        shards,
        mesh=mesh,
        in_specs=placed,
        out_specs=(
            P(("cuts", "fsdp"), None),
            P(("cuts", "fsdp"), None),
            P(("cuts", "fsdp"), None),
            P(("cuts", "fsdp"), None),
            P(("cuts", "fsdp"), None),
            P(("cuts", "fsdp"), None),
        ),
        check_vma=False,
    )
```

```python
import functools

import jax
import jax.numpy as jnp
from jax import lax
from jax.experimental import pallas as pl
from jax.experimental.pallas import tpu as pltpu
from jax.sharding import PartitionSpec as P

STEP = 2000


beta_first = 0.9
beta_second = 0.95
adam_epsilon = 1e-05
learn_rate = 0.001
weight_decay = 0.1
clip_norm = 1.0
tiny_scale = 1e-30

AXES = ("cuts", "fsdp")
LIMIT = 48 * 1024 * 1024
TAIL = 16


class Grid:
    def __init__(self, cuts, fsdp):
        self.cuts, self.fsdp = cuts, fsdp
        self.ny = cuts // 2
        self.nz = 4
        self.nx = fsdp // 4
        self.size = cuts * fsdp

    def split(self, i):
        x = i % self.nx
        z = (i // self.nx) % self.nz
        c = (i // self.fsdp) % 2
        y = i // (2 * self.fsdp)
        return y, c, z, x

    def join(self, y, c, z, x):
        return ((y * 2 + c) * self.nz + z) * self.nx + x

    def send(self, a, dy=0, dc=0, dz=0, dx=0):
        pairs = []
        for i in range(self.size):
            y, c, z, x = self.split(i)
            pairs.append((i, self.join(y ^ dy, c ^ dc, z ^ dz, x ^ dx)))
        return lax.ppermute(a, AXES, pairs)


def params():
    return pltpu.CompilerParams(vmem_limit_bytes=LIMIT)


def encode(g):
    top = jnp.max(jnp.abs(g), axis=0, keepdims=True)
    k = jnp.ceil(jnp.log2(jnp.maximum(top, 1e-30) / 32700.0) * 256.0)
    q = jnp.round(g * jnp.exp2(k * (-1.0 / 256.0)))
    return q.astype(jnp.int32).astype(jnp.int16), k


def tail_rows(ks, columns):
    filled = jnp.concatenate(list(ks) + [jnp.zeros((TAIL - len(ks), columns), jnp.float32)])
    return filled.astype(jnp.int32).astype(jnp.int16)


def scales_of(ref, row):
    k = ref[pl.ds(row, TAIL), :].astype(jnp.int32).astype(jnp.float32)
    return jnp.exp2(k * (1.0 / 256.0))


def decode(ref, row, rows, scale):
    return ref[pl.ds(row, rows), :].astype(jnp.int32).astype(jnp.float32) * scale


def copy_kernel(cols_ref, in_ref, out_ref):
    out_ref[...] = in_ref[...]


def pick_columns(cols, hidden, rows):
    nz, tokens = cols.shape[0], hidden.shape[0]
    if rows % 128:
        return jnp.stack([lax.dynamic_slice_in_dim(hidden, cols[i] * rows, rows, 1) for i in range(nz)])
    return pl.pallas_call(
        copy_kernel,
        out_shape=jax.ShapeDtypeStruct((nz, tokens, rows), hidden.dtype),
        grid_spec=pltpu.PrefetchScalarGridSpec(
            num_scalar_prefetch=1,
            grid=(nz,),
            in_specs=[pl.BlockSpec((tokens, rows), lambda i, cols: (0, cols[i]))],
            out_specs=pl.BlockSpec((None, tokens, rows), lambda i, cols: (i, 0, 0)),
        ),
        compiler_params=params(),
        name="pick_columns",
    )(cols, hidden)


def partial_kernel(coded, cols_ref, own_ref, part_ref, c_ref, cp_ref, *refs):
    outs, scale_refs = refs[:2], refs[2:]
    step, steps = pl.program_id(0), pl.num_programs(0)
    g = jnp.dot(c_ref[...], own_ref[...], preferred_element_type=jnp.float32)
    g = g + jnp.dot(cp_ref[...], part_ref[...], preferred_element_type=jnp.float32)
    half = g.shape[0] // 2
    for i, out in enumerate(outs):
        part = g[i * half : (i + 1) * half]
        if not coded[i]:
            out[0] = part
            continue
        q, k = encode(part)
        out[pl.ds(pl.multiple_of(step * half, half), half), :] = q
        kept = scale_refs[i]
        kept[pl.ds(step, 1), :] = k

        @pl.when(step == steps - 1)
        def _(out=out, kept=kept):
            count = out.shape[0] - TAIL
            nz = count // half
            out[pl.ds(count, TAIL), :] = tail_rows([kept[:nz, :]], kept.shape[1]) if nz == TAIL else jnp.concatenate(
                [kept[:nz, :], jnp.zeros((TAIL - nz, kept.shape[1]), jnp.float32)]
            ).astype(jnp.int32).astype(jnp.int16)


def partial_sums(coded, cols, hidden, part, cot, cot_part, rows):
    width, tokens = cot.shape
    nz, half = cols.shape[0], width // 2
    shapes = [
        jax.ShapeDtypeStruct((nz * half + TAIL, rows), jnp.int16)
        if k
        else jax.ShapeDtypeStruct((nz, half, rows), jnp.float32)
        for k in coded
    ]
    whole = pl.BlockSpec((width, tokens), lambda i, cols: (0, 0))
    block = pl.BlockSpec((None, tokens, rows), lambda i, cols: (i, 0, 0))
    if rows % 128 == 0:
        own_spec, own = pl.BlockSpec((tokens, rows), lambda i, cols: (0, cols[i])), hidden
    else:
        own_spec, own = block, pick_columns(cols, hidden, rows)
    return pl.pallas_call(
        functools.partial(partial_kernel, coded),
        out_shape=shapes,
        grid_spec=pltpu.PrefetchScalarGridSpec(
            num_scalar_prefetch=1,
            grid=(nz,),
            in_specs=[own_spec, block, whole, whole],
            out_specs=[
                pl.BlockSpec(s.shape, lambda i, cols: (0, 0))
                if k
                else pl.BlockSpec((1, half, rows), lambda i, cols: (i, 0, 0))
                for k, s in zip(coded, shapes)
            ],
            scratch_shapes=[pltpu.VMEM((8, rows), jnp.float32)] * 2,
        ),
        compiler_params=params(),
        cost_estimate=pl.CostEstimate(
            flops=4 * tokens * nz * rows * width, bytes_accessed=4 * tokens * nz * rows + 4 * nz * rows * width, transcendentals=0
        ),
        name="partial_sums",
    )(cols, own, part, cot, cot_part)


def relay_kernel(count, keep_ref, *refs):
    out = refs[count]
    nz, half, rows = keep_ref.shape
    scales = [scales_of(ref, nz * half) for ref in refs[:count]]
    ks = []
    for i in range(nz):
        total = keep_ref[i]
        for ref, s in zip(refs[:count], scales):
            total = total + decode(ref, i * half, half, s[i : i + 1])
        q, k = encode(total)
        out[pl.ds(i * half, half), :] = q
        ks.append(k)
    out[pl.ds(nz * half, TAIL), :] = tail_rows(ks, rows)


def relay(keep, coded):
    nz, half, rows = keep.shape
    return pl.pallas_call(
        functools.partial(relay_kernel, len(coded)),
        out_shape=jax.ShapeDtypeStruct((nz * half + TAIL, rows), jnp.int16),
        compiler_params=params(),
        name="relay",
    )(keep, *coded)


def corner_kernel(counts, keep_a, keep_b, *refs):
    coded, outs = refs[: sum(counts)], refs[sum(counts) :]
    nz, half, rows = keep_a.shape
    scales = [scales_of(ref, nz * half) for ref in coded]
    for dz in range(nz):
        ks = []
        for i, keep in enumerate((keep_a, keep_b)):
            total = keep[dz]
            for j in range(i * counts[0], i * counts[0] + counts[i]):
                total = total + decode(coded[j], dz * half, half, scales[j][dz : dz + 1])
            if dz == 0:
                outs[0][pl.ds(i * half, half), :] = total
            else:
                q, k = encode(total)
                outs[dz][pl.ds(i * half, half), :] = q
                ks.append(k)
        if dz:
            outs[dz][pl.ds(2 * half, TAIL), :] = tail_rows(ks, rows)


def corner(keep_a, keep_b, coded_a, coded_b):
    nz, half, rows = keep_a.shape
    shapes = [jax.ShapeDtypeStruct((2 * half, rows), jnp.float32)]
    shapes += [jax.ShapeDtypeStruct((2 * half + TAIL, rows), jnp.int16)] * (nz - 1)
    return pl.pallas_call(
        functools.partial(corner_kernel, (len(coded_a), len(coded_b))),
        out_shape=shapes,
        compiler_params=params(),
        name="corner",
    )(keep_a, keep_b, *coded_a, *coded_b)


def total_kernel(tokens, keep_ref, *refs):
    grad_ref, sum_ref = refs[-2:]
    width, rows = keep_ref.shape
    half = width // 2
    scales = [scales_of(ref, width) for ref in refs[:-2]]
    square = jnp.zeros((1, rows), jnp.float32)
    for i in range(2):
        total = keep_ref[pl.ds(i * half, half), :]
        for ref, s in zip(refs[:-2], scales):
            total = total + decode(ref, i * half, half, s[i : i + 1])
        total = total / tokens
        grad_ref[:, i * half : (i + 1) * half] = jnp.transpose(total)
        square = square + jnp.sum(total * total, axis=0, keepdims=True)
    sum_ref[...] = jnp.broadcast_to(jnp.sum(square, axis=1, keepdims=True), sum_ref.shape)


def total_gradient(tokens, keep, coded):
    width, rows = keep.shape
    return pl.pallas_call(
        functools.partial(total_kernel, tokens),
        out_shape=[jax.ShapeDtypeStruct((rows, width), jnp.float32), jax.ShapeDtypeStruct((8, 128), jnp.float32)],
        compiler_params=params(),
        name="total_gradient",
    )(keep, *coded)


def adam_kernel(sums_ref, grad_ref, w_ref, f_ref, fs_ref, s_ref, ss_ref, wo, mo, mso, vo, vso):
    sums = sums_ref[...]
    square_sum = jnp.sum(sums, axis=0, keepdims=True)[:, :1]
    factor = jnp.minimum(1.0, clip_norm / (jnp.sqrt(square_sum) + 1e-06))
    rows, width = grad_ref.shape
    blocks = fs_ref.shape[1]
    size = width // blocks
    for i in range(blocks):
        at = slice(i * size, (i + 1) * size)
        clipped = grad_ref[:, at] * factor
        m_old = f_ref[:, at].astype(jnp.float32) * fs_ref[:, i : i + 1]
        v_old = s_ref[:, at].astype(jnp.float32) * ss_ref[:, i : i + 1]
        m_new = beta_first * m_old + (1.0 - beta_first) * clipped
        v_new = beta_second * v_old + (1.0 - beta_second) * clipped * clipped
        m_hat = m_new / (1.0 - beta_first**STEP)
        v_hat = v_new / (1.0 - beta_second**STEP)
        w_old = w_ref[:, at].astype(jnp.float32)
        wo[:, at] = (
            w_old - learn_rate * (m_hat / (jnp.sqrt(v_hat) + adam_epsilon) + weight_decay * w_old)
        ).astype(jnp.bfloat16)
        m_scale = jnp.max(jnp.abs(m_new), axis=1, keepdims=True) + tiny_scale
        v_scale = jnp.max(v_new, axis=1, keepdims=True) + tiny_scale
        mo[:, at] = (m_new / m_scale).astype(jnp.bfloat16)
        vo[:, at] = (v_new / v_scale).astype(jnp.bfloat16)
        mso[i : i + 1, :] = jnp.transpose(jnp.broadcast_to(m_scale, (rows, 128)))[:1]
        vso[i : i + 1, :] = jnp.transpose(jnp.broadcast_to(v_scale, (rows, 128)))[:1]


def adam_step(sums, grad, weight, first, first_scale, second, second_scale):
    rows, width = grad.shape
    codes = jax.ShapeDtypeStruct((rows, width), jnp.bfloat16)
    scale = jax.ShapeDtypeStruct(first_scale.shape[::-1], jnp.float32)
    w_new, m_code, m_scale, v_code, v_scale = pl.pallas_call(
        adam_kernel,
        out_shape=[codes, codes, scale, codes, scale],
        compiler_params=params(),
        name="adam",
    )(sums, grad, weight, first, first_scale, second, second_scale)
    return w_new, m_code, m_scale.T, v_code, v_scale.T


def pack_kernel(start_ref, first_ref, second_ref, out_ref):
    peers, lanes = out_ref.shape[:2]
    for e in range(peers):
        for k in range(lanes):
            s = jnp.minimum(start_ref[e] + k, peers - 1)
            out_ref[e, k, 0] = first_ref[s]
            out_ref[e, k, 1] = second_ref[s]


def pack_units(start, first, second, lanes):
    return pl.pallas_call(
        pack_kernel,
        out_shape=jax.ShapeDtypeStruct((first.shape[0], lanes, 2) + first.shape[1:], first.dtype),
        in_specs=[pl.BlockSpec(memory_space=pltpu.SMEM)] + [pl.BlockSpec(memory_space=pltpu.VMEM)] * 2,
        compiler_params=params(),
        name="pack_units",
    )(start, first, second)


def unpack_kernel(pick_ref, got_ref, first_ref, second_ref):
    peers, lanes = got_ref.shape[:2]
    for u in range(first_ref.shape[0]):
        p = pick_ref[u]
        first_ref[u] = got_ref[p // lanes, p % lanes, 0]
        second_ref[u] = got_ref[p // lanes, p % lanes, 1]


def unpack_units(pick, got):
    units = jax.ShapeDtypeStruct((pick.shape[0],) + got.shape[3:], got.dtype)
    return pl.pallas_call(
        unpack_kernel,
        out_shape=[units, units],
        in_specs=[pl.BlockSpec(memory_space=pltpu.SMEM), pl.BlockSpec(memory_space=pltpu.VMEM)],
        compiler_params=params(),
        name="unpack_units",
    )(pick, got)


def split_kernel(*refs):
    out_a, out_b = refs[-2:]
    cut = out_a.shape[1]
    for i, ref in enumerate(refs[:-2]):
        out_a[i] = ref[:cut]
        out_b[i] = ref[cut:]


def split_units(parts):
    count, (units, rows, width) = len(parts), parts[0].shape
    shape = jax.ShapeDtypeStruct((count, units // 2, rows, width), parts[0].dtype)
    return pl.pallas_call(
        split_kernel,
        out_shape=[shape, shape],
        compiler_params=params(),
        name="split_units",
    )(*parts)


def product_kernel(count, group, pick_ref, cot_ref, *refs):
    parts, (out_ref, own_ref, held, tile, sems) = refs[:count], refs[count:]
    step = pl.program_id(0)
    copies, at = [], 0
    for i, ref in enumerate(parts):
        copies.append(pltpu.make_async_copy(ref, held.at[pl.ds(at, ref.shape[0])], sems.at[i]))
        at += ref.shape[0]

    @pl.when(step == 0)
    def _():
        for copy in copies:
            copy.start()
        for copy in copies:
            copy.wait()

    for u in range(group):
        tile[u] = held[pick_ref[step * group + u]]
    weight = tile[...].reshape(group * tile.shape[1], tile.shape[2])
    out_ref[...] = lax.dot_general(
        cot_ref[...], weight, (((1,), (1,)), ((), ())), preferred_element_type=jnp.float32
    ).astype(out_ref.dtype)

    @pl.when(step == 0)
    def _():
        first = pick_ref.shape[0] - own_ref.shape[0]
        for u in range(own_ref.shape[0]):
            own_ref[u] = held[pick_ref[first + u]]


def product(pick, cot, parts, own_units):
    rows, width = parts[0].shape[-2:]
    parts = [p.reshape(-1, rows, width) for p in parts]
    total = pick.shape[0] - own_units
    group = 64
    tokens = cot.shape[0]
    return pl.pallas_call(
        functools.partial(product_kernel, len(parts), group),
        out_shape=[
            jax.ShapeDtypeStruct((tokens, total * rows), cot.dtype),
            jax.ShapeDtypeStruct((own_units, rows, width), cot.dtype),
        ],
        grid_spec=pltpu.PrefetchScalarGridSpec(
            num_scalar_prefetch=1,
            grid=(total // group,),
            in_specs=[pl.BlockSpec((tokens, width), lambda i, pick: (0, 0))] + [pl.BlockSpec(memory_space=pl.ANY)] * len(parts),
            out_specs=[
                pl.BlockSpec((tokens, group * rows), lambda i, pick: (0, i)),
                pl.BlockSpec((own_units, rows, width), lambda i, pick: (0, 0, 0)),
            ],
            scratch_shapes=[
                pltpu.VMEM((sum(p.shape[0] for p in parts), rows, width), cot.dtype),
                pltpu.VMEM((group, rows, width), cot.dtype),
                pltpu.SemaphoreType.DMA((len(parts),)),
            ],
        ),
        compiler_params=params(),
        cost_estimate=pl.CostEstimate(
            flops=2 * tokens * total * rows * width, bytes_accessed=4 * total * rows * width, transcendentals=0
        ),
        name="product",
    )(pick, cot, *parts)


def after(a, *others):
    return lax.optimization_barrier((a, others))[0]


def state_by_units(grid, me, cot, w, f, fs, s, ss, counts, key_width, gates):
    peers = grid.size
    slots, block = w.shape
    unit = slots // peers
    per_row = key_width // block
    unit_rows = unit // per_row
    lanes = 2
    shape = (peers, unit_rows, key_width)
    facts = jnp.concatenate([fs, ss, counts[0].astype(jnp.float32)])[None]
    facts = jnp.broadcast_to(facts[None], (peers,) + facts.shape)
    facts = lax.all_to_all(facts, AXES, 0, 0, tiled=True)[:, 0]

    row_units = counts[0] // unit
    start = jnp.cumsum(row_units) - row_units
    packed = pack_units(after(start, gates[1]), f.reshape(shape), s.reshape(shape), lanes)
    got = lax.all_to_all(packed, AXES, 0, 0, tiled=True)

    mine = after(w, gates[0]).reshape(shape)
    split = split_units([mine] + [grid.send(mine, dz=dz) for dz in range(1, grid.nz)])
    split = after(split, gates[2])
    spread = []
    for half in range(2):
        held = {(0, 0): split[half]}
        for d in range(1, grid.nx if half == 0 else grid.ny):
            move = {"dx": d} if half == 0 else {"dy": d}
            held[(0, d) if half == 0 else (d, 0)] = grid.send(split[half], **move)
        for at, part in list(held.items()):
            for d in range(1, grid.ny if half == 0 else grid.nx):
                move = {"dy": d} if half == 0 else {"dx": d}
                held[(d, at[1]) if half == 0 else (at[0], d)] = grid.send(part, **move)
        spread.append([held[dy, dx] for dy in range(grid.ny) for dx in range(grid.nx)])
    spread = [parts + [grid.send(p, dc=1) for p in parts] for parts in spread]

    holder = jnp.arange(peers, dtype=jnp.int32)
    dy, dc, dz, dx = (p ^ q for p, q in zip(grid.split(holder), grid.split(me)))
    place = ((dc * grid.ny + dy) * grid.nx + dx) * grid.nz + dz
    table = facts[:, 2 * slots :].astype(jnp.int32) // unit
    starts = jnp.cumsum(table, axis=1) - table
    offsets = jnp.cumsum(table, axis=0) - table

    u = jnp.arange(peers, dtype=jnp.int32)
    ahead = u[None, None, :] - offsets[:, :, None]
    hit = (ahead >= 0) & (ahead < table[:, :, None])
    slot = starts[:, :, None] + ahead
    cut = peers // 2
    from_place = jnp.where(slot < cut, 0, peers * cut - cut) + place[:, None, None] * cut + slot
    pick = jnp.sum(jnp.where(hit, from_place, 0), axis=0)
    lane = holder[:, None, None] * lanes + ahead
    own = lambda a: lax.dynamic_index_in_dim(a, me, 0, keepdims=False)
    pick_state = own(jnp.sum(jnp.where(hit, lane, 0), axis=0))
    pick_scale = own(jnp.sum(jnp.where(hit, holder[:, None, None] * peers + slot, 0), axis=0))

    pick = jnp.concatenate([pick.reshape(-1), own(pick)])
    input_grad, own_weight = product(pick, cot, spread[0] + spread[1], peers)
    first, second = unpack_units(pick_state, got)
    rows = slots // per_row
    scale = lambda a: a.reshape(peers * peers, unit)[pick_scale].reshape(rows, per_row)
    two = lambda a: a.reshape(rows, key_width)
    return input_grad, two(own_weight), two(first), scale(facts[:, :slots]), two(second), scale(facts[:, slots : 2 * slots])


def state_by_blocks(grid, me, cot, w, f, fs, s, ss, counts, key_width, gates):
    peers = grid.size
    slots, block = w.shape
    per_row = key_width // block
    rows = slots // per_row
    gather = lambda a: lax.all_gather(a, AXES, axis=0, tiled=True)
    table = gather(counts)
    starts = jnp.cumsum(table, axis=1) - table
    offsets = jnp.cumsum(table, axis=0) - table
    j = jnp.arange(slots, dtype=jnp.int32)
    ahead = j[None, None, :] - offsets[:, :, None]
    hit = (ahead >= 0) & (ahead < table[:, :, None])
    holder = jnp.arange(peers, dtype=jnp.int32)[:, None, None]
    pick = jnp.sum(jnp.where(hit, holder * slots + starts[:, :, None] + ahead, 0), axis=0)
    weight = gather(w)[pick.reshape(-1)].reshape(-1, key_width)
    mine = lax.dynamic_index_in_dim(pick, me, 0, keepdims=False)
    own_weight = lax.dynamic_slice_in_dim(weight, me * rows, rows, 0)
    two = lambda a: gather(a)[mine].reshape(rows, key_width)
    scale = lambda a: gather(a)[mine].reshape(rows, per_row)
    input_grad = lax.dot_general(
        cot, weight, (((1,), (1,)), ((), ())), preferred_element_type=jnp.float32
    ).astype(jnp.bfloat16)
    return input_grad, own_weight, two(f), scale(fs), two(s), scale(ss)


def shards(
    hidden_states,
    key_cotangent,
    old_weight,
    old_first,
    old_first_scale,
    old_second,
    old_second_scale,
    send_counts,
):
    grid = Grid(lax.axis_size("cuts"), lax.axis_size("fsdp"))
    me = lax.axis_index(AXES).astype(jnp.int32)
    y, c, z, x = grid.split(me)
    slots, block = old_weight.shape
    key_width = key_cotangent.shape[1]
    rows = slots * block // key_width
    tokens = hidden_states.shape[0]
    peers = grid.size
    per_row = key_width // block
    unit = slots // peers
    by_units = unit % per_row == 0 and unit // per_row >= 8 and peers % 2 == 0
    state = state_by_units if by_units else state_by_blocks

    groups = [(dy, dx) for dy in range(grid.ny) for dx in range(grid.nx)]
    groups.sort(key=lambda g: (g == (0, 0), not (g[0] and g[1])))

    def columns(dy, dx, core):
        return jnp.stack([grid.join(y ^ dy, core, z ^ dz, x ^ dx) for dz in range(grid.nz)])

    cot = key_cotangent.T
    cot_part = grid.send(cot, dc=1)
    keep, sent = {}, {}
    arrived, last = None, None
    for dy, dx in groups:
        part = grid.send(pick_columns(columns(dy, dx, 1 - c), hidden_states, rows), dc=1)
        if arrived is None:
            arrived = part
        coded = (dx != 0, dy != 0)
        got = partial_sums(coded, columns(dy, dx, c), hidden_states, part, cot, cot_part, rows)
        last = got
        for half in range(2):
            if coded[half]:
                sent[half, dy, dx] = grid.send(got[half], **({"dx": dx} if half == 0 else {"dy": dy}))
            else:
                keep[half, dy, dx] = got[half]
    late, coded_late = [[], []], []
    for dy in range(1, grid.ny):
        coded_late.append(relay(keep[0, dy, 0], [sent[0, dy, dx] for dx in range(1, grid.nx)]))
        late[0].append(grid.send(coded_late[-1], dy=dy))
    for dx in range(1, grid.nx):
        coded_late.append(relay(keep[1, 0, dx], [sent[1, dy, dx] for dy in range(1, grid.ny)]))
        late[1].append(grid.send(coded_late[-1], dx=dx))
    mine = corner(
        keep[0, 0, 0],
        keep[1, 0, 0],
        [sent[0, 0, dx] for dx in range(1, grid.nx)] + late[0],
        [sent[1, dy, 0] for dy in range(1, grid.ny)] + late[1],
    )
    over_z = [grid.send(mine[dz], dz=dz) for dz in range(1, grid.nz)]
    gradient, square = total_gradient(tokens * peers, mine[0], over_z)
    sums = lax.all_to_all(
        jnp.broadcast_to(square[None, :1], (peers, 1, 128)), AXES, 0, 0, tiled=True
    ).reshape(peers, 128)

    gates = (arrived, last, coded_late)
    input_grad, own_weight, first, first_scale, second, second_scale = state(
        grid, me, key_cotangent, old_weight, old_first, old_first_scale, old_second, old_second_scale, send_counts, key_width, gates
    )
    w_new, m_code, m_scale, v_code, v_scale = adam_step(
        sums, gradient, own_weight, first, first_scale, second, second_scale
    )
    return input_grad, w_new, m_code, m_scale, v_code, v_scale


def solution(mesh):
    placed = (
        P(("cuts", "fsdp"), None),
        P(("cuts", "fsdp"), None),
        P(("cuts", "fsdp"), None),
        P(("cuts", "fsdp"), None),
        P(("cuts", "fsdp")),
        P(("cuts", "fsdp"), None),
        P(("cuts", "fsdp")),
        P(("cuts", "fsdp"), None),
    )
    return jax.shard_map(
        shards,
        mesh=mesh,
        in_specs=placed,
        out_specs=(
            P(("cuts", "fsdp"), None),
            P(("cuts", "fsdp"), None),
            P(("cuts", "fsdp"), None),
            P(("cuts", "fsdp"), None),
            P(("cuts", "fsdp"), None),
            P(("cuts", "fsdp"), None),
        ),
        check_vma=False,
    )
```

```python
import functools

import jax
import jax.numpy as jnp
from jax import lax
from jax.experimental import pallas as pl
from jax.experimental.pallas import tpu as pltpu
from jax.sharding import PartitionSpec as P

STEP = 2000


beta_first = 0.9
beta_second = 0.95
adam_epsilon = 1e-05
learn_rate = 0.001
weight_decay = 0.1
clip_norm = 1.0
tiny_scale = 1e-30

AXES = ("cuts", "fsdp")
TAIL = 16
GROUP = 128


class Grid:
    def __init__(self, cuts, fsdp):
        self.cuts, self.fsdp = cuts, fsdp
        self.ny = cuts // 2
        self.nz = 4
        self.nx = fsdp // 4
        self.size = cuts * fsdp

    def split(self, i):
        x = i % self.nx
        z = (i // self.nx) % self.nz
        c = (i // self.fsdp) % 2
        y = i // (2 * self.fsdp)
        return y, c, z, x

    def join(self, y, c, z, x):
        return ((y * 2 + c) * self.nz + z) * self.nx + x

    def send(self, a, dy=0, dc=0, dz=0, dx=0):
        pairs = []
        for i in range(self.size):
            y, c, z, x = self.split(i)
            pairs.append((i, self.join(y ^ dy, c ^ dc, z ^ dz, x ^ dx)))
        return lax.ppermute(a, AXES, pairs)


SMALL = pl.CostEstimate(flops=1, bytes_accessed=1, transcendentals=0)


def params(mib):
    return pltpu.CompilerParams(vmem_limit_bytes=mib * 1024 * 1024)


def encode(g):
    top = jnp.max(jnp.abs(g), axis=0, keepdims=True)
    k = jnp.ceil(jnp.log2(jnp.maximum(top, 1e-30) / 32700.0) * 256.0)
    q = jnp.round(g * jnp.exp2(k * (-1.0 / 256.0)))
    return q.astype(jnp.int32).astype(jnp.int16), k


def tail_rows(ks, columns):
    filled = list(ks)
    if len(ks) < TAIL:
        filled.append(jnp.zeros((TAIL - len(ks), columns), jnp.float32))
    filled = jnp.concatenate(filled)
    return filled.astype(jnp.int32).astype(jnp.int16)


def scales_of(ref, row):
    k = ref[pl.ds(row, TAIL), :].astype(jnp.int32).astype(jnp.float32)
    return jnp.exp2(k * (1.0 / 256.0))


def decode(ref, row, rows, scale):
    return ref[pl.ds(row, rows), :].astype(jnp.int32).astype(jnp.float32) * scale


def pick_kernel(grid, core, groups, me_ref, hidden_ref, *refs):
    out, sems = refs[-2:]
    rows = out.shape[2]
    y, c, z, x = grid.split(me_ref[0])
    owners = [grid.join(y ^ dy, c ^ core, z ^ dz, x ^ dx) for dy, dx in groups for dz in range(grid.nz)]
    copies = []
    for i, owner in enumerate(owners):
        at = pl.multiple_of(owner * rows, rows)
        copies.append(pltpu.make_async_copy(hidden_ref.at[:, pl.ds(at, rows)], out.at[i], sems.at[i]))
    for i in range(len(owners), out.shape[0]):
        at = (i - len(owners)) * rows
        copies.append(pltpu.make_async_copy(refs[0].at[:, pl.ds(at, rows)], out.at[i], sems.at[i]))
    for copy in copies:
        copy.start()
    for copy in copies:
        copy.wait()


def pick_columns(grid, me, core, groups, hidden, rows, *more):
    tokens = hidden.shape[0]
    if rows % 128:
        cut = lambda a, at: lax.dynamic_slice_in_dim(a, at * rows, rows, 1)
        y, c, z, x = grid.split(me[0])
        owners = [grid.join(y ^ dy, c ^ core, z ^ dz, x ^ dx) for dy, dx in groups for dz in range(grid.nz)]
        return jnp.stack([cut(hidden, o) for o in owners] + [cut(a, i) for a in more for i in range(a.shape[1] // rows)])
    blocks = len(groups) * grid.nz + sum(a.shape[1] // rows for a in more)
    return pl.pallas_call(
        functools.partial(pick_kernel, grid, core, groups),
        out_shape=jax.ShapeDtypeStruct((blocks, tokens, rows), hidden.dtype),
        in_specs=[pl.BlockSpec(memory_space=pltpu.SMEM)] + [pl.BlockSpec(memory_space=pl.ANY)] * (1 + len(more)),
        out_specs=pl.BlockSpec(memory_space=pltpu.VMEM),
        scratch_shapes=[pltpu.SemaphoreType.DMA((blocks,))],
        compiler_params=params(56),
        cost_estimate=SMALL,
        name="pick_columns",
    )(me, hidden, *more)


def partial_kernel(coded, jobs, nz, count, c_ref, *refs):
    owns, parts, out = refs[:count], refs[count:-1], refs[-1]
    tokens, width = c_ref.shape
    half, rows = width // 2, owns[0].shape[2]
    last = parts[0].shape[0] - width // rows
    across = (((0,), (0,)), ((), ()))
    ks = []
    for n, (which, at, side) in enumerate(jobs):
        mine = c_ref[:, side * half : (side + 1) * half]
        blocks = range(last + side * half // rows, last + (side + 1) * half // rows)
        other = [parts[0][b] for b in blocks]
        other = other[0] if len(other) == 1 else jnp.concatenate(other, axis=1)
        for i in range(nz):
            g = lax.dot_general(mine, owns[which][at + i], across, preferred_element_type=jnp.float32)
            g = g + lax.dot_general(other, parts[which][at + i], across, preferred_element_type=jnp.float32)
            if coded:
                q, k = encode(g)
                out[pl.ds((n * nz + i) * half, half), :] = q
                ks.append(k)
            else:
                out[n * nz + i] = g
    if coded:
        out[pl.ds(len(jobs) * nz * half, TAIL), :] = tail_rows(ks, rows)


def partial_sums(coded, jobs, nz, cot, owns, parts):
    _, width = cot.shape
    half, rows = width // 2, owns[0].shape[2]
    blocks = len(jobs) * nz
    return pl.pallas_call(
        functools.partial(partial_kernel, coded, jobs, nz, len(owns)),
        out_shape=jax.ShapeDtypeStruct((blocks * half + TAIL, rows), jnp.int16)
        if coded
        else jax.ShapeDtypeStruct((blocks, half, rows), jnp.float32),
        compiler_params=params(24),
        cost_estimate=SMALL,
        name="partial_sums",
    )(cot, *owns, *parts)


def relay_kernel(keep_at, coded_at, nz, keep_ref, *refs):
    coded, out = refs[:-1], refs[-1]
    _, half, rows = keep_ref.shape
    tables = [scales_of(ref, ref.shape[0] - TAIL) for ref in coded]
    ks = []
    for i in range(nz):
        total = keep_ref[keep_at + i]
        for ref, s in zip(coded, tables):
            at = coded_at + i
            total = total + decode(ref, at * half, half, s[at : at + 1])
        q, k = encode(total)
        out[pl.ds(i * half, half), :] = q
        ks.append(k)
    out[pl.ds(nz * half, TAIL), :] = tail_rows(ks, rows)


def relay(nz, keep, keep_at, coded, coded_at):
    _, half, rows = keep.shape
    return pl.pallas_call(
        functools.partial(relay_kernel, keep_at, coded_at, nz),
        out_shape=jax.ShapeDtypeStruct((nz * half + TAIL, rows), jnp.int16),
        compiler_params=params(14),
        cost_estimate=SMALL,
        name="relay",
    )(keep, *coded)


def corner_kernel(counts, keep_at, nz, keep_ref, *refs):
    coded, outs = refs[: sum(counts)], refs[sum(counts) :]
    _, half, rows = keep_ref.shape
    tables = [scales_of(ref, ref.shape[0] - TAIL) for ref in coded]
    for dz in range(nz):
        ks = []
        for i in range(2):
            total = keep_ref[keep_at[i] + dz]
            for j in range(i * counts[0], i * counts[0] + counts[i]):
                total = total + decode(coded[j], dz * half, half, tables[j][dz : dz + 1])
            if dz == 0:
                outs[0][pl.ds(i * half, half), :] = total
            else:
                q, k = encode(total)
                outs[dz][pl.ds(i * half, half), :] = q
                ks.append(k)
        if dz:
            outs[dz][pl.ds(2 * half, TAIL), :] = tail_rows(ks, rows)


def corner(nz, keep, keep_at, coded_a, coded_b):
    _, half, rows = keep.shape
    shapes = [jax.ShapeDtypeStruct((2 * half, rows), jnp.float32)]
    shapes += [jax.ShapeDtypeStruct((2 * half + TAIL, rows), jnp.int16)] * (nz - 1)
    return pl.pallas_call(
        functools.partial(corner_kernel, (len(coded_a), len(coded_b)), keep_at, nz),
        out_shape=shapes,
        compiler_params=params(18),
        cost_estimate=SMALL,
        name="corner",
    )(keep, *coded_a, *coded_b)


def total_kernel(tokens, keep_ref, *refs):
    grad_ref, sum_ref = refs[-2:]
    width, rows = keep_ref.shape
    half = width // 2
    scales = [scales_of(ref, width) for ref in refs[:-2]]
    square = jnp.zeros((1, rows), jnp.float32)
    for i in range(2):
        total = keep_ref[pl.ds(i * half, half), :]
        for ref, s in zip(refs[:-2], scales):
            total = total + decode(ref, i * half, half, s[i : i + 1])
        total = total / tokens
        grad_ref[:, i * half : (i + 1) * half] = jnp.transpose(total)
        square = square + jnp.sum(total * total, axis=0, keepdims=True)
    sum_ref[...] = jnp.broadcast_to(jnp.sum(square, axis=1, keepdims=True), sum_ref.shape)


def total_gradient(tokens, keep, coded):
    width, rows = keep.shape
    return pl.pallas_call(
        functools.partial(total_kernel, tokens),
        out_shape=[jax.ShapeDtypeStruct((rows, width), jnp.float32), jax.ShapeDtypeStruct((8, 128), jnp.float32)],
        compiler_params=params(6),
        cost_estimate=SMALL,
        name="total_gradient",
    )(keep, *coded)


def adam_kernel(sums_ref, grad_ref, w_ref, f_ref, fs_ref, s_ref, ss_ref, wo, mo, mso, vo, vso):
    sums = sums_ref[...]
    square_sum = jnp.sum(sums, axis=0, keepdims=True)[:, :1]
    factor = jnp.minimum(1.0, clip_norm / (jnp.sqrt(square_sum) + 1e-06))
    rows, width = grad_ref.shape
    blocks = fs_ref.shape[1]
    size = width // blocks
    for i in range(blocks):
        at = slice(i * size, (i + 1) * size)
        clipped = grad_ref[:, at] * factor
        m_old = f_ref[:, at].astype(jnp.float32) * fs_ref[:, i : i + 1]
        v_old = s_ref[:, at].astype(jnp.float32) * ss_ref[:, i : i + 1]
        m_new = beta_first * m_old + (1.0 - beta_first) * clipped
        v_new = beta_second * v_old + (1.0 - beta_second) * clipped * clipped
        m_hat = m_new / (1.0 - beta_first**STEP)
        v_hat = v_new / (1.0 - beta_second**STEP)
        w_old = w_ref[:, at].astype(jnp.float32)
        wo[:, at] = (
            w_old - learn_rate * (m_hat / (jnp.sqrt(v_hat) + adam_epsilon) + weight_decay * w_old)
        ).astype(jnp.bfloat16)
        m_scale = jnp.max(jnp.abs(m_new), axis=1, keepdims=True) + tiny_scale
        v_scale = jnp.max(v_new, axis=1, keepdims=True) + tiny_scale
        mo[:, at] = (m_new / m_scale).astype(jnp.bfloat16)
        vo[:, at] = (v_new / v_scale).astype(jnp.bfloat16)
        mso[i : i + 1, :] = jnp.transpose(jnp.broadcast_to(m_scale, (rows, 128)))[:1]
        vso[i : i + 1, :] = jnp.transpose(jnp.broadcast_to(v_scale, (rows, 128)))[:1]


def adam_step(sums, grad, weight, first, first_scale, second, second_scale):
    rows, width = grad.shape
    codes = jax.ShapeDtypeStruct((rows, width), jnp.bfloat16)
    scale = jax.ShapeDtypeStruct(first_scale.shape[::-1], jnp.float32)
    w_new, m_code, m_scale, v_code, v_scale = pl.pallas_call(
        adam_kernel,
        out_shape=[codes, codes, scale, codes, scale],
        compiler_params=params(8),
        cost_estimate=SMALL,
        name="adam",
    )(sums, grad, weight, first, first_scale, second, second_scale)
    return w_new, m_code, m_scale.T, v_code, v_scale.T


def three_parts(a):
    high = a.astype(jnp.bfloat16)
    rest = a - high.astype(jnp.float32)
    mid = rest.astype(jnp.bfloat16)
    return [high, mid, (rest - mid.astype(jnp.float32)).astype(jnp.bfloat16)]


def pack_kernel(unit, counts_ref, facts_ref, w_ref, f_ref, s_ref, out_ref, pay_ref, wide, first, second):
    peers, _, rows, width = out_ref.shape
    per_row = unit // rows

    def by_rows(ref):
        for j in range(wide.shape[0]):
            wide[j] = ref[:, j * 128 : (j + 1) * 128].astype(jnp.float32)
        sides = [
            wide[j, pl.ds(i, peers * rows, stride=per_row), :] for i in range(per_row) for j in range(wide.shape[0])
        ]
        return jnp.concatenate(sides, axis=1).astype(jnp.bfloat16).reshape(peers, rows, width)

    pay_ref[:peers] = by_rows(w_ref)
    first[...] = by_rows(f_ref)
    second[...] = by_rows(s_ref)
    start, extra = jnp.int32(0), jnp.int32(0)
    for e in range(peers):
        units = counts_ref[0, e] // unit
        at = jnp.minimum(start, peers - 1)
        out_ref[e, 0] = first[at]
        out_ref[e, 1] = second[at]
        extra = jnp.where(units == 2, start + 1, extra)
        start = start + units
    pay_ref[peers] = first[extra]
    pay_ref[peers + 1] = second[extra]
    facts = facts_ref[...]
    meta = [p.astype(jnp.float32) for i in range(2) for p in three_parts(facts[i : i + 1])]
    meta = jnp.concatenate(meta + [facts[2:3], jnp.zeros((rows - 7, width), jnp.float32)])
    pay_ref[peers + 2] = meta.astype(jnp.bfloat16)


def pack_units(unit, counts, facts, w, f, s, shape):
    peers, rows, width = shape
    return pl.pallas_call(
        functools.partial(pack_kernel, unit),
        out_shape=[
            jax.ShapeDtypeStruct((peers, 2, rows, width), w.dtype),
            jax.ShapeDtypeStruct((peers + 3, rows, width), w.dtype),
        ],
        in_specs=[pl.BlockSpec(memory_space=pltpu.SMEM)] + [pl.BlockSpec(memory_space=pltpu.VMEM)] * 4,
        scratch_shapes=[pltpu.VMEM((w.shape[1] // 128, w.shape[0], 128), jnp.float32)] + [pltpu.VMEM(shape, w.dtype)] * 2,
        compiler_params=params(8),
        cost_estimate=SMALL,
        name="pack_units",
    )(counts, facts, w, f, s)


def place_of(grid, units, me, holder, slot):
    dy, dc, dz, dx = (p ^ q for p, q in zip(grid.split(holder), grid.split(me)))
    nx, ny, nz = grid.nx, grid.ny, grid.nz
    cut = (units + 1) // 2
    whole = nz * units
    straight = jnp.where(dy == 0, dx, nx - 1 + dy) * whole + dz * units
    across = (nx + ny - 1 + (dy - 1) * (nx - 1) + (dx - 1)) * whole
    on_axis = (dy == 0) | (dx == 0)
    first = jnp.where(on_axis, straight, across + dz * cut)
    second = jnp.where(on_axis, straight, across + nz * cut + dz * (units - cut) - cut)
    return dc * (nx * ny * whole) + slot + jnp.where(slot < cut, first, second)


def plan_kernel(grid, unit, units, me_ref, *refs):
    parts, (place_ref, holder_ref, ahead_ref, slot_ref, meta_ref, sems) = refs[:-6], refs[-6:]
    peers, lanes = place_ref.shape
    me = me_ref[0]
    copies = []
    for rel in range(peers):
        at, which = place_of_static(grid, units, rel, units - 1), 0
        while at >= parts[which].shape[0]:
            at -= parts[which].shape[0]
            which += 1
        copies.append(pltpu.make_async_copy(parts[which].at[at], meta_ref.at[me ^ rel], sems.at[rel]))
    for copy in copies:
        copy.start()
    for copy in copies:
        copy.wait()
    table = jnp.concatenate([meta_ref[d].astype(jnp.float32)[6:7, :lanes] for d in range(peers)]) * (1.0 / unit)
    row = lax.broadcasted_iota(jnp.int32, (lanes, lanes), 0)
    col = lax.broadcasted_iota(jnp.int32, (lanes, lanes), 1)
    starts = jnp.dot(table, (row < col).astype(jnp.float32), preferred_element_type=jnp.float32).astype(jnp.int32)
    ahead_of = (col < row).astype(jnp.float32)[:peers, :peers]
    offsets = jnp.dot(ahead_of, table, preferred_element_type=jnp.float32).astype(jnp.int32)
    table = table.astype(jnp.int32)
    unit_at = lax.broadcasted_iota(jnp.int32, (peers, lanes), 0)
    zero = jnp.zeros((peers, lanes), jnp.int32)
    place, holder, late, slots = zero, zero, zero, zero
    for d in range(peers):
        ahead = unit_at - offsets[d : d + 1]
        hit = (ahead >= 0) & (ahead < table[d : d + 1])
        slot = starts[d : d + 1] + ahead
        place = jnp.where(hit, place_of(grid, units, me, d, slot), place)
        holder = jnp.where(hit, d, holder)
        late = jnp.where(hit, ahead, late)
        slots = jnp.where(hit, slot, slots)
    place_ref[...] = place
    holder_ref[...] = holder
    ahead_ref[...] = late
    slot_ref[...] = slots


def place_of_static(grid, units, rel, slot):
    dy, dc, dz, dx = grid.split(rel)
    nx, ny, nz = grid.nx, grid.ny, grid.nz
    cut = (units + 1) // 2
    whole = nz * units
    at = dc * (nx * ny * whole) + slot
    if dy == 0 or dx == 0:
        return at + (dx if dy == 0 else nx - 1 + dy) * whole + dz * units
    at += (nx + ny - 1 + (dy - 1) * (nx - 1) + (dx - 1)) * whole
    return at + (dz * cut if slot < cut else nz * cut + dz * (units - cut) - cut)


def plan_units(grid, unit, me, parts):
    lanes = max(128, grid.size)
    rows, width = parts[0].shape[-2:]
    units = parts[0].shape[1]
    parts = [p.reshape(-1, rows, width) for p in parts]
    return pl.pallas_call(
        functools.partial(plan_kernel, grid, unit, units),
        out_shape=[jax.ShapeDtypeStruct((grid.size, lanes), jnp.int32)] * 4
        + [jax.ShapeDtypeStruct((grid.size, rows, width), parts[0].dtype)],
        in_specs=[pl.BlockSpec(memory_space=pltpu.SMEM)] + [pl.BlockSpec(memory_space=pl.ANY)] * len(parts),
        scratch_shapes=[pltpu.SemaphoreType.DMA((grid.size,))],
        compiler_params=params(8),
        cost_estimate=SMALL,
        name="plan_units",
    )(me, *parts)


def unpack_kernel(unit, me_ref, holder_ref, ahead_ref, slot_ref, meta_ref, got_ref, extra_ref, first_ref, second_ref, fs_ref, ss_ref, scales):
    peers, rows, width = first_ref.shape
    me = me_ref[0]
    for d in range(peers):
        meta = meta_ref[d].astype(jnp.float32)
        scales[0, pl.ds(d, 1), :] = meta[0:1] + meta[1:2] + meta[2:3]
        scales[1, pl.ds(d, 1), :] = meta[3:4] + meta[4:5] + meta[5:6]
    per_row = unit // rows
    lane = lax.broadcasted_iota(jnp.int32, (rows, width), 1)
    block = lax.broadcasted_iota(jnp.int32, (rows, width), 0) * per_row
    late = jnp.int32(0)
    for u in range(peers):
        p = holder_ref[u, me]
        first_ref[u] = got_ref[p, 0]
        second_ref[u] = got_ref[p, 1]
        late = jnp.where(ahead_ref[u, me] == 1, u, late)
        at = lane - (slot_ref[u, me] * unit + block)
        for i, out in enumerate((fs_ref, ss_ref)):
            line = jnp.broadcast_to(scales[i, pl.ds(p, 1), :], (rows, width))
            for h in range(per_row):
                value = jnp.sum(jnp.where(at == h, line, 0.0), axis=1, keepdims=True)
                out[pl.ds(u * rows, rows), h : h + 1] = value
    first_ref[late] = extra_ref[0]
    second_ref[late] = extra_ref[1]


def unpack_units(unit, me, plan, got, extra):
    peers, _, rows, width = got.shape
    units = jax.ShapeDtypeStruct((peers, rows, width), got.dtype)
    scale = jax.ShapeDtypeStruct((peers * rows, unit // rows), jnp.float32)
    smem, vmem = pl.BlockSpec(memory_space=pltpu.SMEM), pl.BlockSpec(memory_space=pltpu.VMEM)
    return pl.pallas_call(
        functools.partial(unpack_kernel, unit),
        out_shape=[units, units, scale, scale],
        in_specs=[smem] * 4 + [vmem] * 3,
        scratch_shapes=[pltpu.VMEM((2, peers, width), jnp.float32)],
        compiler_params=params(8),
        cost_estimate=SMALL,
        name="unpack_units",
    )(me, *plan[1:], got, extra)


def stack_kernel(*refs):
    for i, ref in enumerate(refs[:-1]):
        refs[-1][i] = ref[...]


def stack_parts(parts):
    return pl.pallas_call(
        stack_kernel,
        out_shape=jax.ShapeDtypeStruct((len(parts),) + parts[0].shape, parts[0].dtype),
        compiler_params=params(8),
        cost_estimate=SMALL,
        name="stack_parts",
    )(*parts)


def halves_kernel(count, *refs):
    sems = refs[-1]
    ins, outs = refs[: len(refs) // 2], refs[len(refs) // 2 : -1]
    copies = []
    for n, (ref, out) in enumerate(zip(ins, outs)):
        cut = out.shape[1]
        copies.append(pltpu.make_async_copy(ref.at[:, pl.ds(0 if n < count else ref.shape[1] - cut, cut)], out, sems.at[n]))
    for copy in copies:
        copy.start()
    for copy in copies:
        copy.wait()


def halves(firsts, seconds):
    ins = firsts + seconds
    nz, units, rows, width = ins[0].shape
    cuts = [(units + 1) // 2] * len(firsts) + [units // 2] * len(seconds)
    outs = pl.pallas_call(
        functools.partial(halves_kernel, len(firsts)),
        out_shape=[jax.ShapeDtypeStruct((nz, cut, rows, width), ins[0].dtype) for cut in cuts],
        in_specs=[pl.BlockSpec(memory_space=pl.ANY)] * len(ins),
        scratch_shapes=[pltpu.SemaphoreType.DMA((len(ins),))],
        compiler_params=params(8),
        cost_estimate=SMALL,
        name="halves",
    )(*ins)
    return outs[: len(firsts)], outs[len(firsts) :]


def product_kernel(count, group, grid, me_ref, place_ref, holder_ref, ahead_ref, cot_ref, *refs):
    parts, (out_ref, own_ref, extra_ref, held, tile, made, sems, out_sems) = refs[:count], refs[count:]
    copies, at = [], 0
    for i, ref in enumerate(parts):
        copies.append(pltpu.make_async_copy(ref, held.at[pl.ds(at, ref.shape[0])], sems.at[i]))
        at += ref.shape[0]
    for copy in copies:
        copy.start()
    for copy in copies:
        copy.wait()
    steps, _, columns = made.shape
    peers = place_ref.shape[0]

    def put(i):
        return pltpu.make_async_copy(
            made.at[i], out_ref.at[:, pl.ds(pl.multiple_of(i * columns, columns), columns)], out_sems.at[i]
        )

    def step(i, carry):
        for u in range(group):
            tile[u] = held[place_ref[u % peers, i * (group // peers) + u // peers]]
        weight = tile[...].reshape(group * tile.shape[1], tile.shape[2])
        made[i] = lax.dot_general(
            cot_ref[...], weight, (((1,), (1,)), ((), ())), preferred_element_type=jnp.float32
        ).astype(made.dtype)
        put(i).start()
        return carry

    lax.fori_loop(0, steps, step, 0, unroll=True)
    me = me_ref[0]
    late = jnp.int32(0)
    for u in range(peers):
        own_ref[u] = held[place_ref[u, me]]
        late = jnp.where(ahead_ref[u, me] == 1, holder_ref[u, me], late)
    extra = place_of(grid, peers + 3, me, late, peers)
    extra_ref[0] = held[extra]
    extra_ref[1] = held[extra + 1]

    def finish(i, carry):
        put(i).wait()
        return carry

    lax.fori_loop(0, steps, finish, 0)


def product(grid, me, plan, cot, parts):
    rows, width = parts[0].shape[-2:]
    parts = [p.reshape(-1, rows, width) for p in parts]
    peers = grid.size
    total = peers * peers
    group = GROUP
    tokens = cot.shape[0]
    smem, vmem, anywhere = (pl.BlockSpec(memory_space=m) for m in (pltpu.SMEM, pltpu.VMEM, pl.ANY))
    return pl.pallas_call(
        functools.partial(product_kernel, len(parts), group, grid),
        out_shape=[
            jax.ShapeDtypeStruct((tokens, total * rows), cot.dtype),
            jax.ShapeDtypeStruct((peers, rows, width), cot.dtype),
            jax.ShapeDtypeStruct((2, rows, width), cot.dtype),
        ],
        in_specs=[smem] * 4 + [vmem] + [anywhere] * len(parts),
        out_specs=[anywhere, vmem, vmem],
        scratch_shapes=[
            pltpu.VMEM((sum(p.shape[0] for p in parts), rows, width), cot.dtype),
            pltpu.VMEM((group, rows, width), cot.dtype),
            pltpu.VMEM((total // group, tokens, group * rows), cot.dtype),
            pltpu.SemaphoreType.DMA((len(parts),)),
            pltpu.SemaphoreType.DMA((total // group,)),
        ],
        compiler_params=params(28),
        cost_estimate=SMALL,
        name="product",
    )(me, *plan[:3], cot, *parts)


def after(a, *others):
    return lax.optimization_barrier((a, others))[0]


def spread_weight(grid, near, gates):
    near = stack_parts(after(near, gates[0]))
    along_x = {dx: grid.send(near, dx=dx) for dx in range(1, grid.nx)}
    along_y = {dy: grid.send(near, dy=dy) for dy in range(1, grid.ny)}
    parts = [near] + list(along_x.values()) + list(along_y.values())
    firsts, seconds = halves(*after((list(along_x.values()), list(along_y.values())), gates[1]))
    for dy in range(1, grid.ny):
        for dx in range(1, grid.nx):
            parts.append(grid.send(firsts[dx - 1], dy=dy))
            parts.append(grid.send(seconds[dy - 1], dx=dx))
    return parts + [grid.send(p, dc=1) for p in parts]


def send_state(grid, w, f, fs, s, ss, counts, key_width, gate):
    peers = grid.size
    slots, block = w.shape
    unit = slots // peers
    per_row = key_width // block
    unit_rows = unit // per_row
    shape = (peers, unit_rows, key_width)
    pad = lambda a: jnp.pad(a, (0, key_width - a.shape[0]))
    facts = jnp.stack([pad(fs), pad(ss), pad(counts[0].astype(jnp.float32))])
    packed, payload = pack_units(unit, counts, facts, *after((w, f, s), gate), shape)
    return packed, [payload] + [grid.send(payload, dz=dz) for dz in range(1, grid.nz)]


def apply_state(grid, me, cot, near, got, w, key_width, gates):
    peers = grid.size
    slots, block = w.shape
    unit = slots // peers
    per_row = key_width // block
    parts = spread_weight(grid, near, gates)
    where = me.reshape(1)
    plan = plan_units(grid, unit, where, parts)
    input_grad, own_units, extra = product(grid, where, plan, cot, parts)
    first, second, first_scale, second_scale = unpack_units(unit, where, plan, got, extra)
    two = lambda a: a.reshape(slots // per_row, key_width)
    return input_grad, two(own_units), two(first), first_scale, two(second), second_scale


def state_by_blocks(grid, me, cot, w, f, fs, s, ss, counts, key_width):
    peers = grid.size
    slots, block = w.shape
    per_row = key_width // block
    rows = slots // per_row
    gather = lambda a: lax.all_gather(a, AXES, axis=0, tiled=True)
    table = gather(counts)
    starts = jnp.cumsum(table, axis=1) - table
    offsets = jnp.cumsum(table, axis=0) - table
    j = jnp.arange(slots, dtype=jnp.int32)
    ahead = j[None, None, :] - offsets[:, :, None]
    hit = (ahead >= 0) & (ahead < table[:, :, None])
    holder = jnp.arange(peers, dtype=jnp.int32)[:, None, None]
    pick = jnp.sum(jnp.where(hit, holder * slots + starts[:, :, None] + ahead, 0), axis=0)
    weight = gather(w)[pick.reshape(-1)].reshape(-1, key_width)
    mine = lax.dynamic_index_in_dim(pick, me, 0, keepdims=False)
    own_weight = lax.dynamic_slice_in_dim(weight, me * rows, rows, 0)
    two = lambda a: gather(a)[mine].reshape(rows, key_width)
    scale = lambda a: gather(a)[mine].reshape(rows, per_row)
    input_grad = lax.dot_general(
        cot, weight, (((1,), (1,)), ((), ())), preferred_element_type=jnp.float32
    ).astype(jnp.bfloat16)
    return input_grad, own_weight, two(f), scale(fs), two(s), scale(ss)


def shards(
    hidden_states,
    key_cotangent,
    old_weight,
    old_first,
    old_first_scale,
    old_second,
    old_second_scale,
    send_counts,
):
    grid = Grid(lax.axis_size("cuts"), lax.axis_size("fsdp"))
    me = lax.axis_index(AXES).astype(jnp.int32)
    y, c, z, x = grid.split(me)
    slots, block = old_weight.shape
    key_width = key_cotangent.shape[1]
    rows = slots * block // key_width
    tokens = hidden_states.shape[0]
    peers = grid.size
    per_row = key_width // block
    unit = slots // peers
    by_units = unit % per_row == 0 and unit // per_row >= 8 and slots <= key_width and peers <= 128

    ny, nz, nx = grid.ny, grid.nz, grid.nx
    batches = [
        [(dy, dx) for dx in range(1, nx) for dy in reversed(range(ny))],
        [(dy, 0) for dy in reversed(range(ny))],
    ]

    where = me.reshape(1)
    pick = functools.partial(pick_columns, grid)
    picked = [pick(where, 1, batches[0], hidden_states, rows, key_cotangent)]
    picked.append(pick(after(where, picked[0]), 1, batches[1], hidden_states, rows))
    parts = [grid.send(p, dc=1) for p in picked]
    owns = [pick(after(where, picked[1]), 0, batches[0], hidden_states, rows)]
    owns.append(pick(after(where, owns[0]), 0, batches[1], hidden_states, rows))

    def job(dy, dx, side):
        which = 0 if dx else 1
        return which, batches[which].index((dy, dx)) * nz, side

    def terms(coded, jobs, *gate):
        count = 1 + max(j[0] for j in jobs)
        return partial_sums(coded, jobs, nz, after(key_cotangent, gate), owns[:count], parts[:count])

    sent_a, sent_b, made = {}, {}, ()
    for dx in range(1, nx):
        made = terms(True, [job(dy, dx, 0) for dy in range(ny)], made)
        sent_a[dx] = grid.send(made, dx=dx)
    first_made = made
    for dy in range(1, ny):
        made = terms(True, [job(dy, dx, 1) for dx in range(nx)], made)
        sent_b[dy] = grid.send(made, dy=dy)
    keep = terms(False, [job(dy, 0, 0) for dy in range(ny)] + [job(0, dx, 1) for dx in range(nx)], made)
    if by_units:
        packed, near = send_state(
            grid, old_weight, old_first, old_first_scale, old_second, old_second_scale, send_counts, key_width, first_made
        )
    late_a, late_b, coded_late = [], [], []
    kept = after(keep, near) if by_units else keep
    for dy in range(1, ny):
        coded_late.append(relay(nz, kept, dy * nz, list(sent_a.values()), dy * nz))
        late_a.append(grid.send(coded_late[-1], dy=dy))
    for dx in range(1, nx):
        coded_late.append(relay(nz, kept, (ny + dx) * nz, list(sent_b.values()), dx * nz))
        late_b.append(grid.send(coded_late[-1], dx=dx))
    if by_units:
        got = lax.all_to_all(after(packed, coded_late), AXES, 0, 0, tiled=True)
        keep = after(keep, got)
    mine = corner(nz, keep, (0, ny * nz), list(sent_a.values()) + late_a, list(sent_b.values()) + late_b)
    over_z = [grid.send(mine[dz], dz=dz) for dz in range(1, grid.nz)]
    gradient, square = total_gradient(tokens * peers, mine[0], over_z)
    sums = lax.all_to_all(
        jnp.broadcast_to(square[None, :1], (peers, 1, 128)), AXES, 0, 0, tiled=True
    ).reshape(peers, 128)

    if by_units:
        state = apply_state(grid, me, key_cotangent, near, got, old_weight, key_width, (mine, mine))
    else:
        state = state_by_blocks(
            grid, me, key_cotangent, old_weight, old_first, old_first_scale, old_second, old_second_scale, send_counts, key_width
        )
    input_grad, own_weight, first, first_scale, second, second_scale = state
    w_new, m_code, m_scale, v_code, v_scale = adam_step(
        sums, gradient, own_weight, first, first_scale, second, second_scale
    )
    return input_grad, w_new, m_code, m_scale, v_code, v_scale


def solution(mesh):
    placed = (
        P(("cuts", "fsdp"), None),
        P(("cuts", "fsdp"), None),
        P(("cuts", "fsdp"), None),
        P(("cuts", "fsdp"), None),
        P(("cuts", "fsdp")),
        P(("cuts", "fsdp"), None),
        P(("cuts", "fsdp")),
        P(("cuts", "fsdp"), None),
    )
    return jax.shard_map(
        shards,
        mesh=mesh,
        in_specs=placed,
        out_specs=(
            P(("cuts", "fsdp"), None),
            P(("cuts", "fsdp"), None),
            P(("cuts", "fsdp"), None),
            P(("cuts", "fsdp"), None),
            P(("cuts", "fsdp"), None),
            P(("cuts", "fsdp"), None),
        ),
        check_vma=False,
    )
```

```python
import functools

import jax
import jax.numpy as jnp
from jax import lax
from jax.experimental import pallas as pl
from jax.experimental.pallas import tpu as pltpu
from jax.sharding import PartitionSpec as P

STEP = 2000


beta_first = 0.9
beta_second = 0.95
adam_epsilon = 1e-05
learn_rate = 0.001
weight_decay = 0.1
clip_norm = 1.0
tiny_scale = 1e-30

AXES = ("cuts", "fsdp")
TAIL = 16
GROUP = 128


class Grid:
    def __init__(self, cuts, fsdp):
        self.cuts, self.fsdp = cuts, fsdp
        self.ny = cuts // 2
        self.nz = 4
        self.nx = fsdp // 4
        self.size = cuts * fsdp

    def split(self, i):
        x = i % self.nx
        z = (i // self.nx) % self.nz
        c = (i // self.fsdp) % 2
        y = i // (2 * self.fsdp)
        return y, c, z, x

    def join(self, y, c, z, x):
        return ((y * 2 + c) * self.nz + z) * self.nx + x

    def send(self, a, dy=0, dc=0, dz=0, dx=0):
        pairs = []
        for i in range(self.size):
            y, c, z, x = self.split(i)
            pairs.append((i, self.join(y ^ dy, c ^ dc, z ^ dz, x ^ dx)))
        return lax.ppermute(a, AXES, pairs)


SMALL = pl.CostEstimate(flops=1, bytes_accessed=1, transcendentals=0)


def params(mib):
    return pltpu.CompilerParams(vmem_limit_bytes=mib * 1024 * 1024)


def encode(g):
    top = jnp.max(jnp.abs(g), axis=0, keepdims=True)
    k = jnp.ceil(jnp.log2(jnp.maximum(top, 1e-30) / 32700.0) * 256.0)
    q = jnp.round(g * jnp.exp2(k * (-1.0 / 256.0)))
    return q.astype(jnp.int32).astype(jnp.int16), k


def tail_rows(ks, columns):
    filled = list(ks)
    if len(ks) < TAIL:
        filled.append(jnp.zeros((TAIL - len(ks), columns), jnp.float32))
    filled = jnp.concatenate(filled)
    return filled.astype(jnp.int32).astype(jnp.int16)


def scales_of(ref, row):
    k = ref[pl.ds(row, TAIL), :].astype(jnp.int32).astype(jnp.float32)
    return jnp.exp2(k * (1.0 / 256.0))


def decode(ref, row, rows, scale):
    return ref[pl.ds(row, rows), :].astype(jnp.int32).astype(jnp.float32) * scale


def pick_kernel(grid, core, groups, me_ref, hidden_ref, *refs):
    out, held, sems, out_sems = refs[-4:]
    rows = out.shape[2]
    y, c, z, x = grid.split(me_ref[0])
    owners = [grid.join(y ^ dy, c ^ core, z ^ dz, x ^ dx) for dy, dx in groups for dz in range(grid.nz)]
    copies, puts = [], []
    for i, owner in enumerate(owners):
        at = pl.multiple_of(owner * rows, rows)
        copies.append(pltpu.make_async_copy(hidden_ref.at[:, pl.ds(at, rows)], held.at[i], sems.at[i]))
    for i in range(len(owners), out.shape[0]):
        at = (i - len(owners)) * rows
        copies.append(pltpu.make_async_copy(refs[0].at[:, pl.ds(at, rows)], held.at[i], sems.at[i]))
    for copy in copies:
        copy.start()
    for i, copy in enumerate(copies):
        copy.wait()
        puts.append(pltpu.make_async_copy(held.at[i], out.at[i], out_sems.at[i]))
        puts[-1].start()
    for put in puts:
        put.wait()


def pick_columns(grid, me, core, groups, hidden, rows, *more):
    tokens = hidden.shape[0]
    if rows % 128:
        cut = lambda a, at: lax.dynamic_slice_in_dim(a, at * rows, rows, 1)
        y, c, z, x = grid.split(me[0])
        owners = [grid.join(y ^ dy, c ^ core, z ^ dz, x ^ dx) for dy, dx in groups for dz in range(grid.nz)]
        return jnp.stack([cut(hidden, o) for o in owners] + [cut(a, i) for a in more for i in range(a.shape[1] // rows)])
    blocks = len(groups) * grid.nz + sum(a.shape[1] // rows for a in more)
    return pl.pallas_call(
        functools.partial(pick_kernel, grid, core, groups),
        out_shape=jax.ShapeDtypeStruct((blocks, tokens, rows), hidden.dtype),
        in_specs=[pl.BlockSpec(memory_space=pltpu.SMEM)] + [pl.BlockSpec(memory_space=pl.ANY)] * (1 + len(more)),
        out_specs=pl.BlockSpec(memory_space=pl.ANY),
        scratch_shapes=[pltpu.VMEM((blocks, tokens, rows), hidden.dtype)] + [pltpu.SemaphoreType.DMA((blocks,))] * 2,
        compiler_params=params(56),
        cost_estimate=SMALL,
        name="pick_columns",
    )(me, hidden, *more)


def partial_kernel(coded, jobs, nz, count, c_ref, *refs):
    owns, parts, out = refs[:count], refs[count:-1], refs[-1]
    tokens, width = c_ref.shape
    half, rows = width // 2, owns[0].shape[2]
    last = parts[0].shape[0] - width // rows
    across = (((0,), (0,)), ((), ()))
    ks = []
    for n, (which, at, side) in enumerate(jobs):
        mine = c_ref[:, side * half : (side + 1) * half]
        blocks = range(last + side * half // rows, last + (side + 1) * half // rows)
        other = [parts[0][b] for b in blocks]
        other = other[0] if len(other) == 1 else jnp.concatenate(other, axis=1)
        for i in range(nz):
            g = lax.dot_general(mine, owns[which][at + i], across, preferred_element_type=jnp.float32)
            g = g + lax.dot_general(other, parts[which][at + i], across, preferred_element_type=jnp.float32)
            if coded:
                q, k = encode(g)
                out[pl.ds((n * nz + i) * half, half), :] = q
                ks.append(k)
            else:
                out[n * nz + i] = g
    if coded:
        out[pl.ds(len(jobs) * nz * half, TAIL), :] = tail_rows(ks, rows)


def partial_sums(coded, jobs, nz, cot, owns, parts):
    _, width = cot.shape
    half, rows = width // 2, owns[0].shape[2]
    blocks = len(jobs) * nz
    return pl.pallas_call(
        functools.partial(partial_kernel, coded, jobs, nz, len(owns)),
        out_shape=jax.ShapeDtypeStruct((blocks * half + TAIL, rows), jnp.int16)
        if coded
        else jax.ShapeDtypeStruct((blocks, half, rows), jnp.float32),
        compiler_params=params(24),
        cost_estimate=SMALL,
        name="partial_sums",
    )(cot, *owns, *parts)


def relay_kernel(keep_at, coded_at, nz, keep_ref, *refs):
    coded, out = refs[:-1], refs[-1]
    _, half, rows = keep_ref.shape
    tables = [scales_of(ref, ref.shape[0] - TAIL) for ref in coded]
    ks = []
    for i in range(nz):
        total = keep_ref[keep_at + i]
        for ref, s in zip(coded, tables):
            at = coded_at + i
            total = total + decode(ref, at * half, half, s[at : at + 1])
        q, k = encode(total)
        out[pl.ds(i * half, half), :] = q
        ks.append(k)
    out[pl.ds(nz * half, TAIL), :] = tail_rows(ks, rows)


def relay(nz, keep, keep_at, coded, coded_at):
    _, half, rows = keep.shape
    return pl.pallas_call(
        functools.partial(relay_kernel, keep_at, coded_at, nz),
        out_shape=jax.ShapeDtypeStruct((nz * half + TAIL, rows), jnp.int16),
        compiler_params=params(14),
        cost_estimate=SMALL,
        name="relay",
    )(keep, *coded)


def gather_kernel(count, nz, keep_ref, *refs):
    number = len(refs) - 3
    coded, (out, held, sems) = refs[:number], refs[number:]
    _, half, rows = keep_ref.shape
    copies = []
    for j, ref in enumerate(coded):
        for i, (at, size, to) in enumerate(((0, nz * half, 0), (ref.shape[0] - TAIL, TAIL, nz * half))):
            copies.append(pltpu.make_async_copy(ref.at[pl.ds(at, size)], held.at[j, pl.ds(to, size)], sems.at[2 * j + i]))
    for copy in copies:
        copy.start()
    for copy in copies:
        copy.wait()
    for n in range(2):
        mine = range(count) if n == 0 else range(count, number)
        tables = {j: scales_of(held.at[j], nz * half) for j in mine}
        for i in range(nz):
            total = keep_ref[n * nz + i]
            for j in mine:
                total = total + decode(held.at[j], i * half, half, tables[j][i : i + 1])
            out[n * nz + i] = total


def gather_terms(nz, keep, coded_a, coded_b):
    _, half, rows = keep.shape
    coded = list(coded_a) + list(coded_b)
    return pl.pallas_call(
        functools.partial(gather_kernel, len(coded_a), nz),
        out_shape=jax.ShapeDtypeStruct(keep.shape, keep.dtype),
        in_specs=[pl.BlockSpec(memory_space=pltpu.VMEM)] + [pl.BlockSpec(memory_space=pl.ANY)] * len(coded),
        scratch_shapes=[pltpu.VMEM((len(coded), nz * half + TAIL, rows), jnp.int16), pltpu.SemaphoreType.DMA((2 * len(coded),))],
        compiler_params=params(14),
        cost_estimate=SMALL,
        name="gather_terms",
    )(keep, *coded)


def corner_kernel(counts, keep_at, nz, keep_ref, *refs):
    coded, outs = refs[: sum(counts)], refs[sum(counts) :]
    _, half, rows = keep_ref.shape
    tables = [scales_of(ref, ref.shape[0] - TAIL) for ref in coded]
    for dz in range(nz):
        ks = []
        for i in range(2):
            total = keep_ref[keep_at[i] + dz]
            for j in range(i * counts[0], i * counts[0] + counts[i]):
                total = total + decode(coded[j], dz * half, half, tables[j][dz : dz + 1])
            if dz == 0:
                outs[0][pl.ds(i * half, half), :] = total
            else:
                q, k = encode(total)
                outs[dz][pl.ds(i * half, half), :] = q
                ks.append(k)
        if dz:
            outs[dz][pl.ds(2 * half, TAIL), :] = tail_rows(ks, rows)


def corner(nz, keep, keep_at, coded_a, coded_b):
    _, half, rows = keep.shape
    shapes = [jax.ShapeDtypeStruct((2 * half, rows), jnp.float32)]
    shapes += [jax.ShapeDtypeStruct((2 * half + TAIL, rows), jnp.int16)] * (nz - 1)
    return pl.pallas_call(
        functools.partial(corner_kernel, (len(coded_a), len(coded_b)), keep_at, nz),
        out_shape=shapes,
        compiler_params=params(18),
        cost_estimate=SMALL,
        name="corner",
    )(keep, *coded_a, *coded_b)


def total_kernel(tokens, keep_ref, *refs):
    grad_ref, sum_ref = refs[-2:]
    width, rows = keep_ref.shape
    half = width // 2
    scales = [scales_of(ref, width) for ref in refs[:-2]]
    square = jnp.zeros((1, rows), jnp.float32)
    for i in range(2):
        total = keep_ref[pl.ds(i * half, half), :]
        for ref, s in zip(refs[:-2], scales):
            total = total + decode(ref, i * half, half, s[i : i + 1])
        total = total / tokens
        grad_ref[:, i * half : (i + 1) * half] = jnp.transpose(total)
        square = square + jnp.sum(total * total, axis=0, keepdims=True)
    sum_ref[...] = jnp.broadcast_to(jnp.sum(square, axis=1, keepdims=True), sum_ref.shape)


def total_gradient(tokens, keep, coded):
    width, rows = keep.shape
    return pl.pallas_call(
        functools.partial(total_kernel, tokens),
        out_shape=[jax.ShapeDtypeStruct((rows, width), jnp.float32), jax.ShapeDtypeStruct((8, 128), jnp.float32)],
        compiler_params=params(6),
        cost_estimate=SMALL,
        name="total_gradient",
    )(keep, *coded)


def adam_rows(sums_ref, grad_ref, w, f, fs_ref, s, ss_ref, wo, mo, mso, vo, vso):
    sums = sums_ref[...]
    square_sum = jnp.sum(sums, axis=0, keepdims=True)[:, :1]
    factor = jnp.minimum(1.0, clip_norm / (jnp.sqrt(square_sum) + 1e-06))
    rows, width = grad_ref.shape
    blocks = fs_ref.shape[1]
    size = width // blocks
    for i in range(blocks):
        at = slice(i * size, (i + 1) * size)
        clipped = grad_ref[:, at] * factor
        m_old = f[:, at].astype(jnp.float32) * fs_ref[:, i : i + 1]
        v_old = s[:, at].astype(jnp.float32) * ss_ref[:, i : i + 1]
        m_new = beta_first * m_old + (1.0 - beta_first) * clipped
        v_new = beta_second * v_old + (1.0 - beta_second) * clipped * clipped
        m_hat = m_new / (1.0 - beta_first**STEP)
        v_hat = v_new / (1.0 - beta_second**STEP)
        w_old = w[:, at].astype(jnp.float32)
        wo[:, at] = (
            w_old - learn_rate * (m_hat / (jnp.sqrt(v_hat) + adam_epsilon) + weight_decay * w_old)
        ).astype(jnp.bfloat16)
        m_scale = jnp.max(jnp.abs(m_new), axis=1, keepdims=True) + tiny_scale
        v_scale = jnp.max(v_new, axis=1, keepdims=True) + tiny_scale
        mo[:, at] = (m_new / m_scale).astype(jnp.bfloat16)
        vo[:, at] = (v_new / v_scale).astype(jnp.bfloat16)
        mso[i : i + 1, :] = jnp.transpose(jnp.broadcast_to(m_scale, (rows, 128)))[:1]
        vso[i : i + 1, :] = jnp.transpose(jnp.broadcast_to(v_scale, (rows, 128)))[:1]


def adam_kernel(sums_ref, grad_ref, w_ref, f_ref, fs_ref, s_ref, ss_ref, *outs):
    adam_rows(sums_ref, grad_ref, w_ref[...], f_ref[...], fs_ref, s_ref[...], ss_ref, *outs)


def adam_outputs(rows, width, blocks):
    codes = jax.ShapeDtypeStruct((rows, width), jnp.bfloat16)
    scale = jax.ShapeDtypeStruct((blocks, rows), jnp.float32)
    return [codes, codes, scale, codes, scale]


def adam_step(sums, grad, weight, first, first_scale, second, second_scale):
    w_new, m_code, m_scale, v_code, v_scale = pl.pallas_call(
        adam_kernel,
        out_shape=adam_outputs(*grad.shape, first_scale.shape[1]),
        compiler_params=params(8),
        cost_estimate=SMALL,
        name="adam",
    )(sums, grad, weight, first, first_scale, second, second_scale)
    return w_new, m_code, m_scale.T, v_code, v_scale.T


def three_parts(a):
    high = a.astype(jnp.bfloat16)
    rest = a - high.astype(jnp.float32)
    mid = rest.astype(jnp.bfloat16)
    return [high, mid, (rest - mid.astype(jnp.float32)).astype(jnp.bfloat16)]


def pack_kernel(unit, counts_ref, facts_ref, w_ref, f_ref, s_ref, out_ref, pay_ref, wide, first, second):
    peers, _, rows, width = out_ref.shape
    per_row = unit // rows

    def by_rows(ref):
        for j in range(wide.shape[0]):
            wide[j] = ref[:, j * 128 : (j + 1) * 128].astype(jnp.float32)
        sides = [
            wide[j, pl.ds(i, peers * rows, stride=per_row), :] for i in range(per_row) for j in range(wide.shape[0])
        ]
        return jnp.concatenate(sides, axis=1).astype(jnp.bfloat16).reshape(peers, rows, width)

    pay_ref[:peers] = by_rows(w_ref)
    first[...] = by_rows(f_ref)
    second[...] = by_rows(s_ref)
    start, extra = jnp.int32(0), jnp.int32(0)
    for e in range(peers):
        units = counts_ref[0, e] // unit
        at = jnp.minimum(start, peers - 1)
        out_ref[e, 0] = first[at]
        out_ref[e, 1] = second[at]
        extra = jnp.where(units == 2, start + 1, extra)
        start = start + units
    pay_ref[peers] = first[extra]
    pay_ref[peers + 1] = second[extra]
    facts = facts_ref[...]
    meta = [p.astype(jnp.float32) for i in range(2) for p in three_parts(facts[i : i + 1])]
    meta = jnp.concatenate(meta + [facts[2:3], jnp.zeros((rows - 7, width), jnp.float32)])
    pay_ref[peers + 2] = meta.astype(jnp.bfloat16)


def pack_units(unit, counts, facts, w, f, s, shape):
    peers, rows, width = shape
    return pl.pallas_call(
        functools.partial(pack_kernel, unit),
        out_shape=[
            jax.ShapeDtypeStruct((peers, 2, rows, width), w.dtype),
            jax.ShapeDtypeStruct((peers + 3, rows, width), w.dtype),
        ],
        in_specs=[pl.BlockSpec(memory_space=pltpu.SMEM)] + [pl.BlockSpec(memory_space=pltpu.VMEM)] * 4,
        scratch_shapes=[pltpu.VMEM((w.shape[1] // 128, w.shape[0], 128), jnp.float32)] + [pltpu.VMEM(shape, w.dtype)] * 2,
        compiler_params=params(8),
        cost_estimate=SMALL,
        name="pack_units",
    )(counts, facts, w, f, s)


def place_of(grid, units, me, holder, slot):
    dy, dc, dz, dx = (p ^ q for p, q in zip(grid.split(holder), grid.split(me)))
    nx, ny, nz = grid.nx, grid.ny, grid.nz
    cut = (units + 1) // 2
    whole = nz * units
    straight = jnp.where(dy == 0, dx, nx - 1 + dy) * whole + dz * units
    across = (nx + ny - 1 + (dy - 1) * (nx - 1) + (dx - 1)) * whole
    on_axis = (dy == 0) | (dx == 0)
    first = jnp.where(on_axis, straight, across + dz * cut)
    second = jnp.where(on_axis, straight, across + nz * cut + dz * (units - cut) - cut)
    return dc * (nx * ny * whole) + slot + jnp.where(slot < cut, first, second)


def plan_kernel(grid, unit, units, me_ref, *refs):
    parts, (plan_ref, meta_ref, sems) = refs[:-3], refs[-3:]
    peers, lanes = meta_ref.shape[0], plan_ref.shape[1]
    me = me_ref[0]
    copies = []
    for rel in range(peers):
        at, which = place_of_static(grid, units, rel, units - 1), 0
        while at >= parts[which].shape[0]:
            at -= parts[which].shape[0]
            which += 1
        copies.append(pltpu.make_async_copy(parts[which].at[at], meta_ref.at[me ^ rel], sems.at[rel]))
    for copy in copies:
        copy.start()
    for copy in copies:
        copy.wait()
    table = jnp.concatenate([meta_ref[d].astype(jnp.float32)[6:7, :lanes] for d in range(peers)]) * (1.0 / unit)
    row = lax.broadcasted_iota(jnp.int32, (lanes, lanes), 0)
    col = lax.broadcasted_iota(jnp.int32, (lanes, lanes), 1)
    starts = jnp.dot(table, (row < col).astype(jnp.float32), preferred_element_type=jnp.float32).astype(jnp.int32)
    ahead_of = (col < row).astype(jnp.float32)[:peers, :peers]
    offsets = jnp.dot(ahead_of, table, preferred_element_type=jnp.float32).astype(jnp.int32)
    table = table.astype(jnp.int32)
    unit_at = lax.broadcasted_iota(jnp.int32, (peers, lanes), 0)
    zero = jnp.zeros((peers, lanes), jnp.int32)
    place, holder, late, slots = zero, zero, zero, zero
    for d in range(peers):
        ahead = unit_at - offsets[d : d + 1]
        hit = (ahead >= 0) & (ahead < table[d : d + 1])
        slot = starts[d : d + 1] + ahead
        place = jnp.where(hit, place_of(grid, units, me, d, slot), place)
        holder = jnp.where(hit, d, holder)
        late = jnp.where(hit, ahead, late)
        slots = jnp.where(hit, slot, slots)
    for i, a in enumerate((place, holder, late, slots)):
        plan_ref[pl.ds(i * peers, peers), :] = a


def place_of_static(grid, units, rel, slot):
    dy, dc, dz, dx = grid.split(rel)
    nx, ny, nz = grid.nx, grid.ny, grid.nz
    cut = (units + 1) // 2
    whole = nz * units
    at = dc * (nx * ny * whole) + slot
    if dy == 0 or dx == 0:
        return at + (dx if dy == 0 else nx - 1 + dy) * whole + dz * units
    at += (nx + ny - 1 + (dy - 1) * (nx - 1) + (dx - 1)) * whole
    return at + (dz * cut if slot < cut else nz * cut + dz * (units - cut) - cut)


def plan_units(grid, unit, me, parts):
    lanes = max(128, grid.size)
    rows, width = parts[0].shape[-2:]
    units = parts[0].shape[1]
    parts = [p.reshape(-1, rows, width) for p in parts]
    return pl.pallas_call(
        functools.partial(plan_kernel, grid, unit, units),
        out_shape=[
            jax.ShapeDtypeStruct((4 * grid.size, lanes), jnp.int32),
            jax.ShapeDtypeStruct((grid.size, rows, width), parts[0].dtype),
        ],
        in_specs=[pl.BlockSpec(memory_space=pltpu.SMEM)] + [pl.BlockSpec(memory_space=pl.ANY)] * len(parts),
        scratch_shapes=[pltpu.SemaphoreType.DMA((grid.size,))],
        compiler_params=params(8),
        cost_estimate=SMALL,
        name="plan_units",
    )(me, *parts)


def finish_kernel(unit, me_ref, sums_ref, *refs):
    ins, outs, (plan, grad_ref, own_ref, extra_ref, meta, got, first, second, fs, ss, scales, sems) = refs[:6], refs[6:11], refs[11:]
    held = (plan, grad_ref, own_ref, extra_ref, meta, got)
    copies = [pltpu.make_async_copy(a, b, sems.at[i]) for i, (a, b) in enumerate(zip(ins, held))]
    for copy in copies:
        copy.start()
    for copy in copies:
        copy.wait()
    peers, rows, width = first.shape
    me = me_ref[0]
    for d in range(peers):
        facts = meta[d].astype(jnp.float32)
        scales[0, pl.ds(d, 1), :] = facts[0:1] + facts[1:2] + facts[2:3]
        scales[1, pl.ds(d, 1), :] = facts[3:4] + facts[4:5] + facts[5:6]
    per_row = unit // rows
    lane = lax.broadcasted_iota(jnp.int32, (rows, width), 1)
    block = lax.broadcasted_iota(jnp.int32, (rows, width), 0) * per_row
    late = jnp.int32(0)
    for u in range(peers):
        p = plan[peers + u, me]
        first[u] = got[p, 0]
        second[u] = got[p, 1]
        late = jnp.where(plan[2 * peers + u, me] == 1, u, late)
        at = lane - (plan[3 * peers + u, me] * unit + block)
        for i, out in enumerate((fs, ss)):
            line = jnp.broadcast_to(scales[i, pl.ds(p, 1), :], (rows, width))
            for h in range(per_row):
                value = jnp.sum(jnp.where(at == h, line, 0.0), axis=1, keepdims=True)
                out[pl.ds(u * rows, rows), h : h + 1] = value
    first[late] = extra_ref[0]
    second[late] = extra_ref[1]
    two = lambda ref: ref[...].reshape(peers * rows, width)
    adam_rows(sums_ref, grad_ref, two(own_ref), two(first), fs, two(second), ss, *outs)


def finish(unit, me, plan, sums, grad, own, extra, got):
    peers, rows, width = own.shape
    blocks = unit // rows
    smem, vmem, anywhere = (pl.BlockSpec(memory_space=m) for m in (pltpu.SMEM, pltpu.VMEM, pl.ANY))
    units, scale = pltpu.VMEM(own.shape, own.dtype), pltpu.VMEM((peers * rows, blocks), jnp.float32)
    w_new, m_code, m_scale, v_code, v_scale = pl.pallas_call(
        functools.partial(finish_kernel, unit),
        out_shape=adam_outputs(peers * rows, width, blocks),
        in_specs=[smem, vmem] + [anywhere] * 6,
        scratch_shapes=[pltpu.SMEM(plan[0].shape, jnp.int32)]
        + [pltpu.VMEM(a.shape, a.dtype) for a in (grad, own, extra, plan[1], got)]
        + [units, units, scale, scale, pltpu.VMEM((2, peers, width), jnp.float32), pltpu.SemaphoreType.DMA((6,))],
        compiler_params=params(56),
        cost_estimate=SMALL,
        name="finish",
    )(me, sums, plan[0], grad, own, extra, plan[1], got)
    return w_new, m_code, m_scale.T, v_code, v_scale.T


def stack_kernel(*refs):
    out, sems = refs[-2:]
    copies = [pltpu.make_async_copy(ref, out.at[i], sems.at[i]) for i, ref in enumerate(refs[:-2])]
    for copy in copies:
        copy.start()
    for copy in copies:
        copy.wait()


def stack_parts(parts):
    return pl.pallas_call(
        stack_kernel,
        out_shape=jax.ShapeDtypeStruct((len(parts),) + parts[0].shape, parts[0].dtype),
        in_specs=[pl.BlockSpec(memory_space=pl.ANY)] * len(parts),
        scratch_shapes=[pltpu.SemaphoreType.DMA((len(parts),))],
        compiler_params=params(56),
        cost_estimate=SMALL,
        name="stack_parts",
    )(*parts)


def halves_kernel(count, *refs):
    sems = refs[-1]
    ins, outs = refs[: len(refs) // 2], refs[len(refs) // 2 : -1]
    copies = []
    for n, (ref, out) in enumerate(zip(ins, outs)):
        cut = out.shape[1]
        copies.append(pltpu.make_async_copy(ref.at[:, pl.ds(0 if n < count else ref.shape[1] - cut, cut)], out, sems.at[n]))
    for copy in copies:
        copy.start()
    for copy in copies:
        copy.wait()


def halves(firsts, seconds):
    ins = firsts + seconds
    nz, units, rows, width = ins[0].shape
    cuts = [(units + 1) // 2] * len(firsts) + [units // 2] * len(seconds)
    outs = pl.pallas_call(
        functools.partial(halves_kernel, len(firsts)),
        out_shape=[jax.ShapeDtypeStruct((nz, cut, rows, width), ins[0].dtype) for cut in cuts],
        in_specs=[pl.BlockSpec(memory_space=pl.ANY)] * len(ins),
        scratch_shapes=[pltpu.SemaphoreType.DMA((len(ins),))],
        compiler_params=params(8),
        cost_estimate=SMALL,
        name="halves",
    )(*ins)
    return outs[: len(firsts)], outs[len(firsts) :]


def product_kernel(count, group, grid, me_ref, plan_ref, cot_ref, *refs):
    parts, (out_ref, own_ref, extra_ref, plan, held, tile, made, sems, out_sems) = refs[:count], refs[count:]
    copies, at = [pltpu.make_async_copy(plan_ref, plan, sems.at[count])], 0
    for i, ref in enumerate(parts):
        copies.append(pltpu.make_async_copy(ref, held.at[pl.ds(at, ref.shape[0])], sems.at[i]))
        at += ref.shape[0]
    for copy in copies:
        copy.start()
    for copy in copies:
        copy.wait()
    steps, _, columns = made.shape
    peers = own_ref.shape[0]

    def put(i):
        return pltpu.make_async_copy(
            made.at[i], out_ref.at[:, pl.ds(pl.multiple_of(i * columns, columns), columns)], out_sems.at[i]
        )

    def step(i, carry):
        for u in range(group):
            tile[u] = held[plan[u % peers, i * (group // peers) + u // peers]]
        weight = tile[...].reshape(group * tile.shape[1], tile.shape[2])
        made[i] = lax.dot_general(
            cot_ref[...], weight, (((1,), (1,)), ((), ())), preferred_element_type=jnp.float32
        ).astype(made.dtype)
        put(i).start()
        return carry

    lax.fori_loop(0, steps, step, 0, unroll=True)
    me = me_ref[0]
    late = jnp.int32(0)
    for u in range(peers):
        own_ref[u] = held[plan[u, me]]
        late = jnp.where(plan[2 * peers + u, me] == 1, plan[peers + u, me], late)
    extra = place_of(grid, peers + 3, me, late, peers)
    extra_ref[0] = held[extra]
    extra_ref[1] = held[extra + 1]

    def finish(i, carry):
        put(i).wait()
        return carry

    lax.fori_loop(0, steps, finish, 0)


def product(grid, me, plan, cot, parts):
    rows, width = parts[0].shape[-2:]
    parts = [p.reshape(-1, rows, width) for p in parts]
    peers = grid.size
    total = peers * peers
    group = GROUP
    tokens = cot.shape[0]
    smem, vmem, anywhere = (pl.BlockSpec(memory_space=m) for m in (pltpu.SMEM, pltpu.VMEM, pl.ANY))
    return pl.pallas_call(
        functools.partial(product_kernel, len(parts), group, grid),
        out_shape=[
            jax.ShapeDtypeStruct((tokens, total * rows), cot.dtype),
            jax.ShapeDtypeStruct((peers, rows, width), cot.dtype),
            jax.ShapeDtypeStruct((2, rows, width), cot.dtype),
        ],
        in_specs=[smem, anywhere, vmem] + [anywhere] * len(parts),
        out_specs=[anywhere, vmem, vmem],
        scratch_shapes=[
            pltpu.SMEM(plan[0].shape, jnp.int32),
            pltpu.VMEM((sum(p.shape[0] for p in parts), rows, width), cot.dtype),
            pltpu.VMEM((group, rows, width), cot.dtype),
            pltpu.VMEM((total // group, tokens, group * rows), cot.dtype),
            pltpu.SemaphoreType.DMA((len(parts) + 1,)),
            pltpu.SemaphoreType.DMA((total // group,)),
        ],
        compiler_params=params(28),
        cost_estimate=SMALL,
        name="product",
    )(me, plan[0], cot, *parts)


def after(a, *others):
    return lax.optimization_barrier((a, others))[0]


def spread_weight(grid, near, gates):
    near = after(stack_parts(after(near, gates[0])), gates[1])
    along_x = {dx: grid.send(near, dx=dx) for dx in range(1, grid.nx)}
    along_y = {dy: grid.send(near, dy=dy) for dy in range(1, grid.ny)}
    parts = [near] + list(along_x.values()) + list(along_y.values())
    firsts, seconds = halves(*after((list(along_x.values()), list(along_y.values())), gates[2]))
    for dy in range(1, grid.ny):
        for dx in range(1, grid.nx):
            parts.append(grid.send(firsts[dx - 1], dy=dy))
            parts.append(grid.send(seconds[dy - 1], dx=dx))
    at = grid.nx + grid.ny - 1
    parts = parts[:at] + after(parts[at:], gates[3])
    return parts + [grid.send(p, dc=1) for p in parts]


def send_state(grid, w, f, fs, s, ss, counts, key_width, gate):
    peers = grid.size
    slots, block = w.shape
    unit = slots // peers
    per_row = key_width // block
    unit_rows = unit // per_row
    shape = (peers, unit_rows, key_width)
    pad = lambda a: jnp.pad(a, (0, key_width - a.shape[0]))
    facts = jnp.stack([pad(fs), pad(ss), pad(counts[0].astype(jnp.float32))])
    packed, payload = pack_units(unit, counts, facts, *after((w, f, s), gate), shape)
    return packed, [payload] + [grid.send(payload, dz=dz) for dz in range(1, grid.nz)]


def apply_state(grid, me, cot, near, got, w, key_width, gates, sums, gradient):
    peers = grid.size
    slots, block = w.shape
    unit = slots // peers
    per_row = key_width // block
    parts = spread_weight(grid, near, gates)
    where = me.reshape(1)
    plan = plan_units(grid, unit, where, parts)
    input_grad, own, extra = product(grid, where, plan, cot, parts)
    return input_grad, *finish(unit, where, plan, sums, gradient, own, extra, got)


def state_by_blocks(grid, me, cot, w, f, fs, s, ss, counts, key_width):
    peers = grid.size
    slots, block = w.shape
    per_row = key_width // block
    rows = slots // per_row
    gather = lambda a: lax.all_gather(a, AXES, axis=0, tiled=True)
    table = gather(counts)
    starts = jnp.cumsum(table, axis=1) - table
    offsets = jnp.cumsum(table, axis=0) - table
    j = jnp.arange(slots, dtype=jnp.int32)
    ahead = j[None, None, :] - offsets[:, :, None]
    hit = (ahead >= 0) & (ahead < table[:, :, None])
    holder = jnp.arange(peers, dtype=jnp.int32)[:, None, None]
    pick = jnp.sum(jnp.where(hit, holder * slots + starts[:, :, None] + ahead, 0), axis=0)
    weight = gather(w)[pick.reshape(-1)].reshape(-1, key_width)
    mine = lax.dynamic_index_in_dim(pick, me, 0, keepdims=False)
    own_weight = lax.dynamic_slice_in_dim(weight, me * rows, rows, 0)
    two = lambda a: gather(a)[mine].reshape(rows, key_width)
    scale = lambda a: gather(a)[mine].reshape(rows, per_row)
    input_grad = lax.dot_general(
        cot, weight, (((1,), (1,)), ((), ())), preferred_element_type=jnp.float32
    ).astype(jnp.bfloat16)
    return input_grad, own_weight, two(f), scale(fs), two(s), scale(ss)


def shards(
    hidden_states,
    key_cotangent,
    old_weight,
    old_first,
    old_first_scale,
    old_second,
    old_second_scale,
    send_counts,
):
    grid = Grid(lax.axis_size("cuts"), lax.axis_size("fsdp"))
    me = lax.axis_index(AXES).astype(jnp.int32)
    y, c, z, x = grid.split(me)
    slots, block = old_weight.shape
    key_width = key_cotangent.shape[1]
    rows = slots * block // key_width
    tokens = hidden_states.shape[0]
    peers = grid.size
    per_row = key_width // block
    unit = slots // peers
    by_units = unit % per_row == 0 and unit // per_row >= 8 and slots <= key_width and peers <= 128

    ny, nz, nx = grid.ny, grid.nz, grid.nx
    batches = [
        [(dy, dx) for dx in range(1, nx) for dy in reversed(range(ny))],
        [(dy, 0) for dy in reversed(range(ny))],
    ]

    where = me.reshape(1)
    pick = functools.partial(pick_columns, grid)
    picked = [pick(where, 1, batches[0], hidden_states, rows, key_cotangent)]
    picked.append(pick(after(where, picked[0]), 1, batches[1], hidden_states, rows))
    parts = [grid.send(p, dc=1) for p in picked]
    owns = [pick(after(where, picked[1]), 0, batches[0], hidden_states, rows)]
    owns.append(pick(after(where, owns[0]), 0, batches[1], hidden_states, rows))

    def job(dy, dx, side):
        which = 0 if dx else 1
        return which, batches[which].index((dy, dx)) * nz, side

    def terms(coded, jobs, *gate):
        count = 1 + max(j[0] for j in jobs)
        return partial_sums(coded, jobs, nz, after(key_cotangent, gate), owns[:count], parts[:count])

    sent_a, sent_b, made = {}, {}, ()
    for dx in range(1, nx):
        made = terms(True, [job(dy, dx, 0) for dy in range(ny)], made)
        sent_a[dx] = grid.send(made, dx=dx)
    first_made = made
    for dy in range(1, ny):
        made = terms(True, [job(dy, dx, 1) for dx in range(nx)], made)
        sent_b[dy] = grid.send(made, dy=dy)
    keep = terms(False, [job(dy, 0, 0) for dy in range(1, ny)] + [job(0, dx, 1) for dx in range(1, nx)], made)
    last = terms(False, [job(0, 0, 0), job(0, 0, 1)], keep)
    if by_units:
        packed, near = send_state(
            grid, old_weight, old_first, old_first_scale, old_second, old_second_scale, send_counts, key_width, picked[1]
        )
    late_a, late_b, coded_late = [], [], []
    kept = after(keep, (near, last)) if by_units else keep
    for dy in range(1, ny):
        coded_late.append(relay(nz, kept, (dy - 1) * nz, list(sent_a.values()), dy * nz))
        late_a.append(grid.send(coded_late[-1], dy=dy))
    for dx in range(1, nx):
        coded_late.append(relay(nz, kept, (ny + dx - 2) * nz, list(sent_b.values()), dx * nz))
        late_b.append(grid.send(coded_late[-1], dx=dx))
    if by_units:
        got = lax.all_to_all(packed, AXES, 0, 0, tiled=True)
    last = gather_terms(nz, after(last, coded_late), list(sent_a.values()), list(sent_b.values()))
    if by_units:
        last = after(last, got)
    mine = corner(nz, last, (0, nz), late_a, late_b)
    over_z = [grid.send(mine[dz], dz=dz) for dz in range(1, grid.nz)]
    gradient, square = total_gradient(tokens * peers, mine[0], over_z)
    sums = lax.all_to_all(
        jnp.broadcast_to(square[None, :1], (peers, 1, 128)), AXES, 0, 0, tiled=True
    ).reshape(peers, 128)

    if by_units:
        gates = (coded_late, (late_a, late_b), mine, square)
        return apply_state(grid, me, key_cotangent, near, got, old_weight, key_width, gates, sums, gradient)
    input_grad, own_weight, first, first_scale, second, second_scale = state_by_blocks(
        grid, me, key_cotangent, old_weight, old_first, old_first_scale, old_second, old_second_scale, send_counts, key_width
    )
    return input_grad, *adam_step(sums, gradient, own_weight, first, first_scale, second, second_scale)


def solution(mesh):
    placed = (
        P(("cuts", "fsdp"), None),
        P(("cuts", "fsdp"), None),
        P(("cuts", "fsdp"), None),
        P(("cuts", "fsdp"), None),
        P(("cuts", "fsdp")),
        P(("cuts", "fsdp"), None),
        P(("cuts", "fsdp")),
        P(("cuts", "fsdp"), None),
    )
    return jax.shard_map(
        shards,
        mesh=mesh,
        in_specs=placed,
        out_specs=(
            P(("cuts", "fsdp"), None),
            P(("cuts", "fsdp"), None),
            P(("cuts", "fsdp"), None),
            P(("cuts", "fsdp"), None),
            P(("cuts", "fsdp"), None),
            P(("cuts", "fsdp"), None),
        ),
        check_vma=False,
    )
```

```python
import functools

import jax
import jax.numpy as jnp
from jax import lax
from jax.experimental import pallas as pl
from jax.experimental.pallas import tpu as pltpu
from jax.sharding import PartitionSpec as P

STEP = 2000


beta_first = 0.9
beta_second = 0.95
adam_epsilon = 1e-05
learn_rate = 0.001
weight_decay = 0.1
clip_norm = 1.0
tiny_scale = 1e-30

AXES = ("cuts", "fsdp")
TAIL = 16
GROUP = 128


class Grid:
    def __init__(self, cuts, fsdp):
        self.cuts, self.fsdp = cuts, fsdp
        self.ny = cuts // 2
        self.nz = 4
        self.nx = fsdp // 4
        self.size = cuts * fsdp

    def split(self, i):
        x = i % self.nx
        z = (i // self.nx) % self.nz
        c = (i // self.fsdp) % 2
        y = i // (2 * self.fsdp)
        return y, c, z, x

    def join(self, y, c, z, x):
        return ((y * 2 + c) * self.nz + z) * self.nx + x

    def send(self, a, dy=0, dc=0, dz=0, dx=0):
        pairs = []
        for i in range(self.size):
            y, c, z, x = self.split(i)
            pairs.append((i, self.join(y ^ dy, c ^ dc, z ^ dz, x ^ dx)))
        return lax.ppermute(a, AXES, pairs)


SMALL = pl.CostEstimate(flops=1, bytes_accessed=1, transcendentals=0)


def params(mib):
    return pltpu.CompilerParams(vmem_limit_bytes=mib * 1024 * 1024)


def encode(g):
    top = jnp.max(jnp.abs(g), axis=0, keepdims=True)
    k = jnp.ceil(jnp.log2(jnp.maximum(top, 1e-30) / 32700.0) * 256.0)
    q = jnp.round(g * jnp.exp2(k * (-1.0 / 256.0)))
    return q.astype(jnp.int32).astype(jnp.int16), k


def tail_rows(ks, columns):
    filled = list(ks)
    if len(ks) < TAIL:
        filled.append(jnp.zeros((TAIL - len(ks), columns), jnp.float32))
    filled = jnp.concatenate(filled)
    return filled.astype(jnp.int32).astype(jnp.int16)


def scales_of(ref, row):
    k = ref[pl.ds(row, TAIL), :].astype(jnp.int32).astype(jnp.float32)
    return jnp.exp2(k * (1.0 / 256.0))


def decode(ref, row, rows, scale):
    return ref[pl.ds(row, rows), :].astype(jnp.int32).astype(jnp.float32) * scale


def pick_kernel(grid, core, groups, me_ref, hidden_ref, *refs):
    out, held, sems, out_sems = refs[-4:]
    rows = out.shape[2]
    y, c, z, x = grid.split(me_ref[0])
    owners = [grid.join(y ^ dy, c ^ core, z ^ dz, x ^ dx) for dy, dx in groups for dz in range(grid.nz)]
    copies, puts = [], []
    for i, owner in enumerate(owners):
        at = pl.multiple_of(owner * rows, rows)
        copies.append(pltpu.make_async_copy(hidden_ref.at[:, pl.ds(at, rows)], held.at[i], sems.at[i]))
    for i in range(len(owners), out.shape[0]):
        at = (i - len(owners)) * rows
        copies.append(pltpu.make_async_copy(refs[0].at[:, pl.ds(at, rows)], held.at[i], sems.at[i]))
    for copy in copies:
        copy.start()
    for i, copy in enumerate(copies):
        copy.wait()
        puts.append(pltpu.make_async_copy(held.at[i], out.at[i], out_sems.at[i]))
        puts[-1].start()
    for put in puts:
        put.wait()


def pick_columns(grid, me, core, groups, hidden, rows, *more):
    tokens = hidden.shape[0]
    if rows % 128:
        cut = lambda a, at: lax.dynamic_slice_in_dim(a, at * rows, rows, 1)
        y, c, z, x = grid.split(me[0])
        owners = [grid.join(y ^ dy, c ^ core, z ^ dz, x ^ dx) for dy, dx in groups for dz in range(grid.nz)]
        return jnp.stack([cut(hidden, o) for o in owners] + [cut(a, i) for a in more for i in range(a.shape[1] // rows)])
    blocks = len(groups) * grid.nz + sum(a.shape[1] // rows for a in more)
    return pl.pallas_call(
        functools.partial(pick_kernel, grid, core, groups),
        out_shape=jax.ShapeDtypeStruct((blocks, tokens, rows), hidden.dtype),
        in_specs=[pl.BlockSpec(memory_space=pltpu.SMEM)] + [pl.BlockSpec(memory_space=pl.ANY)] * (1 + len(more)),
        out_specs=pl.BlockSpec(memory_space=pl.ANY),
        scratch_shapes=[pltpu.VMEM((blocks, tokens, rows), hidden.dtype)] + [pltpu.SemaphoreType.DMA((blocks,))] * 2,
        compiler_params=params(56),
        cost_estimate=SMALL,
        name="pick_columns",
    )(me, hidden, *more)


def partial_kernel(coded, jobs, nz, count, c_ref, *refs):
    owns, parts, out = refs[:count], refs[count:-1], refs[-1]
    tokens, width = c_ref.shape
    half, rows = width // 2, owns[0].shape[2]
    last = parts[0].shape[0] - width // rows
    across = (((0,), (0,)), ((), ()))
    ks = []
    for n, (which, at, side) in enumerate(jobs):
        mine = c_ref[:, side * half : (side + 1) * half]
        blocks = range(last + side * half // rows, last + (side + 1) * half // rows)
        other = [parts[0][b] for b in blocks]
        other = other[0] if len(other) == 1 else jnp.concatenate(other, axis=1)
        for i in range(nz):
            g = lax.dot_general(mine, owns[which][at + i], across, preferred_element_type=jnp.float32)
            g = g + lax.dot_general(other, parts[which][at + i], across, preferred_element_type=jnp.float32)
            if coded:
                q, k = encode(g)
                out[pl.ds((n * nz + i) * half, half), :] = q
                ks.append(k)
            else:
                out[n * nz + i] = g
    if coded:
        out[pl.ds(len(jobs) * nz * half, TAIL), :] = tail_rows(ks, rows)


def partial_sums(coded, jobs, nz, cot, owns, parts):
    _, width = cot.shape
    half, rows = width // 2, owns[0].shape[2]
    blocks = len(jobs) * nz
    return pl.pallas_call(
        functools.partial(partial_kernel, coded, jobs, nz, len(owns)),
        out_shape=jax.ShapeDtypeStruct((blocks * half + TAIL, rows), jnp.int16)
        if coded
        else jax.ShapeDtypeStruct((blocks, half, rows), jnp.float32),
        compiler_params=params(24),
        cost_estimate=SMALL,
        name="partial_sums",
    )(cot, *owns, *parts)


def relay_kernel(keep_at, coded_at, nz, keep_ref, *refs):
    coded, out = refs[:-1], refs[-1]
    _, half, rows = keep_ref.shape
    tables = [scales_of(ref, ref.shape[0] - TAIL) for ref in coded]
    ks = []
    for i in range(nz):
        total = keep_ref[keep_at + i]
        for ref, s in zip(coded, tables):
            at = coded_at + i
            total = total + decode(ref, at * half, half, s[at : at + 1])
        q, k = encode(total)
        out[pl.ds(i * half, half), :] = q
        ks.append(k)
    out[pl.ds(nz * half, TAIL), :] = tail_rows(ks, rows)


def relay(nz, keep, keep_at, coded, coded_at):
    _, half, rows = keep.shape
    return pl.pallas_call(
        functools.partial(relay_kernel, keep_at, coded_at, nz),
        out_shape=jax.ShapeDtypeStruct((nz * half + TAIL, rows), jnp.int16),
        compiler_params=params(14),
        cost_estimate=SMALL,
        name="relay",
    )(keep, *coded)


def gather_kernel(count, nz, keep_ref, *refs):
    number = len(refs) - 3
    coded, (out, held, sems) = refs[:number], refs[number:]
    _, half, rows = keep_ref.shape
    copies = []
    for j, ref in enumerate(coded):
        for i, (at, size, to) in enumerate(((0, nz * half, 0), (ref.shape[0] - TAIL, TAIL, nz * half))):
            copies.append(pltpu.make_async_copy(ref.at[pl.ds(at, size)], held.at[j, pl.ds(to, size)], sems.at[2 * j + i]))
    for copy in copies:
        copy.start()
    for copy in copies:
        copy.wait()
    for n in range(2):
        mine = range(count) if n == 0 else range(count, number)
        tables = {j: scales_of(held.at[j], nz * half) for j in mine}
        for i in range(nz):
            total = keep_ref[n * nz + i]
            for j in mine:
                total = total + decode(held.at[j], i * half, half, tables[j][i : i + 1])
            out[n * nz + i] = total


def gather_terms(nz, keep, coded_a, coded_b):
    _, half, rows = keep.shape
    coded = list(coded_a) + list(coded_b)
    return pl.pallas_call(
        functools.partial(gather_kernel, len(coded_a), nz),
        out_shape=jax.ShapeDtypeStruct(keep.shape, keep.dtype),
        in_specs=[pl.BlockSpec(memory_space=pltpu.VMEM)] + [pl.BlockSpec(memory_space=pl.ANY)] * len(coded),
        scratch_shapes=[pltpu.VMEM((len(coded), nz * half + TAIL, rows), jnp.int16), pltpu.SemaphoreType.DMA((2 * len(coded),))],
        compiler_params=params(14),
        cost_estimate=SMALL,
        name="gather_terms",
    )(keep, *coded)


def corner_kernel(counts, keep_at, nz, keep_ref, *refs):
    coded, outs = refs[: sum(counts)], refs[sum(counts) :]
    _, half, rows = keep_ref.shape
    tables = [scales_of(ref, ref.shape[0] - TAIL) for ref in coded]
    for dz in range(nz):
        ks = []
        for i in range(2):
            total = keep_ref[keep_at[i] + dz]
            for j in range(i * counts[0], i * counts[0] + counts[i]):
                total = total + decode(coded[j], dz * half, half, tables[j][dz : dz + 1])
            if dz == 0:
                outs[0][pl.ds(i * half, half), :] = total
            else:
                q, k = encode(total)
                outs[dz][pl.ds(i * half, half), :] = q
                ks.append(k)
        if dz:
            outs[dz][pl.ds(2 * half, TAIL), :] = tail_rows(ks, rows)


def corner(nz, keep, keep_at, coded_a, coded_b):
    _, half, rows = keep.shape
    shapes = [jax.ShapeDtypeStruct((2 * half, rows), jnp.float32)]
    shapes += [jax.ShapeDtypeStruct((2 * half + TAIL, rows), jnp.int16)] * (nz - 1)
    return pl.pallas_call(
        functools.partial(corner_kernel, (len(coded_a), len(coded_b)), keep_at, nz),
        out_shape=shapes,
        compiler_params=params(18),
        cost_estimate=SMALL,
        name="corner",
    )(keep, *coded_a, *coded_b)


def total_kernel(tokens, keep_ref, *refs):
    grad_ref, sum_ref = refs[-2:]
    width, rows = keep_ref.shape
    half = width // 2
    scales = [scales_of(ref, width) for ref in refs[:-2]]
    square = jnp.zeros((1, rows), jnp.float32)
    for i in range(2):
        total = keep_ref[pl.ds(i * half, half), :]
        for ref, s in zip(refs[:-2], scales):
            total = total + decode(ref, i * half, half, s[i : i + 1])
        total = total / tokens
        grad_ref[:, i * half : (i + 1) * half] = jnp.transpose(total)
        square = square + jnp.sum(total * total, axis=0, keepdims=True)
    sum_ref[...] = jnp.broadcast_to(jnp.sum(square, axis=1, keepdims=True), sum_ref.shape)


def total_gradient(tokens, keep, coded, copies):
    width, rows = keep.shape
    return pl.pallas_call(
        functools.partial(total_kernel, tokens),
        out_shape=[jax.ShapeDtypeStruct((rows, width), jnp.float32), jax.ShapeDtypeStruct((copies, 1, 128), jnp.float32)],
        compiler_params=params(6),
        cost_estimate=SMALL,
        name="total_gradient",
    )(keep, *coded)


def adam_rows(sums_ref, grad_ref, w, f, fs_ref, s, ss_ref, wo, mo, mso, vo, vso):
    sums = sums_ref[...]
    square_sum = jnp.sum(sums, axis=0, keepdims=True)[:, :1]
    factor = jnp.minimum(1.0, clip_norm / (jnp.sqrt(square_sum) + 1e-06))
    rows, width = grad_ref.shape
    blocks = fs_ref.shape[1]
    size = width // blocks
    for i in range(blocks):
        at = slice(i * size, (i + 1) * size)
        clipped = grad_ref[:, at] * factor
        m_old = f[:, at].astype(jnp.float32) * fs_ref[:, i : i + 1]
        v_old = s[:, at].astype(jnp.float32) * ss_ref[:, i : i + 1]
        m_new = beta_first * m_old + (1.0 - beta_first) * clipped
        v_new = beta_second * v_old + (1.0 - beta_second) * clipped * clipped
        m_hat = m_new / (1.0 - beta_first**STEP)
        v_hat = v_new / (1.0 - beta_second**STEP)
        w_old = w[:, at].astype(jnp.float32)
        wo[:, at] = (
            w_old - learn_rate * (m_hat / (jnp.sqrt(v_hat) + adam_epsilon) + weight_decay * w_old)
        ).astype(jnp.bfloat16)
        m_scale = jnp.max(jnp.abs(m_new), axis=1, keepdims=True) + tiny_scale
        v_scale = jnp.max(v_new, axis=1, keepdims=True) + tiny_scale
        mo[:, at] = (m_new / m_scale).astype(jnp.bfloat16)
        vo[:, at] = (v_new / v_scale).astype(jnp.bfloat16)
        mso[i : i + 1, :] = jnp.transpose(jnp.broadcast_to(m_scale, (rows, 128)))[:1]
        vso[i : i + 1, :] = jnp.transpose(jnp.broadcast_to(v_scale, (rows, 128)))[:1]


def adam_kernel(sums_ref, grad_ref, w_ref, f_ref, fs_ref, s_ref, ss_ref, *outs):
    adam_rows(sums_ref, grad_ref, w_ref[...], f_ref[...], fs_ref, s_ref[...], ss_ref, *outs)


def adam_outputs(rows, width, blocks):
    codes = jax.ShapeDtypeStruct((rows, width), jnp.bfloat16)
    scale = jax.ShapeDtypeStruct((blocks, rows), jnp.float32)
    return [codes, codes, scale, codes, scale]


def adam_step(sums, grad, weight, first, first_scale, second, second_scale):
    w_new, m_code, m_scale, v_code, v_scale = pl.pallas_call(
        adam_kernel,
        out_shape=adam_outputs(*grad.shape, first_scale.shape[1]),
        compiler_params=params(8),
        cost_estimate=SMALL,
        name="adam",
    )(sums, grad, weight, first, first_scale, second, second_scale)
    return w_new, m_code, m_scale.T, v_code, v_scale.T


def three_parts(a):
    high = a.astype(jnp.bfloat16)
    rest = a - high.astype(jnp.float32)
    mid = rest.astype(jnp.bfloat16)
    return [high, mid, (rest - mid.astype(jnp.float32)).astype(jnp.bfloat16)]


def pack_kernel(unit, counts_ref, facts_ref, w_ref, f_ref, s_ref, out_ref, pay_ref, wide, first, second):
    peers, _, rows, width = out_ref.shape
    per_row = unit // rows

    def by_rows(ref):
        for j in range(wide.shape[0]):
            wide[j] = ref[:, j * 128 : (j + 1) * 128].astype(jnp.float32)
        sides = [
            wide[j, pl.ds(i, peers * rows, stride=per_row), :] for i in range(per_row) for j in range(wide.shape[0])
        ]
        return jnp.concatenate(sides, axis=1).astype(jnp.bfloat16).reshape(peers, rows, width)

    pay_ref[:peers] = by_rows(w_ref)
    first[...] = by_rows(f_ref)
    second[...] = by_rows(s_ref)
    start, extra = jnp.int32(0), jnp.int32(0)
    for e in range(peers):
        units = counts_ref[0, e] // unit
        at = jnp.minimum(start, peers - 1)
        out_ref[e, 0] = first[at]
        out_ref[e, 1] = second[at]
        extra = jnp.where(units == 2, start + 1, extra)
        start = start + units
    pay_ref[peers] = first[extra]
    pay_ref[peers + 1] = second[extra]
    facts = facts_ref[...]
    meta = [p.astype(jnp.float32) for i in range(2) for p in three_parts(facts[i : i + 1])]
    meta = jnp.concatenate(meta + [facts[2:3], jnp.zeros((rows - 7, width), jnp.float32)])
    pay_ref[peers + 2] = meta.astype(jnp.bfloat16)


def pack_units(unit, counts, facts, w, f, s, shape):
    peers, rows, width = shape
    return pl.pallas_call(
        functools.partial(pack_kernel, unit),
        out_shape=[
            jax.ShapeDtypeStruct((peers, 2, rows, width), w.dtype),
            jax.ShapeDtypeStruct((peers + 3, rows, width), w.dtype),
        ],
        in_specs=[pl.BlockSpec(memory_space=pltpu.SMEM)] + [pl.BlockSpec(memory_space=pltpu.VMEM)] * 4,
        scratch_shapes=[pltpu.VMEM((w.shape[1] // 128, w.shape[0], 128), jnp.float32)] + [pltpu.VMEM(shape, w.dtype)] * 2,
        compiler_params=params(8),
        cost_estimate=SMALL,
        name="pack_units",
    )(counts, facts, w, f, s)


def place_of(grid, units, me, holder, slot):
    dy, dc, dz, dx = (p ^ q for p, q in zip(grid.split(holder), grid.split(me)))
    nx, ny, nz = grid.nx, grid.ny, grid.nz
    cut = (units + 1) // 2
    whole = nz * units
    straight = jnp.where(dy == 0, dx, nx - 1 + dy) * whole + dz * units
    across = (nx + ny - 1 + (dy - 1) * (nx - 1) + (dx - 1)) * whole
    on_axis = (dy == 0) | (dx == 0)
    first = jnp.where(on_axis, straight, across + dz * cut)
    second = jnp.where(on_axis, straight, across + nz * cut + dz * (units - cut) - cut)
    return dc * (nx * ny * whole) + slot + jnp.where(slot < cut, first, second)


def plan_kernel(grid, unit, units, me_ref, *refs):
    parts, (plan_ref, meta_ref, sems) = refs[:-3], refs[-3:]
    peers, lanes = meta_ref.shape[0], plan_ref.shape[1]
    me = me_ref[0]
    copies = []
    for rel in range(peers):
        at, which = place_of_static(grid, units, rel, units - 1), 0
        while at >= parts[which].shape[0]:
            at -= parts[which].shape[0]
            which += 1
        copies.append(pltpu.make_async_copy(parts[which].at[at], meta_ref.at[me ^ rel], sems.at[rel]))
    for copy in copies:
        copy.start()
    for copy in copies:
        copy.wait()
    table = jnp.concatenate([meta_ref[d].astype(jnp.float32)[6:7, :lanes] for d in range(peers)]) * (1.0 / unit)
    row = lax.broadcasted_iota(jnp.int32, (lanes, lanes), 0)
    col = lax.broadcasted_iota(jnp.int32, (lanes, lanes), 1)
    starts = jnp.dot(table, (row < col).astype(jnp.float32), preferred_element_type=jnp.float32).astype(jnp.int32)
    ahead_of = (col < row).astype(jnp.float32)[:peers, :peers]
    offsets = jnp.dot(ahead_of, table, preferred_element_type=jnp.float32).astype(jnp.int32)
    table = table.astype(jnp.int32)
    unit_at = lax.broadcasted_iota(jnp.int32, (peers, lanes), 0)
    zero = jnp.zeros((peers, lanes), jnp.int32)
    place, holder, late, slots = zero, zero, zero, zero
    for d in range(peers):
        ahead = unit_at - offsets[d : d + 1]
        hit = (ahead >= 0) & (ahead < table[d : d + 1])
        slot = starts[d : d + 1] + ahead
        place = jnp.where(hit, place_of(grid, units, me, d, slot), place)
        holder = jnp.where(hit, d, holder)
        late = jnp.where(hit, ahead, late)
        slots = jnp.where(hit, slot, slots)
    for i, a in enumerate((place, holder, late, slots)):
        plan_ref[pl.ds(i * peers, peers), :] = a


def place_of_static(grid, units, rel, slot):
    dy, dc, dz, dx = grid.split(rel)
    nx, ny, nz = grid.nx, grid.ny, grid.nz
    cut = (units + 1) // 2
    whole = nz * units
    at = dc * (nx * ny * whole) + slot
    if dy == 0 or dx == 0:
        return at + (dx if dy == 0 else nx - 1 + dy) * whole + dz * units
    at += (nx + ny - 1 + (dy - 1) * (nx - 1) + (dx - 1)) * whole
    return at + (dz * cut if slot < cut else nz * cut + dz * (units - cut) - cut)


def plan_units(grid, unit, me, parts):
    lanes = max(128, grid.size)
    rows, width = parts[0].shape[-2:]
    units = parts[0].shape[1]
    parts = [p.reshape(-1, rows, width) for p in parts]
    return pl.pallas_call(
        functools.partial(plan_kernel, grid, unit, units),
        out_shape=[
            jax.ShapeDtypeStruct((4 * grid.size, lanes), jnp.int32),
            jax.ShapeDtypeStruct((grid.size, rows, width), parts[0].dtype),
        ],
        in_specs=[pl.BlockSpec(memory_space=pltpu.SMEM)] + [pl.BlockSpec(memory_space=pl.ANY)] * len(parts),
        scratch_shapes=[pltpu.SemaphoreType.DMA((grid.size,))],
        compiler_params=params(8),
        cost_estimate=SMALL,
        name="plan_units",
    )(me, *parts)


def finish_kernel(unit, me_ref, sums_ref, *refs):
    ins, outs, (plan, grad_ref, own_ref, meta, got, first, second, fs, ss, scales, sems) = refs[:5], refs[5:10], refs[10:]
    held = (plan, grad_ref, own_ref, meta, got)
    copies = [pltpu.make_async_copy(a, b, sems.at[i]) for i, (a, b) in enumerate(zip(ins, held))]
    for copy in copies:
        copy.start()
    for copy in copies:
        copy.wait()
    peers, rows, width = first.shape
    me = me_ref[0]
    for d in range(peers):
        facts = meta[d].astype(jnp.float32)
        scales[0, pl.ds(d, 1), :] = facts[0:1] + facts[1:2] + facts[2:3]
        scales[1, pl.ds(d, 1), :] = facts[3:4] + facts[4:5] + facts[5:6]
    per_row = unit // rows
    lane = lax.broadcasted_iota(jnp.int32, (rows, width), 1)
    block = lax.broadcasted_iota(jnp.int32, (rows, width), 0) * per_row
    late = jnp.int32(0)
    for u in range(peers):
        p = plan[peers + u, me]
        first[u] = got[p, 0]
        second[u] = got[p, 1]
        late = jnp.where(plan[2 * peers + u, me] == 1, u, late)
        at = lane - (plan[3 * peers + u, me] * unit + block)
        for i, out in enumerate((fs, ss)):
            line = jnp.broadcast_to(scales[i, pl.ds(p, 1), :], (rows, width))
            for h in range(per_row):
                value = jnp.sum(jnp.where(at == h, line, 0.0), axis=1, keepdims=True)
                out[pl.ds(u * rows, rows), h : h + 1] = value
    first[late] = own_ref[peers]
    second[late] = own_ref[peers + 1]
    two = lambda ref: ref[:peers].reshape(peers * rows, width)
    adam_rows(sums_ref, grad_ref, two(own_ref), two(first), fs, two(second), ss, *outs)


def finish(unit, me, plan, sums, grad, own, got):
    peers, rows, width = plan[1].shape
    blocks = unit // rows
    smem, vmem, anywhere = (pl.BlockSpec(memory_space=m) for m in (pltpu.SMEM, pltpu.VMEM, pl.ANY))
    units, scale = pltpu.VMEM(plan[1].shape, own.dtype), pltpu.VMEM((peers * rows, blocks), jnp.float32)
    w_new, m_code, m_scale, v_code, v_scale = pl.pallas_call(
        functools.partial(finish_kernel, unit),
        out_shape=adam_outputs(peers * rows, width, blocks),
        in_specs=[smem, vmem] + [anywhere] * 5,
        scratch_shapes=[pltpu.SMEM(plan[0].shape, jnp.int32)]
        + [pltpu.VMEM(a.shape, a.dtype) for a in (grad, own, plan[1], got)]
        + [units, units, scale, scale, pltpu.VMEM((2, peers, width), jnp.float32), pltpu.SemaphoreType.DMA((5,))],
        compiler_params=params(56),
        cost_estimate=SMALL,
        name="finish",
    )(me, sums, plan[0], grad, own, plan[1], got)
    return w_new, m_code, m_scale.T, v_code, v_scale.T


def stack_kernel(*refs):
    out, sems = refs[-2:]
    copies = [pltpu.make_async_copy(ref, out.at[i], sems.at[i]) for i, ref in enumerate(refs[:-2])]
    for copy in copies:
        copy.start()
    for copy in copies:
        copy.wait()


def stack_parts(parts):
    return pl.pallas_call(
        stack_kernel,
        out_shape=jax.ShapeDtypeStruct((len(parts),) + parts[0].shape, parts[0].dtype),
        in_specs=[pl.BlockSpec(memory_space=pl.ANY)] * len(parts),
        scratch_shapes=[pltpu.SemaphoreType.DMA((len(parts),))],
        compiler_params=params(56),
        cost_estimate=SMALL,
        name="stack_parts",
    )(*parts)


def halves_kernel(count, *refs):
    sems = refs[-1]
    ins, outs = refs[: len(refs) // 2], refs[len(refs) // 2 : -1]
    copies = []
    for n, (ref, out) in enumerate(zip(ins, outs)):
        cut = out.shape[1]
        copies.append(pltpu.make_async_copy(ref.at[:, pl.ds(0 if n < count else ref.shape[1] - cut, cut)], out, sems.at[n]))
    for copy in copies:
        copy.start()
    for copy in copies:
        copy.wait()


def halves(firsts, seconds):
    ins = firsts + seconds
    nz, units, rows, width = ins[0].shape
    cuts = [(units + 1) // 2] * len(firsts) + [units // 2] * len(seconds)
    outs = pl.pallas_call(
        functools.partial(halves_kernel, len(firsts)),
        out_shape=[jax.ShapeDtypeStruct((nz, cut, rows, width), ins[0].dtype) for cut in cuts],
        in_specs=[pl.BlockSpec(memory_space=pl.ANY)] * len(ins),
        scratch_shapes=[pltpu.SemaphoreType.DMA((len(ins),))],
        compiler_params=params(8),
        cost_estimate=SMALL,
        name="halves",
    )(*ins)
    return outs[: len(firsts)], outs[len(firsts) :]


def product_kernel(count, group, grid, me_ref, plan_ref, cot_ref, *refs):
    parts, (out_ref, own_ref, plan, held, tile, made, sems, out_sems) = refs[:count], refs[count:]
    copies, at = [pltpu.make_async_copy(plan_ref, plan, sems.at[count])], 0
    for i, ref in enumerate(parts):
        copies.append(pltpu.make_async_copy(ref, held.at[pl.ds(at, ref.shape[0])], sems.at[i]))
        at += ref.shape[0]
    for copy in copies:
        copy.start()
    for copy in copies:
        copy.wait()
    steps, _, columns = made.shape
    peers = own_ref.shape[0] - 2

    def put(i):
        return pltpu.make_async_copy(
            made.at[i], out_ref.at[:, pl.ds(pl.multiple_of(i * columns, columns), columns)], out_sems.at[i]
        )

    def step(i, carry):
        for u in range(group):
            tile[u] = held[plan[u % peers, i * (group // peers) + u // peers]]
        weight = tile[...].reshape(group * tile.shape[1], tile.shape[2])
        made[i] = lax.dot_general(
            cot_ref[...], weight, (((1,), (1,)), ((), ())), preferred_element_type=jnp.float32
        ).astype(made.dtype)
        put(i).start()
        return carry

    lax.fori_loop(0, steps, step, 0, unroll=True)
    me = me_ref[0]
    late = jnp.int32(0)
    for u in range(peers):
        own_ref[u] = held[plan[u, me]]
        late = jnp.where(plan[2 * peers + u, me] == 1, plan[peers + u, me], late)
    extra = place_of(grid, peers + 3, me, late, peers)
    own_ref[peers] = held[extra]
    own_ref[peers + 1] = held[extra + 1]

    def finish(i, carry):
        put(i).wait()
        return carry

    lax.fori_loop(0, steps, finish, 0)


def product(grid, me, plan, cot, parts):
    rows, width = parts[0].shape[-2:]
    parts = [p.reshape(-1, rows, width) for p in parts]
    peers = grid.size
    total = peers * peers
    group = GROUP
    tokens = cot.shape[0]
    smem, vmem, anywhere = (pl.BlockSpec(memory_space=m) for m in (pltpu.SMEM, pltpu.VMEM, pl.ANY))
    return pl.pallas_call(
        functools.partial(product_kernel, len(parts), group, grid),
        out_shape=[
            jax.ShapeDtypeStruct((tokens, total * rows), cot.dtype),
            jax.ShapeDtypeStruct((peers + 2, rows, width), cot.dtype),
        ],
        in_specs=[smem, anywhere, vmem] + [anywhere] * len(parts),
        out_specs=[anywhere, vmem],
        scratch_shapes=[
            pltpu.SMEM(plan[0].shape, jnp.int32),
            pltpu.VMEM((sum(p.shape[0] for p in parts), rows, width), cot.dtype),
            pltpu.VMEM((group, rows, width), cot.dtype),
            pltpu.VMEM((total // group, tokens, group * rows), cot.dtype),
            pltpu.SemaphoreType.DMA((len(parts) + 1,)),
            pltpu.SemaphoreType.DMA((total // group,)),
        ],
        compiler_params=params(28),
        cost_estimate=SMALL,
        name="product",
    )(me, plan[0], cot, *parts)


def after(a, *others):
    return lax.optimization_barrier((a, others))[0]


def spread_weight(grid, near, gates):
    near = after(stack_parts(after(near, gates[0])), gates[1])
    along_x = {dx: grid.send(near, dx=dx) for dx in range(1, grid.nx)}
    along_y = {dy: grid.send(near, dy=dy) for dy in range(1, grid.ny)}
    parts = [near] + list(along_x.values()) + list(along_y.values())
    firsts, seconds = halves(*after((list(along_x.values()), list(along_y.values())), gates[2]))
    for dy in range(1, grid.ny):
        for dx in range(1, grid.nx):
            parts.append(grid.send(firsts[dx - 1], dy=dy))
            parts.append(grid.send(seconds[dy - 1], dx=dx))
    at = grid.nx + grid.ny - 1
    parts = parts[:at] + after(parts[at:], gates[3])
    return parts + [grid.send(p, dc=1) for p in parts]


def send_state(grid, w, f, fs, s, ss, counts, key_width, gate):
    peers = grid.size
    slots, block = w.shape
    unit = slots // peers
    per_row = key_width // block
    unit_rows = unit // per_row
    shape = (peers, unit_rows, key_width)
    pad = lambda a: jnp.pad(a, (0, key_width - a.shape[0]))
    facts = jnp.stack([pad(fs), pad(ss), pad(counts[0].astype(jnp.float32))])
    packed, payload = pack_units(unit, counts, facts, *after((w, f, s), gate), shape)
    return packed, [payload] + [grid.send(payload, dz=dz) for dz in range(1, grid.nz)]


def apply_state(grid, me, cot, near, got, w, key_width, gates, sums, gradient):
    peers = grid.size
    slots, block = w.shape
    unit = slots // peers
    per_row = key_width // block
    parts = spread_weight(grid, near, gates)
    where = me.reshape(1)
    plan = plan_units(grid, unit, where, parts)
    input_grad, own = product(grid, where, plan, cot, parts)
    return input_grad, *finish(unit, where, plan, sums, gradient, own, got)


def state_by_blocks(grid, me, cot, w, f, fs, s, ss, counts, key_width):
    peers = grid.size
    slots, block = w.shape
    per_row = key_width // block
    rows = slots // per_row
    gather = lambda a: lax.all_gather(a, AXES, axis=0, tiled=True)
    table = gather(counts)
    starts = jnp.cumsum(table, axis=1) - table
    offsets = jnp.cumsum(table, axis=0) - table
    j = jnp.arange(slots, dtype=jnp.int32)
    ahead = j[None, None, :] - offsets[:, :, None]
    hit = (ahead >= 0) & (ahead < table[:, :, None])
    holder = jnp.arange(peers, dtype=jnp.int32)[:, None, None]
    pick = jnp.sum(jnp.where(hit, holder * slots + starts[:, :, None] + ahead, 0), axis=0)
    weight = gather(w)[pick.reshape(-1)].reshape(-1, key_width)
    mine = lax.dynamic_index_in_dim(pick, me, 0, keepdims=False)
    own_weight = lax.dynamic_slice_in_dim(weight, me * rows, rows, 0)
    two = lambda a: gather(a)[mine].reshape(rows, key_width)
    scale = lambda a: gather(a)[mine].reshape(rows, per_row)
    input_grad = lax.dot_general(
        cot, weight, (((1,), (1,)), ((), ())), preferred_element_type=jnp.float32
    ).astype(jnp.bfloat16)
    return input_grad, own_weight, two(f), scale(fs), two(s), scale(ss)


def shards(
    hidden_states,
    key_cotangent,
    old_weight,
    old_first,
    old_first_scale,
    old_second,
    old_second_scale,
    send_counts,
):
    grid = Grid(lax.axis_size("cuts"), lax.axis_size("fsdp"))
    me = lax.axis_index(AXES).astype(jnp.int32)
    y, c, z, x = grid.split(me)
    slots, block = old_weight.shape
    key_width = key_cotangent.shape[1]
    rows = slots * block // key_width
    tokens = hidden_states.shape[0]
    peers = grid.size
    per_row = key_width // block
    unit = slots // peers
    by_units = unit % per_row == 0 and unit // per_row >= 8 and slots <= key_width and peers <= 128

    ny, nz, nx = grid.ny, grid.nz, grid.nx
    batches = [
        [(dy, dx) for dx in range(1, nx) for dy in reversed(range(ny))],
        [(dy, 0) for dy in reversed(range(ny))],
    ]

    where = me.reshape(1)
    pick = functools.partial(pick_columns, grid)
    picked = [pick(where, 1, batches[0], hidden_states, rows, key_cotangent)]
    picked.append(pick(after(where, picked[0]), 1, batches[1], hidden_states, rows))
    parts = [grid.send(p, dc=1) for p in picked]
    owns = [pick(after(where, picked[1]), 0, batches[0], hidden_states, rows)]
    owns.append(pick(after(where, owns[0]), 0, batches[1], hidden_states, rows))

    def job(dy, dx, side):
        which = 0 if dx else 1
        return which, batches[which].index((dy, dx)) * nz, side

    def terms(coded, jobs, *gate):
        count = 1 + max(j[0] for j in jobs)
        return partial_sums(coded, jobs, nz, after(key_cotangent, gate), owns[:count], parts[:count])

    sent_a, sent_b, made = {}, {}, ()
    for dx in range(1, nx):
        made = terms(True, [job(dy, dx, 0) for dy in range(ny)], made)
        sent_a[dx] = grid.send(made, dx=dx)
    first_made = made
    for dy in range(1, ny):
        made = terms(True, [job(dy, dx, 1) for dx in range(nx)], made)
        sent_b[dy] = grid.send(made, dy=dy)
    keep = terms(False, [job(dy, 0, 0) for dy in range(1, ny)] + [job(0, dx, 1) for dx in range(1, nx)], made)
    last = terms(False, [job(0, 0, 0), job(0, 0, 1)], keep)
    if by_units:
        packed, near = send_state(
            grid, old_weight, old_first, old_first_scale, old_second, old_second_scale, send_counts, key_width, picked[1]
        )
    late_a, late_b, coded_late = [], [], []
    kept = after(keep, (near, last)) if by_units else keep
    for dy in range(1, ny):
        coded_late.append(relay(nz, kept, (dy - 1) * nz, list(sent_a.values()), dy * nz))
        late_a.append(grid.send(coded_late[-1], dy=dy))
    for dx in range(1, nx):
        coded_late.append(relay(nz, kept, (ny + dx - 2) * nz, list(sent_b.values()), dx * nz))
        late_b.append(grid.send(coded_late[-1], dx=dx))
    if by_units:
        got = lax.all_to_all(packed, AXES, 0, 0, tiled=True)
    last = gather_terms(nz, after(last, coded_late), list(sent_a.values()), list(sent_b.values()))
    if by_units:
        last = after(last, got)
    mine = corner(nz, last, (0, nz), late_a, late_b)
    over_z = [grid.send(mine[dz], dz=dz) for dz in range(1, grid.nz)]
    gradient, square = total_gradient(tokens * peers, mine[0], over_z, peers)
    sums = lax.all_to_all(square, AXES, 0, 0, tiled=True).reshape(peers, 128)

    if by_units:
        gates = (coded_late, (late_a, late_b), mine, square)
        return apply_state(grid, me, key_cotangent, near, got, old_weight, key_width, gates, sums, gradient)
    input_grad, own_weight, first, first_scale, second, second_scale = state_by_blocks(
        grid, me, key_cotangent, old_weight, old_first, old_first_scale, old_second, old_second_scale, send_counts, key_width
    )
    return input_grad, *adam_step(sums, gradient, own_weight, first, first_scale, second, second_scale)


def solution(mesh):
    placed = (
        P(("cuts", "fsdp"), None),
        P(("cuts", "fsdp"), None),
        P(("cuts", "fsdp"), None),
        P(("cuts", "fsdp"), None),
        P(("cuts", "fsdp")),
        P(("cuts", "fsdp"), None),
        P(("cuts", "fsdp")),
        P(("cuts", "fsdp"), None),
    )
    return jax.shard_map(
        shards,
        mesh=mesh,
        in_specs=placed,
        out_specs=(
            P(("cuts", "fsdp"), None),
            P(("cuts", "fsdp"), None),
            P(("cuts", "fsdp"), None),
            P(("cuts", "fsdp"), None),
            P(("cuts", "fsdp"), None),
            P(("cuts", "fsdp"), None),
        ),
        check_vma=False,
    )
```

```python
import functools

import jax
import jax.numpy as jnp
from jax import lax
from jax.experimental import pallas as pl
from jax.experimental.pallas import tpu as pltpu
from jax.sharding import PartitionSpec as P

STEP = 2000


beta_first = 0.9
beta_second = 0.95
adam_epsilon = 1e-05
learn_rate = 0.001
weight_decay = 0.1
clip_norm = 1.0
tiny_scale = 1e-30

AXES = ("cuts", "fsdp")
TAIL = 16
GROUP = 128


class Grid:
    def __init__(self, cuts, fsdp):
        self.cuts, self.fsdp = cuts, fsdp
        self.ny = cuts // 2
        self.nz = 4
        self.nx = fsdp // 4
        self.size = cuts * fsdp

    def split(self, i):
        x = i % self.nx
        z = (i // self.nx) % self.nz
        c = (i // self.fsdp) % 2
        y = i // (2 * self.fsdp)
        return y, c, z, x

    def join(self, y, c, z, x):
        return ((y * 2 + c) * self.nz + z) * self.nx + x

    def send(self, a, dy=0, dc=0, dz=0, dx=0):
        pairs = []
        for i in range(self.size):
            y, c, z, x = self.split(i)
            pairs.append((i, self.join(y ^ dy, c ^ dc, z ^ dz, x ^ dx)))
        return lax.ppermute(a, AXES, pairs)


SMALL = pl.CostEstimate(flops=1, bytes_accessed=1, transcendentals=0)


def params(mib):
    return pltpu.CompilerParams(vmem_limit_bytes=mib * 1024 * 1024)


def encode(g):
    top = jnp.max(jnp.abs(g), axis=0, keepdims=True)
    k = jnp.ceil(jnp.log2(jnp.maximum(top, 1e-30) / 32700.0) * 256.0)
    q = jnp.round(g * jnp.exp2(k * (-1.0 / 256.0)))
    return q.astype(jnp.int32).astype(jnp.int16), k


def tail_rows(ks, columns):
    filled = list(ks)
    if len(ks) < TAIL:
        filled.append(jnp.zeros((TAIL - len(ks), columns), jnp.float32))
    filled = jnp.concatenate(filled)
    return filled.astype(jnp.int32).astype(jnp.int16)


def scales_of(ref, row):
    k = ref[pl.ds(row, TAIL), :].astype(jnp.int32).astype(jnp.float32)
    return jnp.exp2(k * (1.0 / 256.0))


def decode(ref, row, rows, scale):
    return ref[pl.ds(row, rows), :].astype(jnp.int32).astype(jnp.float32) * scale


def pick_kernel(grid, core, groups, me_ref, hidden_ref, *refs):
    out, held, sems, out_sems = refs[-4:]
    rows = out.shape[2]
    y, c, z, x = grid.split(me_ref[0])
    owners = [grid.join(y ^ dy, c ^ core, z ^ dz, x ^ dx) for dy, dx in groups for dz in range(grid.nz)]
    copies, puts = [], []
    for i, owner in enumerate(owners):
        at = pl.multiple_of(owner * rows, rows)
        copies.append(pltpu.make_async_copy(hidden_ref.at[:, pl.ds(at, rows)], held.at[i], sems.at[i]))
    for i in range(len(owners), out.shape[0]):
        at = (i - len(owners)) * rows
        copies.append(pltpu.make_async_copy(refs[0].at[:, pl.ds(at, rows)], held.at[i], sems.at[i]))
    for copy in copies:
        copy.start()
    for i, copy in enumerate(copies):
        copy.wait()
        puts.append(pltpu.make_async_copy(held.at[i], out.at[i], out_sems.at[i]))
        puts[-1].start()
    for put in puts:
        put.wait()


def pick_columns(grid, me, core, groups, hidden, rows, *more):
    tokens = hidden.shape[0]
    if rows % 128:
        cut = lambda a, at: lax.dynamic_slice_in_dim(a, at * rows, rows, 1)
        y, c, z, x = grid.split(me[0])
        owners = [grid.join(y ^ dy, c ^ core, z ^ dz, x ^ dx) for dy, dx in groups for dz in range(grid.nz)]
        return jnp.stack([cut(hidden, o) for o in owners] + [cut(a, i) for a in more for i in range(a.shape[1] // rows)])
    blocks = len(groups) * grid.nz + sum(a.shape[1] // rows for a in more)
    return pl.pallas_call(
        functools.partial(pick_kernel, grid, core, groups),
        out_shape=jax.ShapeDtypeStruct((blocks, tokens, rows), hidden.dtype),
        in_specs=[pl.BlockSpec(memory_space=pltpu.SMEM)] + [pl.BlockSpec(memory_space=pl.ANY)] * (1 + len(more)),
        out_specs=pl.BlockSpec(memory_space=pl.ANY),
        scratch_shapes=[pltpu.VMEM((blocks, tokens, rows), hidden.dtype)] + [pltpu.SemaphoreType.DMA((blocks,))] * 2,
        compiler_params=params(56),
        cost_estimate=SMALL,
        name="pick_columns",
    )(me, hidden, *more)


def partial_kernel(coded, jobs, nz, count, c_ref, *refs):
    owns, parts, out = refs[:count], refs[count:-1], refs[-1]
    tokens, width = c_ref.shape
    half, rows = width // 2, owns[0].shape[2]
    last = parts[0].shape[0] - width // rows
    across = (((0,), (0,)), ((), ()))
    ks = []
    for n, (which, at, side) in enumerate(jobs):
        mine = c_ref[:, side * half : (side + 1) * half]
        blocks = range(last + side * half // rows, last + (side + 1) * half // rows)
        other = [parts[0][b] for b in blocks]
        other = other[0] if len(other) == 1 else jnp.concatenate(other, axis=1)
        for i in range(nz):
            g = lax.dot_general(mine, owns[which][at + i], across, preferred_element_type=jnp.float32)
            g = g + lax.dot_general(other, parts[which][at + i], across, preferred_element_type=jnp.float32)
            if coded:
                q, k = encode(g)
                out[pl.ds((n * nz + i) * half, half), :] = q
                ks.append(k)
            else:
                out[n * nz + i] = g
    if coded:
        out[pl.ds(len(jobs) * nz * half, TAIL), :] = tail_rows(ks, rows)


def partial_sums(coded, jobs, nz, cot, owns, parts):
    _, width = cot.shape
    half, rows = width // 2, owns[0].shape[2]
    blocks = len(jobs) * nz
    return pl.pallas_call(
        functools.partial(partial_kernel, coded, jobs, nz, len(owns)),
        out_shape=jax.ShapeDtypeStruct((blocks * half + TAIL, rows), jnp.int16)
        if coded
        else jax.ShapeDtypeStruct((blocks, half, rows), jnp.float32),
        compiler_params=params(24),
        cost_estimate=SMALL,
        name="partial_sums",
    )(cot, *owns, *parts)


def relay_kernel(keep_at, coded_at, nz, keep_ref, *refs):
    coded, out = refs[:-1], refs[-1]
    _, half, rows = keep_ref.shape
    tables = [scales_of(ref, ref.shape[0] - TAIL) for ref in coded]
    ks = []
    for i in range(nz):
        total = keep_ref[keep_at + i]
        for ref, s in zip(coded, tables):
            at = coded_at + i
            total = total + decode(ref, at * half, half, s[at : at + 1])
        q, k = encode(total)
        out[pl.ds(i * half, half), :] = q
        ks.append(k)
    out[pl.ds(nz * half, TAIL), :] = tail_rows(ks, rows)


def relay(nz, keep, keep_at, coded, coded_at):
    _, half, rows = keep.shape
    return pl.pallas_call(
        functools.partial(relay_kernel, keep_at, coded_at, nz),
        out_shape=jax.ShapeDtypeStruct((nz * half + TAIL, rows), jnp.int16),
        compiler_params=params(14),
        cost_estimate=SMALL,
        name="relay",
    )(keep, *coded)


def gather_kernel(count, nz, keep_ref, *refs):
    number = len(refs) - 3
    coded, (out, held, sems) = refs[:number], refs[number:]
    _, half, rows = keep_ref.shape
    copies = []
    for j, ref in enumerate(coded):
        for i, (at, size, to) in enumerate(((0, nz * half, 0), (ref.shape[0] - TAIL, TAIL, nz * half))):
            copies.append(pltpu.make_async_copy(ref.at[pl.ds(at, size)], held.at[j, pl.ds(to, size)], sems.at[2 * j + i]))
    for copy in copies:
        copy.start()
    for copy in copies:
        copy.wait()
    for n in range(2):
        mine = range(count) if n == 0 else range(count, number)
        tables = {j: scales_of(held.at[j], nz * half) for j in mine}
        for i in range(nz):
            total = keep_ref[n * nz + i]
            for j in mine:
                total = total + decode(held.at[j], i * half, half, tables[j][i : i + 1])
            out[n * nz + i] = total


def gather_terms(nz, keep, coded_a, coded_b):
    _, half, rows = keep.shape
    coded = list(coded_a) + list(coded_b)
    return pl.pallas_call(
        functools.partial(gather_kernel, len(coded_a), nz),
        out_shape=jax.ShapeDtypeStruct(keep.shape, keep.dtype),
        in_specs=[pl.BlockSpec(memory_space=pltpu.VMEM)] + [pl.BlockSpec(memory_space=pl.ANY)] * len(coded),
        scratch_shapes=[pltpu.VMEM((len(coded), nz * half + TAIL, rows), jnp.int16), pltpu.SemaphoreType.DMA((2 * len(coded),))],
        compiler_params=params(14),
        cost_estimate=SMALL,
        name="gather_terms",
    )(keep, *coded)


def corner_kernel(counts, keep_at, nz, keep_ref, *refs):
    coded, outs = refs[: sum(counts)], refs[sum(counts) :]
    _, half, rows = keep_ref.shape
    tables = [scales_of(ref, ref.shape[0] - TAIL) for ref in coded]
    for dz in range(nz):
        ks = []
        for i in range(2):
            total = keep_ref[keep_at[i] + dz]
            for j in range(i * counts[0], i * counts[0] + counts[i]):
                total = total + decode(coded[j], dz * half, half, tables[j][dz : dz + 1])
            if dz == 0:
                outs[0][pl.ds(i * half, half), :] = total
            else:
                q, k = encode(total)
                outs[dz][pl.ds(i * half, half), :] = q
                ks.append(k)
        if dz:
            outs[dz][pl.ds(2 * half, TAIL), :] = tail_rows(ks, rows)


def corner(nz, keep, keep_at, coded_a, coded_b):
    _, half, rows = keep.shape
    shapes = [jax.ShapeDtypeStruct((2 * half, rows), jnp.float32)]
    shapes += [jax.ShapeDtypeStruct((2 * half + TAIL, rows), jnp.int16)] * (nz - 1)
    return pl.pallas_call(
        functools.partial(corner_kernel, (len(coded_a), len(coded_b)), keep_at, nz),
        out_shape=shapes,
        compiler_params=params(18),
        cost_estimate=SMALL,
        name="corner",
    )(keep, *coded_a, *coded_b)


def total_kernel(tokens, keep_ref, *refs):
    grad_ref, sum_ref = refs[-2:]
    width, rows = keep_ref.shape
    half = width // 2
    scales = [scales_of(ref, width) for ref in refs[:-2]]
    square = jnp.zeros((1, rows), jnp.float32)
    for i in range(2):
        total = keep_ref[pl.ds(i * half, half), :]
        for ref, s in zip(refs[:-2], scales):
            total = total + decode(ref, i * half, half, s[i : i + 1])
        total = total / tokens
        grad_ref[:, i * half : (i + 1) * half] = jnp.transpose(total)
        square = square + jnp.sum(total * total, axis=0, keepdims=True)
    sum_ref[...] = jnp.broadcast_to(jnp.sum(square, axis=1, keepdims=True), sum_ref.shape)


def total_gradient(tokens, keep, coded, copies):
    width, rows = keep.shape
    return pl.pallas_call(
        functools.partial(total_kernel, tokens),
        out_shape=[jax.ShapeDtypeStruct((rows, width), jnp.float32), jax.ShapeDtypeStruct((copies, 1, 128), jnp.float32)],
        compiler_params=params(6),
        cost_estimate=SMALL,
        name="total_gradient",
    )(keep, *coded)


def adam_rows(sums_ref, grad_ref, w, f, fs_ref, s, ss_ref, wo, mo, mso, vo, vso):
    sums = sums_ref[...]
    square_sum = jnp.sum(sums, axis=0, keepdims=True)[:, :1]
    factor = jnp.minimum(1.0, clip_norm / (jnp.sqrt(square_sum) + 1e-06))
    rows, width = grad_ref.shape
    blocks = fs_ref.shape[1]
    size = width // blocks
    for i in range(blocks):
        at = slice(i * size, (i + 1) * size)
        clipped = grad_ref[:, at] * factor
        m_old = f[:, at].astype(jnp.float32) * fs_ref[:, i : i + 1]
        v_old = s[:, at].astype(jnp.float32) * ss_ref[:, i : i + 1]
        m_new = beta_first * m_old + (1.0 - beta_first) * clipped
        v_new = beta_second * v_old + (1.0 - beta_second) * clipped * clipped
        m_hat = m_new / (1.0 - beta_first**STEP)
        v_hat = v_new / (1.0 - beta_second**STEP)
        w_old = w[:, at].astype(jnp.float32)
        wo[:, at] = (
            w_old - learn_rate * (m_hat / (jnp.sqrt(v_hat) + adam_epsilon) + weight_decay * w_old)
        ).astype(jnp.bfloat16)
        m_scale = jnp.max(jnp.abs(m_new), axis=1, keepdims=True) + tiny_scale
        v_scale = jnp.max(v_new, axis=1, keepdims=True) + tiny_scale
        mo[:, at] = (m_new / m_scale).astype(jnp.bfloat16)
        vo[:, at] = (v_new / v_scale).astype(jnp.bfloat16)
        mso[i : i + 1, :] = jnp.transpose(jnp.broadcast_to(m_scale, (rows, 128)))[:1]
        vso[i : i + 1, :] = jnp.transpose(jnp.broadcast_to(v_scale, (rows, 128)))[:1]


def adam_kernel(sums_ref, grad_ref, w_ref, f_ref, fs_ref, s_ref, ss_ref, *outs):
    adam_rows(sums_ref, grad_ref, w_ref[...], f_ref[...], fs_ref, s_ref[...], ss_ref, *outs)


def adam_outputs(rows, width, blocks):
    codes = jax.ShapeDtypeStruct((rows, width), jnp.bfloat16)
    scale = jax.ShapeDtypeStruct((blocks, rows), jnp.float32)
    return [codes, codes, scale, codes, scale]


def adam_step(sums, grad, weight, first, first_scale, second, second_scale):
    w_new, m_code, m_scale, v_code, v_scale = pl.pallas_call(
        adam_kernel,
        out_shape=adam_outputs(*grad.shape, first_scale.shape[1]),
        compiler_params=params(8),
        cost_estimate=SMALL,
        name="adam",
    )(sums, grad, weight, first, first_scale, second, second_scale)
    return w_new, m_code, m_scale.T, v_code, v_scale.T


def three_parts(a):
    high = a.astype(jnp.bfloat16)
    rest = a - high.astype(jnp.float32)
    mid = rest.astype(jnp.bfloat16)
    return [high, mid, (rest - mid.astype(jnp.float32)).astype(jnp.bfloat16)]


def pack_kernel(unit, counts_ref, facts_ref, w_ref, f_ref, s_ref, out_ref, pay_ref, wide, first, second):
    peers, _, rows, width = out_ref.shape
    per_row = unit // rows

    def by_rows(ref):
        for j in range(wide.shape[0]):
            wide[j] = ref[:, j * 128 : (j + 1) * 128].astype(jnp.float32)
        sides = [
            wide[j, pl.ds(i, peers * rows, stride=per_row), :] for i in range(per_row) for j in range(wide.shape[0])
        ]
        return jnp.concatenate(sides, axis=1).astype(jnp.bfloat16).reshape(peers, rows, width)

    pay_ref[:peers] = by_rows(w_ref)
    first[...] = by_rows(f_ref)
    second[...] = by_rows(s_ref)
    start, extra = jnp.int32(0), jnp.int32(0)
    for e in range(peers):
        units = counts_ref[0, e] // unit
        at = jnp.minimum(start, peers - 1)
        out_ref[e, 0] = first[at]
        out_ref[e, 1] = second[at]
        extra = jnp.where(units == 2, start + 1, extra)
        start = start + units
    pay_ref[peers] = first[extra]
    pay_ref[peers + 1] = second[extra]
    facts = facts_ref[...]
    meta = [p.astype(jnp.float32) for i in range(2) for p in three_parts(facts[i : i + 1])]
    meta = jnp.concatenate(meta + [facts[2:3], jnp.zeros((rows - 7, width), jnp.float32)])
    pay_ref[peers + 2] = meta.astype(jnp.bfloat16)


def pack_units(unit, counts, facts, w, f, s, shape):
    peers, rows, width = shape
    return pl.pallas_call(
        functools.partial(pack_kernel, unit),
        out_shape=[
            jax.ShapeDtypeStruct((peers, 2, rows, width), w.dtype),
            jax.ShapeDtypeStruct((peers + 3, rows, width), w.dtype),
        ],
        in_specs=[pl.BlockSpec(memory_space=pltpu.SMEM)] + [pl.BlockSpec(memory_space=pltpu.VMEM)] * 4,
        scratch_shapes=[pltpu.VMEM((w.shape[1] // 128, w.shape[0], 128), jnp.float32)] + [pltpu.VMEM(shape, w.dtype)] * 2,
        compiler_params=params(8),
        cost_estimate=SMALL,
        name="pack_units",
    )(counts, facts, w, f, s)


def place_of(grid, units, me, holder, slot):
    dy, dc, dz, dx = (p ^ q for p, q in zip(grid.split(holder), grid.split(me)))
    nx, ny, nz = grid.nx, grid.ny, grid.nz
    cut = (units + 1) // 2
    whole = nz * units
    straight = jnp.where(dy == 0, dx, nx - 1 + dy) * whole + dz * units
    across = (nx + ny - 1 + (dy - 1) * (nx - 1) + (dx - 1)) * whole
    on_axis = (dy == 0) | (dx == 0)
    first = jnp.where(on_axis, straight, across + dz * cut)
    second = jnp.where(on_axis, straight, across + nz * cut + dz * (units - cut) - cut)
    return dc * (nx * ny * whole) + slot + jnp.where(slot < cut, first, second)


def plan_kernel(grid, unit, units, me_ref, *refs):
    parts, (plan_ref, meta_ref, sems) = refs[:-3], refs[-3:]
    peers, lanes = meta_ref.shape[0], plan_ref.shape[1]
    me = me_ref[0]
    copies = []
    for rel in range(peers):
        at, which = place_of_static(grid, units, rel, units - 1), 0
        while at >= parts[which].shape[0]:
            at -= parts[which].shape[0]
            which += 1
        copies.append(pltpu.make_async_copy(parts[which].at[at], meta_ref.at[me ^ rel], sems.at[rel]))
    for copy in copies:
        copy.start()
    for copy in copies:
        copy.wait()
    table = jnp.concatenate([meta_ref[d].astype(jnp.float32)[6:7, :lanes] for d in range(peers)]) * (1.0 / unit)
    row = lax.broadcasted_iota(jnp.int32, (lanes, lanes), 0)
    col = lax.broadcasted_iota(jnp.int32, (lanes, lanes), 1)
    starts = jnp.dot(table, (row < col).astype(jnp.float32), preferred_element_type=jnp.float32).astype(jnp.int32)
    ahead_of = (col < row).astype(jnp.float32)[:peers, :peers]
    offsets = jnp.dot(ahead_of, table, preferred_element_type=jnp.float32).astype(jnp.int32)
    table = table.astype(jnp.int32)
    unit_at = lax.broadcasted_iota(jnp.int32, (peers, lanes), 0)
    zero = jnp.zeros((peers, lanes), jnp.int32)
    place, holder, late, slots = zero, zero, zero, zero
    for d in range(peers):
        ahead = unit_at - offsets[d : d + 1]
        hit = (ahead >= 0) & (ahead < table[d : d + 1])
        slot = starts[d : d + 1] + ahead
        place = jnp.where(hit, place_of(grid, units, me, d, slot), place)
        holder = jnp.where(hit, d, holder)
        late = jnp.where(hit, ahead, late)
        slots = jnp.where(hit, slot, slots)
    for i, a in enumerate((place, holder, late, slots)):
        plan_ref[pl.ds(i * peers, peers), :] = a


def place_of_static(grid, units, rel, slot):
    dy, dc, dz, dx = grid.split(rel)
    nx, ny, nz = grid.nx, grid.ny, grid.nz
    cut = (units + 1) // 2
    whole = nz * units
    at = dc * (nx * ny * whole) + slot
    if dy == 0 or dx == 0:
        return at + (dx if dy == 0 else nx - 1 + dy) * whole + dz * units
    at += (nx + ny - 1 + (dy - 1) * (nx - 1) + (dx - 1)) * whole
    return at + (dz * cut if slot < cut else nz * cut + dz * (units - cut) - cut)


def plan_units(grid, unit, me, parts):
    lanes = max(128, grid.size)
    rows, width = parts[0].shape[-2:]
    units = parts[0].shape[1]
    parts = [p.reshape(-1, rows, width) for p in parts]
    return pl.pallas_call(
        functools.partial(plan_kernel, grid, unit, units),
        out_shape=[
            jax.ShapeDtypeStruct((4 * grid.size, lanes), jnp.int32),
            jax.ShapeDtypeStruct((grid.size, rows, width), parts[0].dtype),
        ],
        in_specs=[pl.BlockSpec(memory_space=pltpu.SMEM)] + [pl.BlockSpec(memory_space=pl.ANY)] * len(parts),
        scratch_shapes=[pltpu.SemaphoreType.DMA((grid.size,))],
        compiler_params=params(8),
        cost_estimate=SMALL,
        name="plan_units",
    )(me, *parts)


def finish_kernel(unit, me_ref, sums_ref, *refs):
    ins, outs, (plan, grad_ref, own_ref, meta, got, first, second, fs, ss, scales, sems) = refs[:5], refs[5:10], refs[10:]
    held = (plan, grad_ref, own_ref, meta, got)
    copies = [pltpu.make_async_copy(a, b, sems.at[i]) for i, (a, b) in enumerate(zip(ins, held))]
    for copy in copies:
        copy.start()
    for copy in copies:
        copy.wait()
    peers, rows, width = first.shape
    me = me_ref[0]
    for d in range(peers):
        facts = meta[d].astype(jnp.float32)
        scales[0, pl.ds(d, 1), :] = facts[0:1] + facts[1:2] + facts[2:3]
        scales[1, pl.ds(d, 1), :] = facts[3:4] + facts[4:5] + facts[5:6]
    per_row = unit // rows
    lane = lax.broadcasted_iota(jnp.int32, (rows, width), 1)
    block = lax.broadcasted_iota(jnp.int32, (rows, width), 0) * per_row
    late = jnp.int32(0)
    for u in range(peers):
        p = plan[peers + u, me]
        first[u] = got[p, 0]
        second[u] = got[p, 1]
        late = jnp.where(plan[2 * peers + u, me] == 1, u, late)
        at = lane - (plan[3 * peers + u, me] * unit + block)
        for i, out in enumerate((fs, ss)):
            line = jnp.broadcast_to(scales[i, pl.ds(p, 1), :], (rows, width))
            for h in range(per_row):
                value = jnp.sum(jnp.where(at == h, line, 0.0), axis=1, keepdims=True)
                out[pl.ds(u * rows, rows), h : h + 1] = value
    first[late] = own_ref[peers]
    second[late] = own_ref[peers + 1]
    two = lambda ref: ref[:peers].reshape(peers * rows, width)
    adam_rows(sums_ref, grad_ref, two(own_ref), two(first), fs, two(second), ss, *outs)


def finish(unit, me, plan, sums, grad, own, got):
    peers, rows, width = plan[1].shape
    blocks = unit // rows
    smem, vmem, anywhere = (pl.BlockSpec(memory_space=m) for m in (pltpu.SMEM, pltpu.VMEM, pl.ANY))
    units, scale = pltpu.VMEM(plan[1].shape, own.dtype), pltpu.VMEM((peers * rows, blocks), jnp.float32)
    w_new, m_code, m_scale, v_code, v_scale = pl.pallas_call(
        functools.partial(finish_kernel, unit),
        out_shape=adam_outputs(peers * rows, width, blocks),
        in_specs=[smem, vmem] + [anywhere] * 5,
        scratch_shapes=[pltpu.SMEM(plan[0].shape, jnp.int32)]
        + [pltpu.VMEM(a.shape, a.dtype) for a in (grad, own, plan[1], got)]
        + [units, units, scale, scale, pltpu.VMEM((2, peers, width), jnp.float32), pltpu.SemaphoreType.DMA((5,))],
        compiler_params=params(56),
        cost_estimate=SMALL,
        name="finish",
    )(me, sums, plan[0], grad, own, plan[1], got)
    return w_new, m_code, m_scale.T, v_code, v_scale.T


def stack_kernel(*refs):
    out, sems = refs[-2:]
    copies = [pltpu.make_async_copy(ref, out.at[i], sems.at[i]) for i, ref in enumerate(refs[:-2])]
    for copy in copies:
        copy.start()
    for copy in copies:
        copy.wait()


def stack_parts(parts):
    return pl.pallas_call(
        stack_kernel,
        out_shape=jax.ShapeDtypeStruct((len(parts),) + parts[0].shape, parts[0].dtype),
        in_specs=[pl.BlockSpec(memory_space=pl.ANY)] * len(parts),
        scratch_shapes=[pltpu.SemaphoreType.DMA((len(parts),))],
        compiler_params=params(56),
        cost_estimate=SMALL,
        name="stack_parts",
    )(*parts)


def halves_kernel(count, *refs):
    sems = refs[-1]
    ins, outs = refs[: len(refs) // 2], refs[len(refs) // 2 : -1]
    copies = []
    for n, (ref, out) in enumerate(zip(ins, outs)):
        cut = out.shape[1]
        copies.append(pltpu.make_async_copy(ref.at[:, pl.ds(0 if n < count else ref.shape[1] - cut, cut)], out, sems.at[n]))
    for copy in copies:
        copy.start()
    for copy in copies:
        copy.wait()


def halves(firsts, seconds):
    ins = firsts + seconds
    nz, units, rows, width = ins[0].shape
    cuts = [(units + 1) // 2] * len(firsts) + [units // 2] * len(seconds)
    outs = pl.pallas_call(
        functools.partial(halves_kernel, len(firsts)),
        out_shape=[jax.ShapeDtypeStruct((nz, cut, rows, width), ins[0].dtype) for cut in cuts],
        in_specs=[pl.BlockSpec(memory_space=pl.ANY)] * len(ins),
        scratch_shapes=[pltpu.SemaphoreType.DMA((len(ins),))],
        compiler_params=params(8),
        cost_estimate=SMALL,
        name="halves",
    )(*ins)
    return outs[: len(firsts)], outs[len(firsts) :]


def product_kernel(count, group, grid, me_ref, plan_ref, cot_ref, *refs):
    parts, (out_ref, own_ref, plan, held, tile, made, sems, out_sems) = refs[:count], refs[count:]
    copies, at = [pltpu.make_async_copy(plan_ref, plan, sems.at[count])], 0
    for i, ref in enumerate(parts):
        copies.append(pltpu.make_async_copy(ref, held.at[pl.ds(at, ref.shape[0])], sems.at[i]))
        at += ref.shape[0]
    for copy in copies:
        copy.start()
    for copy in copies:
        copy.wait()
    steps, _, columns = made.shape
    peers = own_ref.shape[0] - 2

    def put(i):
        return pltpu.make_async_copy(
            made.at[i], out_ref.at[:, pl.ds(pl.multiple_of(i * columns, columns), columns)], out_sems.at[i]
        )

    def step(i, carry):
        for u in range(group):
            tile[u] = held[plan[u % peers, i * (group // peers) + u // peers]]
        weight = tile[...].reshape(group * tile.shape[1], tile.shape[2])
        made[i] = lax.dot_general(
            cot_ref[...], weight, (((1,), (1,)), ((), ())), preferred_element_type=jnp.float32
        ).astype(made.dtype)
        put(i).start()
        return carry

    lax.fori_loop(0, steps, step, 0, unroll=True)
    me = me_ref[0]
    late = jnp.int32(0)
    for u in range(peers):
        own_ref[u] = held[plan[u, me]]
        late = jnp.where(plan[2 * peers + u, me] == 1, plan[peers + u, me], late)
    extra = place_of(grid, peers + 3, me, late, peers)
    own_ref[peers] = held[extra]
    own_ref[peers + 1] = held[extra + 1]

    def finish(i, carry):
        put(i).wait()
        return carry

    lax.fori_loop(0, steps, finish, 0)


def product(grid, me, plan, cot, parts):
    rows, width = parts[0].shape[-2:]
    parts = [p.reshape(-1, rows, width) for p in parts]
    peers = grid.size
    total = peers * peers
    group = GROUP
    tokens = cot.shape[0]
    smem, vmem, anywhere = (pl.BlockSpec(memory_space=m) for m in (pltpu.SMEM, pltpu.VMEM, pl.ANY))
    return pl.pallas_call(
        functools.partial(product_kernel, len(parts), group, grid),
        out_shape=[
            jax.ShapeDtypeStruct((tokens, total * rows), cot.dtype),
            jax.ShapeDtypeStruct((peers + 2, rows, width), cot.dtype),
        ],
        in_specs=[smem, anywhere, vmem] + [anywhere] * len(parts),
        out_specs=[anywhere, vmem],
        scratch_shapes=[
            pltpu.SMEM(plan[0].shape, jnp.int32),
            pltpu.VMEM((sum(p.shape[0] for p in parts), rows, width), cot.dtype),
            pltpu.VMEM((group, rows, width), cot.dtype),
            pltpu.VMEM((total // group, tokens, group * rows), cot.dtype),
            pltpu.SemaphoreType.DMA((len(parts) + 1,)),
            pltpu.SemaphoreType.DMA((total // group,)),
        ],
        compiler_params=params(28),
        cost_estimate=SMALL,
        name="product",
    )(me, plan[0], cot, *parts)


def after(a, *others):
    return lax.optimization_barrier((a, others))[0]


def spread_weight(grid, near, gates):
    near = after(stack_parts(after(near, gates[0])), gates[1])
    along_x = {dx: grid.send(near, dx=dx) for dx in range(1, grid.nx)}
    along_y = {dy: grid.send(near, dy=dy) for dy in range(1, grid.ny)}
    parts = [near] + list(along_x.values()) + list(along_y.values())
    firsts, seconds = halves(*after((list(along_x.values()), list(along_y.values())), gates[2]))
    for dy in range(1, grid.ny):
        for dx in range(1, grid.nx):
            parts.append(grid.send(firsts[dx - 1], dy=dy))
            parts.append(grid.send(seconds[dy - 1], dx=dx))
    at = grid.nx + grid.ny - 1
    parts = parts[:at] + after(parts[at:], gates[3])
    return parts + [grid.send(p, dc=1) for p in parts]


def send_state(grid, w, f, fs, s, ss, counts, key_width, gate):
    peers = grid.size
    slots, block = w.shape
    unit = slots // peers
    per_row = key_width // block
    unit_rows = unit // per_row
    shape = (peers, unit_rows, key_width)
    pad = lambda a: jnp.pad(a, (0, key_width - a.shape[0]))
    facts = jnp.stack([pad(fs), pad(ss), pad(counts[0].astype(jnp.float32))])
    packed, payload = pack_units(unit, counts, facts, *after((w, f, s), gate), shape)
    return packed, [payload] + [grid.send(payload, dz=dz) for dz in range(1, grid.nz)]


def apply_state(grid, me, cot, near, got, w, key_width, gates, sums, gradient):
    peers = grid.size
    slots, block = w.shape
    unit = slots // peers
    per_row = key_width // block
    parts = spread_weight(grid, near, gates)
    where = me.reshape(1)
    plan = plan_units(grid, unit, where, parts)
    input_grad, own = product(grid, where, plan, cot, parts)
    return input_grad, *finish(unit, where, plan, sums, gradient, own, got)


def state_by_blocks(grid, me, cot, w, f, fs, s, ss, counts, key_width):
    peers = grid.size
    slots, block = w.shape
    per_row = key_width // block
    rows = slots // per_row
    gather = lambda a: lax.all_gather(a, AXES, axis=0, tiled=True)
    table = gather(counts)
    starts = jnp.cumsum(table, axis=1) - table
    offsets = jnp.cumsum(table, axis=0) - table
    j = jnp.arange(slots, dtype=jnp.int32)
    ahead = j[None, None, :] - offsets[:, :, None]
    hit = (ahead >= 0) & (ahead < table[:, :, None])
    holder = jnp.arange(peers, dtype=jnp.int32)[:, None, None]
    pick = jnp.sum(jnp.where(hit, holder * slots + starts[:, :, None] + ahead, 0), axis=0)
    weight = gather(w)[pick.reshape(-1)].reshape(-1, key_width)
    mine = lax.dynamic_index_in_dim(pick, me, 0, keepdims=False)
    own_weight = lax.dynamic_slice_in_dim(weight, me * rows, rows, 0)
    two = lambda a: gather(a)[mine].reshape(rows, key_width)
    scale = lambda a: gather(a)[mine].reshape(rows, per_row)
    input_grad = lax.dot_general(
        cot, weight, (((1,), (1,)), ((), ())), preferred_element_type=jnp.float32
    ).astype(jnp.bfloat16)
    return input_grad, own_weight, two(f), scale(fs), two(s), scale(ss)


def shards(
    hidden_states,
    key_cotangent,
    old_weight,
    old_first,
    old_first_scale,
    old_second,
    old_second_scale,
    send_counts,
):
    grid = Grid(lax.axis_size("cuts"), lax.axis_size("fsdp"))
    me = lax.axis_index(AXES).astype(jnp.int32)
    y, c, z, x = grid.split(me)
    slots, block = old_weight.shape
    key_width = key_cotangent.shape[1]
    rows = slots * block // key_width
    tokens = hidden_states.shape[0]
    peers = grid.size
    per_row = key_width // block
    unit = slots // peers
    by_units = unit % per_row == 0 and unit // per_row >= 8 and slots <= key_width and peers <= 128

    ny, nz, nx = grid.ny, grid.nz, grid.nx
    batches = [
        [(dy, dx) for dx in range(1, nx) for dy in reversed(range(ny))],
        [(dy, 0) for dy in reversed(range(ny))],
    ]

    where = me.reshape(1)
    pick = functools.partial(pick_columns, grid)
    picked = [pick(where, 1, batches[0], hidden_states, rows, key_cotangent)]
    picked.append(pick(after(where, picked[0]), 1, batches[1], hidden_states, rows))
    parts = [grid.send(p, dc=1) for p in picked]
    owns = [pick(after(where, picked[1]), 0, batches[0], hidden_states, rows)]
    owns.append(pick(after(where, owns[0]), 0, batches[1], hidden_states, rows))

    def job(dy, dx, side):
        which = 0 if dx else 1
        return which, batches[which].index((dy, dx)) * nz, side

    def terms(coded, jobs, *gate):
        count = 1 + max(j[0] for j in jobs)
        return partial_sums(coded, jobs, nz, after(key_cotangent, gate), owns[:count], parts[:count])

    sent_a, sent_b, made = {}, {}, ()
    for dx in range(1, nx):
        made = terms(True, [job(dy, dx, 0) for dy in range(ny)], made)
        sent_a[dx] = grid.send(made, dx=dx)
    first_made = made
    for dy in range(1, ny):
        made = terms(True, [job(dy, dx, 1) for dx in range(nx)], made)
        sent_b[dy] = grid.send(made, dy=dy)
    keep = terms(False, [job(dy, 0, 0) for dy in range(1, ny)] + [job(0, dx, 1) for dx in range(1, nx)], made)
    last = terms(False, [job(0, 0, 0), job(0, 0, 1)], keep)
    if by_units:
        packed, near = send_state(
            grid, old_weight, old_first, old_first_scale, old_second, old_second_scale, send_counts, key_width, picked[1]
        )
    late_a, late_b, coded_late = [], [], []
    kept = after(keep, (near[:3], last)) if by_units else keep
    for dy in range(1, ny):
        coded_late.append(relay(nz, kept, (dy - 1) * nz, list(sent_a.values()), dy * nz))
        late_a.append(grid.send(coded_late[-1], dy=dy))
    for dx in range(1, nx):
        coded_late.append(relay(nz, kept, (ny + dx - 2) * nz, list(sent_b.values()), dx * nz))
        late_b.append(grid.send(coded_late[-1], dx=dx))
    if by_units:
        got = lax.all_to_all(packed, AXES, 0, 0, tiled=True)
    last = gather_terms(nz, after(last, coded_late), list(sent_a.values()), list(sent_b.values()))
    if by_units:
        last = after(last, got)
    mine = corner(nz, last, (0, nz), late_a, late_b)
    over_z = [grid.send(mine[dz], dz=dz) for dz in range(1, grid.nz)]
    gradient, square = total_gradient(tokens * peers, mine[0], over_z, peers)
    sums = lax.all_to_all(square, AXES, 0, 0, tiled=True).reshape(peers, 128)

    if by_units:
        gates = (coded_late, (late_a, late_b), mine, square)
        return apply_state(grid, me, key_cotangent, near, got, old_weight, key_width, gates, sums, gradient)
    input_grad, own_weight, first, first_scale, second, second_scale = state_by_blocks(
        grid, me, key_cotangent, old_weight, old_first, old_first_scale, old_second, old_second_scale, send_counts, key_width
    )
    return input_grad, *adam_step(sums, gradient, own_weight, first, first_scale, second, second_scale)


def solution(mesh):
    placed = (
        P(("cuts", "fsdp"), None),
        P(("cuts", "fsdp"), None),
        P(("cuts", "fsdp"), None),
        P(("cuts", "fsdp"), None),
        P(("cuts", "fsdp")),
        P(("cuts", "fsdp"), None),
        P(("cuts", "fsdp")),
        P(("cuts", "fsdp"), None),
    )
    return jax.shard_map(
        shards,
        mesh=mesh,
        in_specs=placed,
        out_specs=(
            P(("cuts", "fsdp"), None),
            P(("cuts", "fsdp"), None),
            P(("cuts", "fsdp"), None),
            P(("cuts", "fsdp"), None),
            P(("cuts", "fsdp"), None),
            P(("cuts", "fsdp"), None),
        ),
        check_vma=False,
    )
```

```python
import functools

import jax
import jax.numpy as jnp
from jax import lax
from jax.experimental import pallas as pl
from jax.experimental.pallas import tpu as pltpu
from jax.sharding import PartitionSpec as P

STEP = 2000


beta_first = 0.9
beta_second = 0.95
adam_epsilon = 1e-05
learn_rate = 0.001
weight_decay = 0.1
clip_norm = 1.0
tiny_scale = 1e-30

AXES = ("cuts", "fsdp")
TAIL = 16
GROUP = 128


class Grid:
    def __init__(self, cuts, fsdp):
        self.cuts, self.fsdp = cuts, fsdp
        self.ny = cuts // 2
        self.nz = 4
        self.nx = fsdp // 4
        self.size = cuts * fsdp

    def split(self, i):
        x = i % self.nx
        z = (i // self.nx) % self.nz
        c = (i // self.fsdp) % 2
        y = i // (2 * self.fsdp)
        return y, c, z, x

    def join(self, y, c, z, x):
        return ((y * 2 + c) * self.nz + z) * self.nx + x

    def send(self, a, dy=0, dc=0, dz=0, dx=0):
        pairs = []
        for i in range(self.size):
            y, c, z, x = self.split(i)
            pairs.append((i, self.join(y ^ dy, c ^ dc, z ^ dz, x ^ dx)))
        return lax.ppermute(a, AXES, pairs)


SMALL = pl.CostEstimate(flops=1, bytes_accessed=1, transcendentals=0)


def params(mib):
    return pltpu.CompilerParams(vmem_limit_bytes=mib * 1024 * 1024)


def encode(g):
    top = jnp.max(jnp.abs(g), axis=0, keepdims=True)
    k = jnp.ceil(jnp.log2(jnp.maximum(top, 1e-30) / 32700.0) * 256.0)
    q = jnp.round(g * jnp.exp2(k * (-1.0 / 256.0)))
    return q.astype(jnp.int32).astype(jnp.int16), k


def tail_rows(ks, columns):
    filled = list(ks)
    if len(ks) < TAIL:
        filled.append(jnp.zeros((TAIL - len(ks), columns), jnp.float32))
    filled = jnp.concatenate(filled)
    return filled.astype(jnp.int32).astype(jnp.int16)


def scales_of(ref, row):
    k = ref[pl.ds(row, TAIL), :].astype(jnp.int32).astype(jnp.float32)
    return jnp.exp2(k * (1.0 / 256.0))


def decode(ref, row, rows, scale):
    return ref[pl.ds(row, rows), :].astype(jnp.int32).astype(jnp.float32) * scale


def pick_kernel(grid, core, groups, me_ref, hidden_ref, *refs):
    out, held, sems, out_sems = refs[-4:]
    rows = out.shape[2]
    y, c, z, x = grid.split(me_ref[0])
    owners = [grid.join(y ^ dy, c ^ core, z ^ dz, x ^ dx) for dy, dx in groups for dz in range(grid.nz)]
    copies, puts = [], []
    for i, owner in enumerate(owners):
        at = pl.multiple_of(owner * rows, rows)
        copies.append(pltpu.make_async_copy(hidden_ref.at[:, pl.ds(at, rows)], held.at[i], sems.at[i]))
    for i in range(len(owners), out.shape[0]):
        at = (i - len(owners)) * rows
        copies.append(pltpu.make_async_copy(refs[0].at[:, pl.ds(at, rows)], held.at[i], sems.at[i]))
    for copy in copies:
        copy.start()
    for i, copy in enumerate(copies):
        copy.wait()
        puts.append(pltpu.make_async_copy(held.at[i], out.at[i], out_sems.at[i]))
        puts[-1].start()
    for put in puts:
        put.wait()


def pick_columns(grid, me, core, groups, hidden, rows, *more):
    tokens = hidden.shape[0]
    if rows % 128:
        cut = lambda a, at: lax.dynamic_slice_in_dim(a, at * rows, rows, 1)
        y, c, z, x = grid.split(me[0])
        owners = [grid.join(y ^ dy, c ^ core, z ^ dz, x ^ dx) for dy, dx in groups for dz in range(grid.nz)]
        return jnp.stack([cut(hidden, o) for o in owners] + [cut(a, i) for a in more for i in range(a.shape[1] // rows)])
    blocks = len(groups) * grid.nz + sum(a.shape[1] // rows for a in more)
    return pl.pallas_call(
        functools.partial(pick_kernel, grid, core, groups),
        out_shape=jax.ShapeDtypeStruct((blocks, tokens, rows), hidden.dtype),
        in_specs=[pl.BlockSpec(memory_space=pltpu.SMEM)] + [pl.BlockSpec(memory_space=pl.ANY)] * (1 + len(more)),
        out_specs=pl.BlockSpec(memory_space=pl.ANY),
        scratch_shapes=[pltpu.VMEM((blocks, tokens, rows), hidden.dtype)] + [pltpu.SemaphoreType.DMA((blocks,))] * 2,
        compiler_params=params(56),
        cost_estimate=SMALL,
        name="pick_columns",
    )(me, hidden, *more)


def partial_kernel(coded, jobs, nz, count, c_ref, *refs):
    owns, parts, out = refs[:count], refs[count:-1], refs[-1]
    tokens, width = c_ref.shape
    half, rows = width // 2, owns[0].shape[2]
    last = parts[0].shape[0] - width // rows
    across = (((0,), (0,)), ((), ()))
    ks = []
    for n, (which, at, side) in enumerate(jobs):
        mine = c_ref[:, side * half : (side + 1) * half]
        blocks = range(last + side * half // rows, last + (side + 1) * half // rows)
        other = [parts[0][b] for b in blocks]
        other = other[0] if len(other) == 1 else jnp.concatenate(other, axis=1)
        for i in range(nz):
            g = lax.dot_general(mine, owns[which][at + i], across, preferred_element_type=jnp.float32)
            g = g + lax.dot_general(other, parts[which][at + i], across, preferred_element_type=jnp.float32)
            if coded:
                q, k = encode(g)
                out[pl.ds((n * nz + i) * half, half), :] = q
                ks.append(k)
            else:
                out[n * nz + i] = g
    if coded:
        out[pl.ds(len(jobs) * nz * half, TAIL), :] = tail_rows(ks, rows)


def partial_sums(coded, jobs, nz, cot, owns, parts):
    _, width = cot.shape
    half, rows = width // 2, owns[0].shape[2]
    blocks = len(jobs) * nz
    return pl.pallas_call(
        functools.partial(partial_kernel, coded, jobs, nz, len(owns)),
        out_shape=jax.ShapeDtypeStruct((blocks * half + TAIL, rows), jnp.int16)
        if coded
        else jax.ShapeDtypeStruct((blocks, half, rows), jnp.float32),
        compiler_params=params(24),
        cost_estimate=SMALL,
        name="partial_sums",
    )(cot, *owns, *parts)


def relay_kernel(keep_at, coded_at, nz, keep_ref, *refs):
    coded, out = refs[:-1], refs[-1]
    _, half, rows = keep_ref.shape
    tables = [scales_of(ref, ref.shape[0] - TAIL) for ref in coded]
    ks = []
    for i in range(nz):
        total = keep_ref[keep_at + i]
        for ref, s in zip(coded, tables):
            at = coded_at + i
            total = total + decode(ref, at * half, half, s[at : at + 1])
        q, k = encode(total)
        out[pl.ds(i * half, half), :] = q
        ks.append(k)
    out[pl.ds(nz * half, TAIL), :] = tail_rows(ks, rows)


def relay(nz, keep, keep_at, coded, coded_at):
    _, half, rows = keep.shape
    return pl.pallas_call(
        functools.partial(relay_kernel, keep_at, coded_at, nz),
        out_shape=jax.ShapeDtypeStruct((nz * half + TAIL, rows), jnp.int16),
        compiler_params=params(14),
        cost_estimate=SMALL,
        name="relay",
    )(keep, *coded)


def gather_kernel(count, nz, keep_ref, *refs):
    number = len(refs) - 3
    coded, (out, held, sems) = refs[:number], refs[number:]
    _, half, rows = keep_ref.shape
    copies = []
    for j, ref in enumerate(coded):
        for i, (at, size, to) in enumerate(((0, nz * half, 0), (ref.shape[0] - TAIL, TAIL, nz * half))):
            copies.append(pltpu.make_async_copy(ref.at[pl.ds(at, size)], held.at[j, pl.ds(to, size)], sems.at[2 * j + i]))
    for copy in copies:
        copy.start()
    for copy in copies:
        copy.wait()
    for n in range(2):
        mine = range(count) if n == 0 else range(count, number)
        tables = {j: scales_of(held.at[j], nz * half) for j in mine}
        for i in range(nz):
            total = keep_ref[n * nz + i]
            for j in mine:
                total = total + decode(held.at[j], i * half, half, tables[j][i : i + 1])
            out[n * nz + i] = total


def gather_terms(nz, keep, coded_a, coded_b):
    _, half, rows = keep.shape
    coded = list(coded_a) + list(coded_b)
    return pl.pallas_call(
        functools.partial(gather_kernel, len(coded_a), nz),
        out_shape=jax.ShapeDtypeStruct(keep.shape, keep.dtype),
        in_specs=[pl.BlockSpec(memory_space=pltpu.VMEM)] + [pl.BlockSpec(memory_space=pl.ANY)] * len(coded),
        scratch_shapes=[pltpu.VMEM((len(coded), nz * half + TAIL, rows), jnp.int16), pltpu.SemaphoreType.DMA((2 * len(coded),))],
        compiler_params=params(14),
        cost_estimate=SMALL,
        name="gather_terms",
    )(keep, *coded)


def corner_kernel(counts, keep_at, nz, keep_ref, *refs):
    coded, outs = refs[: sum(counts)], refs[sum(counts) :]
    _, half, rows = keep_ref.shape
    tables = [scales_of(ref, ref.shape[0] - TAIL) for ref in coded]
    for dz in range(nz):
        ks = []
        for i in range(2):
            total = keep_ref[keep_at[i] + dz]
            for j in range(i * counts[0], i * counts[0] + counts[i]):
                total = total + decode(coded[j], dz * half, half, tables[j][dz : dz + 1])
            if dz == 0:
                outs[0][pl.ds(i * half, half), :] = total
            else:
                q, k = encode(total)
                outs[dz][pl.ds(i * half, half), :] = q
                ks.append(k)
        if dz:
            outs[dz][pl.ds(2 * half, TAIL), :] = tail_rows(ks, rows)


def corner(nz, keep, keep_at, coded_a, coded_b):
    _, half, rows = keep.shape
    shapes = [jax.ShapeDtypeStruct((2 * half, rows), jnp.float32)]
    shapes += [jax.ShapeDtypeStruct((2 * half + TAIL, rows), jnp.int16)] * (nz - 1)
    return pl.pallas_call(
        functools.partial(corner_kernel, (len(coded_a), len(coded_b)), keep_at, nz),
        out_shape=shapes,
        compiler_params=params(18),
        cost_estimate=SMALL,
        name="corner",
    )(keep, *coded_a, *coded_b)


def total_kernel(tokens, keep_ref, *refs):
    grad_ref, sum_ref = refs[-2:]
    width, rows = keep_ref.shape
    half = width // 2
    scales = [scales_of(ref, width) for ref in refs[:-2]]
    square = jnp.zeros((1, rows), jnp.float32)
    for i in range(2):
        total = keep_ref[pl.ds(i * half, half), :]
        for ref, s in zip(refs[:-2], scales):
            total = total + decode(ref, i * half, half, s[i : i + 1])
        total = total / tokens
        grad_ref[:, i * half : (i + 1) * half] = jnp.transpose(total)
        square = square + jnp.sum(total * total, axis=0, keepdims=True)
    sum_ref[...] = jnp.broadcast_to(jnp.sum(square, axis=1, keepdims=True), sum_ref.shape)


def total_gradient(tokens, keep, coded, copies):
    width, rows = keep.shape
    return pl.pallas_call(
        functools.partial(total_kernel, tokens),
        out_shape=[jax.ShapeDtypeStruct((rows, width), jnp.float32), jax.ShapeDtypeStruct((copies, 1, 128), jnp.float32)],
        compiler_params=params(6),
        cost_estimate=SMALL,
        name="total_gradient",
    )(keep, *coded)


def adam_rows(sums_ref, grad_ref, w, f, fs_ref, s, ss_ref, wo, mo, mso, vo, vso):
    sums = sums_ref[...]
    square_sum = jnp.sum(sums, axis=0, keepdims=True)[:, :1]
    factor = jnp.minimum(1.0, clip_norm / (jnp.sqrt(square_sum) + 1e-06))
    rows, width = grad_ref.shape
    blocks = fs_ref.shape[1]
    size = width // blocks
    for i in range(blocks):
        at = slice(i * size, (i + 1) * size)
        clipped = grad_ref[:, at] * factor
        m_old = f[:, at].astype(jnp.float32) * fs_ref[:, i : i + 1]
        v_old = s[:, at].astype(jnp.float32) * ss_ref[:, i : i + 1]
        m_new = beta_first * m_old + (1.0 - beta_first) * clipped
        v_new = beta_second * v_old + (1.0 - beta_second) * clipped * clipped
        m_hat = m_new / (1.0 - beta_first**STEP)
        v_hat = v_new / (1.0 - beta_second**STEP)
        w_old = w[:, at].astype(jnp.float32)
        wo[:, at] = (
            w_old - learn_rate * (m_hat / (jnp.sqrt(v_hat) + adam_epsilon) + weight_decay * w_old)
        ).astype(jnp.bfloat16)
        m_scale = jnp.max(jnp.abs(m_new), axis=1, keepdims=True) + tiny_scale
        v_scale = jnp.max(v_new, axis=1, keepdims=True) + tiny_scale
        mo[:, at] = (m_new / m_scale).astype(jnp.bfloat16)
        vo[:, at] = (v_new / v_scale).astype(jnp.bfloat16)
        mso[i : i + 1, :] = jnp.transpose(jnp.broadcast_to(m_scale, (rows, 128)))[:1]
        vso[i : i + 1, :] = jnp.transpose(jnp.broadcast_to(v_scale, (rows, 128)))[:1]


def adam_kernel(sums_ref, grad_ref, w_ref, f_ref, fs_ref, s_ref, ss_ref, *outs):
    adam_rows(sums_ref, grad_ref, w_ref[...], f_ref[...], fs_ref, s_ref[...], ss_ref, *outs)


def adam_outputs(rows, width, blocks):
    codes = jax.ShapeDtypeStruct((rows, width), jnp.bfloat16)
    scale = jax.ShapeDtypeStruct((blocks, rows), jnp.float32)
    return [codes, codes, scale, codes, scale]


def adam_step(sums, grad, weight, first, first_scale, second, second_scale):
    w_new, m_code, m_scale, v_code, v_scale = pl.pallas_call(
        adam_kernel,
        out_shape=adam_outputs(*grad.shape, first_scale.shape[1]),
        compiler_params=params(8),
        cost_estimate=SMALL,
        name="adam",
    )(sums, grad, weight, first, first_scale, second, second_scale)
    return w_new, m_code, m_scale.T, v_code, v_scale.T


def three_parts(a):
    high = a.astype(jnp.bfloat16)
    rest = a - high.astype(jnp.float32)
    mid = rest.astype(jnp.bfloat16)
    return [high, mid, (rest - mid.astype(jnp.float32)).astype(jnp.bfloat16)]


def pack_kernel(unit, counts_ref, facts_ref, w_ref, f_ref, s_ref, out_ref, pay_ref, wide, first, second):
    peers, _, rows, width = out_ref.shape
    per_row = unit // rows

    def by_rows(ref):
        for j in range(wide.shape[0]):
            wide[j] = ref[:, j * 128 : (j + 1) * 128].astype(jnp.float32)
        sides = [
            wide[j, pl.ds(i, peers * rows, stride=per_row), :] for i in range(per_row) for j in range(wide.shape[0])
        ]
        return jnp.concatenate(sides, axis=1).astype(jnp.bfloat16).reshape(peers, rows, width)

    pay_ref[:peers] = by_rows(w_ref)
    first[...] = by_rows(f_ref)
    second[...] = by_rows(s_ref)
    start, extra = jnp.int32(0), jnp.int32(0)
    for e in range(peers):
        units = counts_ref[0, e] // unit
        at = jnp.minimum(start, peers - 1)
        out_ref[e, 0] = first[at]
        out_ref[e, 1] = second[at]
        extra = jnp.where(units == 2, start + 1, extra)
        start = start + units
    pay_ref[peers] = first[extra]
    pay_ref[peers + 1] = second[extra]
    facts = facts_ref[...]
    meta = [p.astype(jnp.float32) for i in range(2) for p in three_parts(facts[i : i + 1])]
    meta = jnp.concatenate(meta + [facts[2:3], jnp.zeros((rows - 7, width), jnp.float32)])
    pay_ref[peers + 2] = meta.astype(jnp.bfloat16)


def pack_units(unit, counts, facts, w, f, s, shape):
    peers, rows, width = shape
    return pl.pallas_call(
        functools.partial(pack_kernel, unit),
        out_shape=[
            jax.ShapeDtypeStruct((peers, 2, rows, width), w.dtype),
            jax.ShapeDtypeStruct((peers + 3, rows, width), w.dtype),
        ],
        in_specs=[pl.BlockSpec(memory_space=pltpu.SMEM)] + [pl.BlockSpec(memory_space=pltpu.VMEM)] * 4,
        scratch_shapes=[pltpu.VMEM((w.shape[1] // 128, w.shape[0], 128), jnp.float32)] + [pltpu.VMEM(shape, w.dtype)] * 2,
        compiler_params=params(8),
        cost_estimate=SMALL,
        name="pack_units",
    )(counts, facts, w, f, s)


def place_of(grid, units, me, holder, slot):
    dy, dc, dz, dx = (p ^ q for p, q in zip(grid.split(holder), grid.split(me)))
    nx, ny, nz = grid.nx, grid.ny, grid.nz
    cut = (units + 1) // 2
    whole = nz * units
    straight = jnp.where(dy == 0, dx, nx - 1 + dy) * whole + dz * units
    across = (nx + ny - 1 + (dy - 1) * (nx - 1) + (dx - 1)) * whole
    on_axis = (dy == 0) | (dx == 0)
    first = jnp.where(on_axis, straight, across + dz * cut)
    second = jnp.where(on_axis, straight, across + nz * cut + dz * (units - cut) - cut)
    return dc * (nx * ny * whole) + slot + jnp.where(slot < cut, first, second)


def fact_copies(grid, units, me, parts, meta_ref, sems):
    peers = grid.size
    copies = []
    for rel in range(peers):
        at, which = place_of_static(grid, units, rel, units - 1), 0
        while at >= parts[which].shape[0]:
            at -= parts[which].shape[0]
            which += 1
        copies.append(pltpu.make_async_copy(parts[which].at[at], meta_ref.at[me ^ rel], sems.at[rel]))
    return copies


def make_plan(grid, unit, units, me, meta_ref, plan_ref):
    peers, lanes = meta_ref.shape[0], plan_ref.shape[1]
    table = jnp.concatenate([meta_ref[d].astype(jnp.float32)[6:7, :lanes] for d in range(peers)]) * (1.0 / unit)
    row = lax.broadcasted_iota(jnp.int32, (lanes, lanes), 0)
    col = lax.broadcasted_iota(jnp.int32, (lanes, lanes), 1)
    starts = jnp.dot(table, (row < col).astype(jnp.float32), preferred_element_type=jnp.float32).astype(jnp.int32)
    ahead_of = (col < row).astype(jnp.float32)[:peers, :peers]
    offsets = jnp.dot(ahead_of, table, preferred_element_type=jnp.float32).astype(jnp.int32)
    table = table.astype(jnp.int32)
    unit_at = lax.broadcasted_iota(jnp.int32, (peers, lanes), 0)
    zero = jnp.zeros((peers, lanes), jnp.int32)
    place, holder, late, slots = zero, zero, zero, zero
    for d in range(peers):
        ahead = unit_at - offsets[d : d + 1]
        hit = (ahead >= 0) & (ahead < table[d : d + 1])
        slot = starts[d : d + 1] + ahead
        place = jnp.where(hit, place_of(grid, units, me, d, slot), place)
        holder = jnp.where(hit, d, holder)
        late = jnp.where(hit, ahead, late)
        slots = jnp.where(hit, slot, slots)
    for i, a in enumerate((place, holder, late, slots)):
        plan_ref[pl.ds(i * peers, peers), :] = a


def place_of_static(grid, units, rel, slot):
    dy, dc, dz, dx = grid.split(rel)
    nx, ny, nz = grid.nx, grid.ny, grid.nz
    cut = (units + 1) // 2
    whole = nz * units
    at = dc * (nx * ny * whole) + slot
    if dy == 0 or dx == 0:
        return at + (dx if dy == 0 else nx - 1 + dy) * whole + dz * units
    at += (nx + ny - 1 + (dy - 1) * (nx - 1) + (dx - 1)) * whole
    return at + (dz * cut if slot < cut else nz * cut + dz * (units - cut) - cut)


def finish_kernel(unit, me_ref, sums_ref, *refs):
    ins, outs, (plan, grad_ref, own_ref, meta, got, first, second, fs, ss, scales, sems) = refs[:5], refs[5:10], refs[10:]
    held = (plan, grad_ref, own_ref, meta, got)
    copies = [pltpu.make_async_copy(a, b, sems.at[i]) for i, (a, b) in enumerate(zip(ins, held))]
    for copy in copies:
        copy.start()
    for copy in copies:
        copy.wait()
    peers, rows, width = first.shape
    me = me_ref[0]
    for d in range(peers):
        facts = meta[d].astype(jnp.float32)
        scales[0, pl.ds(d, 1), :] = facts[0:1] + facts[1:2] + facts[2:3]
        scales[1, pl.ds(d, 1), :] = facts[3:4] + facts[4:5] + facts[5:6]
    per_row = unit // rows
    lane = lax.broadcasted_iota(jnp.int32, (rows, width), 1)
    block = lax.broadcasted_iota(jnp.int32, (rows, width), 0) * per_row
    late = jnp.int32(0)
    for u in range(peers):
        p = plan[peers + u, me]
        first[u] = got[p, 0]
        second[u] = got[p, 1]
        late = jnp.where(plan[2 * peers + u, me] == 1, u, late)
        at = lane - (plan[3 * peers + u, me] * unit + block)
        for i, out in enumerate((fs, ss)):
            line = jnp.broadcast_to(scales[i, pl.ds(p, 1), :], (rows, width))
            for h in range(per_row):
                value = jnp.sum(jnp.where(at == h, line, 0.0), axis=1, keepdims=True)
                out[pl.ds(u * rows, rows), h : h + 1] = value
    first[late] = own_ref[peers]
    second[late] = own_ref[peers + 1]
    two = lambda ref: ref[:peers].reshape(peers * rows, width)
    adam_rows(sums_ref, grad_ref, two(own_ref), two(first), fs, two(second), ss, *outs)


def finish(unit, me, plan, sums, grad, own, got):
    peers, rows, width = plan[1].shape
    blocks = unit // rows
    smem, vmem, anywhere = (pl.BlockSpec(memory_space=m) for m in (pltpu.SMEM, pltpu.VMEM, pl.ANY))
    units, scale = pltpu.VMEM(plan[1].shape, own.dtype), pltpu.VMEM((peers * rows, blocks), jnp.float32)
    w_new, m_code, m_scale, v_code, v_scale = pl.pallas_call(
        functools.partial(finish_kernel, unit),
        out_shape=adam_outputs(peers * rows, width, blocks),
        in_specs=[smem, vmem] + [anywhere] * 5,
        scratch_shapes=[pltpu.SMEM(plan[0].shape, jnp.int32)]
        + [pltpu.VMEM(a.shape, a.dtype) for a in (grad, own, plan[1], got)]
        + [units, units, scale, scale, pltpu.VMEM((2, peers, width), jnp.float32), pltpu.SemaphoreType.DMA((5,))],
        compiler_params=params(51),
        cost_estimate=SMALL,
        name="finish",
    )(me, sums, plan[0], grad, own, plan[1], got)
    return w_new, m_code, m_scale.T, v_code, v_scale.T


def stack_kernel(*refs):
    out, sems = refs[-2:]
    copies = [pltpu.make_async_copy(ref, out.at[i], sems.at[i]) for i, ref in enumerate(refs[:-2])]
    for copy in copies:
        copy.start()
    for copy in copies:
        copy.wait()


def stack_parts(parts):
    return pl.pallas_call(
        stack_kernel,
        out_shape=jax.ShapeDtypeStruct((len(parts),) + parts[0].shape, parts[0].dtype),
        in_specs=[pl.BlockSpec(memory_space=pl.ANY)] * len(parts),
        scratch_shapes=[pltpu.SemaphoreType.DMA((len(parts),))],
        compiler_params=params(56),
        cost_estimate=SMALL,
        name="stack_parts",
    )(*parts)


def halves_kernel(count, *refs):
    sems = refs[-1]
    ins, outs = refs[: len(refs) // 2], refs[len(refs) // 2 : -1]
    copies = []
    for n, (ref, out) in enumerate(zip(ins, outs)):
        cut = out.shape[1]
        copies.append(pltpu.make_async_copy(ref.at[:, pl.ds(0 if n < count else ref.shape[1] - cut, cut)], out, sems.at[n]))
    for copy in copies:
        copy.start()
    for copy in copies:
        copy.wait()


def halves(firsts, seconds):
    ins = firsts + seconds
    nz, units, rows, width = ins[0].shape
    cuts = [(units + 1) // 2] * len(firsts) + [units // 2] * len(seconds)
    outs = pl.pallas_call(
        functools.partial(halves_kernel, len(firsts)),
        out_shape=[jax.ShapeDtypeStruct((nz, cut, rows, width), ins[0].dtype) for cut in cuts],
        in_specs=[pl.BlockSpec(memory_space=pl.ANY)] * len(ins),
        scratch_shapes=[pltpu.SemaphoreType.DMA((len(ins),))],
        compiler_params=params(8),
        cost_estimate=SMALL,
        name="halves",
    )(*ins)
    return outs[: len(firsts)], outs[len(firsts) :]


def product_kernel(count, group, grid, unit, units, me_ref, cot_ref, *refs):
    parts, (out_ref, own_ref, plan_ref, meta_ref, plan, held, tile, made, sems, out_sems, fact_sems) = refs[:count], refs[count:]
    facts = fact_copies(grid, units, me_ref[0], parts, meta_ref, fact_sems)
    for copy in facts:
        copy.start()
    copies, at = [], 0
    for i, ref in enumerate(parts):
        copies.append(pltpu.make_async_copy(ref, held.at[pl.ds(at, ref.shape[0])], sems.at[i]))
        at += ref.shape[0]
    for copy in copies:
        copy.start()
    for copy in facts:
        copy.wait()
    make_plan(grid, unit, units, me_ref[0], meta_ref, plan_ref)
    copies.append(pltpu.make_async_copy(plan_ref, plan, sems.at[count]))
    copies[-1].start()
    for copy in copies:
        copy.wait()
    steps, _, columns = made.shape
    peers = own_ref.shape[0] - 2

    def put(i):
        return pltpu.make_async_copy(
            made.at[i], out_ref.at[:, pl.ds(pl.multiple_of(i * columns, columns), columns)], out_sems.at[i]
        )

    def step(i, carry):
        for u in range(group):
            tile[u] = held[plan[u % peers, i * (group // peers) + u // peers]]
        weight = tile[...].reshape(group * tile.shape[1], tile.shape[2])
        made[i] = lax.dot_general(
            cot_ref[...], weight, (((1,), (1,)), ((), ())), preferred_element_type=jnp.float32
        ).astype(made.dtype)
        put(i).start()
        return carry

    lax.fori_loop(0, steps, step, 0, unroll=True)
    me = me_ref[0]
    late = jnp.int32(0)
    for u in range(peers):
        own_ref[u] = held[plan[u, me]]
        late = jnp.where(plan[2 * peers + u, me] == 1, plan[peers + u, me], late)
    extra = place_of(grid, peers + 3, me, late, peers)
    own_ref[peers] = held[extra]
    own_ref[peers + 1] = held[extra + 1]

    def finish(i, carry):
        put(i).wait()
        return carry

    lax.fori_loop(0, steps, finish, 0)


def product(grid, unit, me, cot, parts):
    units, rows, width = parts[0].shape[1:]
    lanes = max(128, grid.size)
    parts = [p.reshape(-1, rows, width) for p in parts]
    peers = grid.size
    total = peers * peers
    group = GROUP
    tokens = cot.shape[0]
    smem, vmem, anywhere = (pl.BlockSpec(memory_space=m) for m in (pltpu.SMEM, pltpu.VMEM, pl.ANY))
    return pl.pallas_call(
        functools.partial(product_kernel, len(parts), group, grid, unit, units),
        out_shape=[
            jax.ShapeDtypeStruct((tokens, total * rows), cot.dtype),
            jax.ShapeDtypeStruct((peers + 2, rows, width), cot.dtype),
            jax.ShapeDtypeStruct((4 * peers, lanes), jnp.int32),
            jax.ShapeDtypeStruct((peers, rows, width), cot.dtype),
        ],
        in_specs=[smem, vmem] + [anywhere] * len(parts),
        out_specs=[anywhere, vmem, vmem, vmem],
        scratch_shapes=[
            pltpu.SMEM((4 * peers, lanes), jnp.int32),
            pltpu.VMEM((sum(p.shape[0] for p in parts), rows, width), cot.dtype),
            pltpu.VMEM((group, rows, width), cot.dtype),
            pltpu.VMEM((total // group, tokens, group * rows), cot.dtype),
            pltpu.SemaphoreType.DMA((len(parts) + 1,)),
            pltpu.SemaphoreType.DMA((total // group,)),
            pltpu.SemaphoreType.DMA((peers,)),
        ],
        compiler_params=params(28),
        cost_estimate=SMALL,
        name="product",
    )(me, cot, *parts)


def after(a, *others):
    return lax.optimization_barrier((a, others))[0]


def spread_weight(grid, near, gates):
    near = after(stack_parts(after(near, gates[0])), gates[1])
    along_x = {dx: grid.send(near, dx=dx) for dx in range(1, grid.nx)}
    along_y = {dy: grid.send(near, dy=dy) for dy in range(1, grid.ny)}
    parts = [near] + list(along_x.values()) + list(along_y.values())
    firsts, seconds = halves(*after((list(along_x.values()), list(along_y.values())), gates[2]))
    for dy in range(1, grid.ny):
        for dx in range(1, grid.nx):
            parts.append(grid.send(firsts[dx - 1], dy=dy))
            parts.append(grid.send(seconds[dy - 1], dx=dx))
    at = grid.nx + grid.ny - 1
    parts = parts[:at] + after(parts[at:], gates[3])
    return parts + [grid.send(p, dc=1) for p in parts]


def send_state(grid, w, f, fs, s, ss, counts, key_width, gate):
    peers = grid.size
    slots, block = w.shape
    unit = slots // peers
    per_row = key_width // block
    unit_rows = unit // per_row
    shape = (peers, unit_rows, key_width)
    pad = lambda a: jnp.pad(a, (0, key_width - a.shape[0]))
    facts = jnp.stack([pad(fs), pad(ss), pad(counts[0].astype(jnp.float32))])
    packed, payload = pack_units(unit, counts, facts, *after((w, f, s), gate), shape)
    return packed, [payload] + [grid.send(payload, dz=dz) for dz in range(1, grid.nz)]


def apply_state(grid, me, cot, near, got, w, key_width, gates, sums, gradient):
    peers = grid.size
    slots, block = w.shape
    unit = slots // peers
    per_row = key_width // block
    parts = spread_weight(grid, near, gates)
    where = me.reshape(1)
    input_grad, own, *plan = product(grid, unit, where, cot, parts)
    return input_grad, *finish(unit, where, plan, sums, gradient, own, got)


def state_by_blocks(grid, me, cot, w, f, fs, s, ss, counts, key_width):
    peers = grid.size
    slots, block = w.shape
    per_row = key_width // block
    rows = slots // per_row
    gather = lambda a: lax.all_gather(a, AXES, axis=0, tiled=True)
    table = gather(counts)
    starts = jnp.cumsum(table, axis=1) - table
    offsets = jnp.cumsum(table, axis=0) - table
    j = jnp.arange(slots, dtype=jnp.int32)
    ahead = j[None, None, :] - offsets[:, :, None]
    hit = (ahead >= 0) & (ahead < table[:, :, None])
    holder = jnp.arange(peers, dtype=jnp.int32)[:, None, None]
    pick = jnp.sum(jnp.where(hit, holder * slots + starts[:, :, None] + ahead, 0), axis=0)
    weight = gather(w)[pick.reshape(-1)].reshape(-1, key_width)
    mine = lax.dynamic_index_in_dim(pick, me, 0, keepdims=False)
    own_weight = lax.dynamic_slice_in_dim(weight, me * rows, rows, 0)
    two = lambda a: gather(a)[mine].reshape(rows, key_width)
    scale = lambda a: gather(a)[mine].reshape(rows, per_row)
    input_grad = lax.dot_general(
        cot, weight, (((1,), (1,)), ((), ())), preferred_element_type=jnp.float32
    ).astype(jnp.bfloat16)
    return input_grad, own_weight, two(f), scale(fs), two(s), scale(ss)


def shards(
    hidden_states,
    key_cotangent,
    old_weight,
    old_first,
    old_first_scale,
    old_second,
    old_second_scale,
    send_counts,
):
    grid = Grid(lax.axis_size("cuts"), lax.axis_size("fsdp"))
    me = lax.axis_index(AXES).astype(jnp.int32)
    y, c, z, x = grid.split(me)
    slots, block = old_weight.shape
    key_width = key_cotangent.shape[1]
    rows = slots * block // key_width
    tokens = hidden_states.shape[0]
    peers = grid.size
    per_row = key_width // block
    unit = slots // peers
    by_units = unit % per_row == 0 and unit // per_row >= 8 and slots <= key_width and peers <= 128

    ny, nz, nx = grid.ny, grid.nz, grid.nx
    batches = [
        [(dy, dx) for dx in range(1, nx) for dy in reversed(range(ny))],
        [(dy, 0) for dy in reversed(range(ny))],
    ]

    where = me.reshape(1)
    pick = functools.partial(pick_columns, grid)
    picked = [pick(where, 1, batches[0], hidden_states, rows, key_cotangent)]
    picked.append(pick(after(where, picked[0]), 1, batches[1], hidden_states, rows))
    parts = [grid.send(p, dc=1) for p in picked]
    owns = [pick(after(where, picked[1]), 0, batches[0], hidden_states, rows)]
    owns.append(pick(after(where, owns[0]), 0, batches[1], hidden_states, rows))

    def job(dy, dx, side):
        which = 0 if dx else 1
        return which, batches[which].index((dy, dx)) * nz, side

    def terms(coded, jobs, *gate):
        count = 1 + max(j[0] for j in jobs)
        return partial_sums(coded, jobs, nz, after(key_cotangent, gate), owns[:count], parts[:count])

    sent_a, sent_b, made = {}, {}, ()
    for dx in range(1, nx):
        made = terms(True, [job(dy, dx, 0) for dy in range(ny)], made)
        sent_a[dx] = grid.send(made, dx=dx)
    first_made = made
    for dy in range(1, ny):
        made = terms(True, [job(dy, dx, 1) for dx in range(nx)], made)
        sent_b[dy] = grid.send(made, dy=dy)
    keep = terms(False, [job(dy, 0, 0) for dy in range(1, ny)] + [job(0, dx, 1) for dx in range(1, nx)], made)
    last = terms(False, [job(0, 0, 0), job(0, 0, 1)], keep)
    if by_units:
        packed, near = send_state(
            grid, old_weight, old_first, old_first_scale, old_second, old_second_scale, send_counts, key_width, picked[1]
        )
    late_a, late_b, coded_late = [], [], []
    kept = after(keep, (near[:3], last)) if by_units else keep
    for dy in range(1, ny):
        coded_late.append(relay(nz, kept, (dy - 1) * nz, list(sent_a.values()), dy * nz))
        late_a.append(grid.send(coded_late[-1], dy=dy))
    for dx in range(1, nx):
        coded_late.append(relay(nz, kept, (ny + dx - 2) * nz, list(sent_b.values()), dx * nz))
        late_b.append(grid.send(coded_late[-1], dx=dx))
    if by_units:
        got = lax.all_to_all(packed, AXES, 0, 0, tiled=True)
    last = gather_terms(nz, after(last, coded_late), list(sent_a.values()), list(sent_b.values()))
    if by_units:
        last = after(last, got)
    mine = corner(nz, last, (0, nz), late_a, late_b)
    over_z = [grid.send(mine[dz], dz=dz) for dz in range(1, grid.nz)]
    gradient, square = total_gradient(tokens * peers, mine[0], over_z, peers)
    sums = lax.all_to_all(square, AXES, 0, 0, tiled=True).reshape(peers, 128)

    if by_units:
        gates = (coded_late, (late_a, late_b), mine, square)
        return apply_state(grid, me, key_cotangent, near, got, old_weight, key_width, gates, sums, gradient)
    input_grad, own_weight, first, first_scale, second, second_scale = state_by_blocks(
        grid, me, key_cotangent, old_weight, old_first, old_first_scale, old_second, old_second_scale, send_counts, key_width
    )
    return input_grad, *adam_step(sums, gradient, own_weight, first, first_scale, second, second_scale)


def solution(mesh):
    placed = (
        P(("cuts", "fsdp"), None),
        P(("cuts", "fsdp"), None),
        P(("cuts", "fsdp"), None),
        P(("cuts", "fsdp"), None),
        P(("cuts", "fsdp")),
        P(("cuts", "fsdp"), None),
        P(("cuts", "fsdp")),
        P(("cuts", "fsdp"), None),
    )
    return jax.shard_map(
        shards,
        mesh=mesh,
        in_specs=placed,
        out_specs=(
            P(("cuts", "fsdp"), None),
            P(("cuts", "fsdp"), None),
            P(("cuts", "fsdp"), None),
            P(("cuts", "fsdp"), None),
            P(("cuts", "fsdp"), None),
            P(("cuts", "fsdp"), None),
        ),
        check_vma=False,
    )
```
